32 devices in a mesh: dp: 8 (over z, y), expert: 4 (over x, core).
Axes of the slice: x: 2, y: 2, z: 4, core: 2. Of those that a mesh axis runs over, the one named last changes fastest.
Arguments:
- token_ids: int32 [32, 1024], P(('dp', 'expert')), may hold values from 0 to 65535
- routes: int32 [32, 1024, 2], P(('dp', 'expert')), may hold values from 0 to 11, all different within a row; in each aligned block of 1024 rows (0 to 1023, 1024 to 2047, ..., all dimensions but the last counted through in order) at most 320 rows name the same one
- last_valid: int32 [32, 4], P(('dp', 'expert')), may hold values from 0 to 127
- rank_pairs: int32 [32, 4, 2], P(('dp', 'expert')), may hold values from 0 to 3, as said below
- embedding: float32 [65536, 768], P('dp'), may hold values from -6 to 6
- embedding_first: float32 [65536, 768], P('dp'), may hold values from -1.66893e-06 to 1.66893e-06
- embedding_second: float32 [65536, 768], P('dp'), may hold values from 7.947286e-14 to 3.1789144e-13
- attend_in: float32 [768, 2304], P('dp'), may hold values from -0.21875 to 0.21875
- attend_in_first: float32 [768, 2304], P('dp'), may hold values from -4.5776367e-05 to 4.5776367e-05
- attend_in_second: float32 [768, 2304], P('dp'), may hold values from 5.6514033e-11 to 2.2605613e-10
- attend_out: float32 [768, 768], P('dp'), may hold values from -1.25 to 1.25
- attend_out_first: float32 [768, 768], P('dp'), may hold values from -7.6293945e-05 to 7.6293945e-05
- attend_out_second: float32 [768, 768], P('dp'), may hold values from 1.695421e-10 to 6.781684e-10
- expert_in: float32 [8, 768, 4096], P('expert', 'dp'), may hold values from -0.21875 to 0.21875
- expert_in_first: float32 [8, 768, 4096], P('expert', 'dp'), may hold values from -2.2888184e-05 to 2.2888184e-05
- expert_in_second: float32 [8, 768, 4096], P('expert', 'dp'), may hold values from 1.5894572e-11 to 6.357829e-11
- expert_out: float32 [8, 2048, 768], P('expert', 'dp'), may hold values from -1 to 1
- expert_out_first: float32 [8, 2048, 768], P('expert', 'dp'), may hold values from -3.0517578e-05 to 3.0517578e-05
- expert_out_second: float32 [8, 2048, 768], P('expert', 'dp'), may hold values from 3.1789144e-11 to 1.2715658e-10
- router: float32 [768, 16], replicated, may hold values from -0.15625 to 0.15625
- router_first: float32 [768, 16], replicated, may hold values from -0.00021362305 to 0.00021362305
- router_second: float32 [768, 16], replicated, may hold values from 1.3020833e-09 to 5.2083333e-09
- norm_gains: float32 [3, 768], replicated, may hold values from 0.5 to 1.5
- norm_gains_first: float32 [3, 768], replicated, may hold values from -0.00024414062 to 0.00024414062
- norm_gains_second: float32 [3, 768], replicated, may hold values from 1.5258789e-09 to 6.1035155e-09
- const_vectors: float32 [2, 768], replicated, may hold values from -6 to 6
- const_vectors_first: float32 [2, 768], replicated, may hold values from -7.6293945e-06 to 7.6293945e-06
- const_vectors_second: float32 [2, 768], replicated, may hold values from 1.695421e-12 to 6.781684e-12
- score_head: float32 [768], replicated, may hold values from -0.21875 to 0.21875
- score_head_first: float32 [768], replicated, may hold values from -0.0068359375 to 0.0068359375
- score_head_second: float32 [768], replicated, may hold values from 1.171875e-06 to 4.6875e-06
Outputs:
- embedding_new: float32 [65536, 768], P('dp')
- embedding_first_new: float32 [65536, 768], P('dp')
- embedding_second_new: float32 [65536, 768], P('dp')
- attend_in_new: float32 [768, 2304], P('dp')
- attend_in_first_new: float32 [768, 2304], P('dp')
- attend_in_second_new: float32 [768, 2304], P('dp')
- attend_out_new: float32 [768, 768], P('dp')
- attend_out_first_new: float32 [768, 768], P('dp')
- attend_out_second_new: float32 [768, 768], P('dp')
- expert_in_new: float32 [8, 768, 4096], P('expert', 'dp')
- expert_in_first_new: float32 [8, 768, 4096], P('expert', 'dp')
- expert_in_second_new: float32 [8, 768, 4096], P('expert', 'dp')
- expert_out_new: float32 [8, 2048, 768], P('expert', 'dp')
- expert_out_first_new: float32 [8, 2048, 768], P('expert', 'dp')
- expert_out_second_new: float32 [8, 2048, 768], P('expert', 'dp')
- router_new: float32 [768, 16], replicated
- router_first_new: float32 [768, 16], replicated
- router_second_new: float32 [768, 16], replicated
- norm_gains_new: float32 [3, 768], replicated
- norm_gains_first_new: float32 [3, 768], replicated
- norm_gains_second_new: float32 [3, 768], replicated
- const_vectors_new: float32 [2, 768], replicated
- const_vectors_first_new: float32 [2, 768], replicated
- const_vectors_second_new: float32 [2, 768], replicated
- score_head_new: float32 [768], replicated
- score_head_first_new: float32 [768], replicated
- score_head_second_new: float32 [768], replicated
- loss_sum: float32 [], replicated
- grad_norm: float32 [], replicated
The draws below stay inside these ranges and needn't reach their ends.
Inputs may be any that keep to these rules, and one draw needn't show every extreme that they name: `routes`: each token names two different experts; 8 is the zero expert, 9 the copy expert, 10 and 11 the constant experts. Among one group's 1024 tokens no expert is named more than 320 times, a bound that some block reaches. `rank_pairs`: the two continuations of a pair differ.
All inputs are finite; a program needn't handle non-finite values.
Results may differ from the reference program's by a relative error of at most 0.019.
Values may be sent and summed in bfloat16 or wider, within the bound.
No kernel may reach another device: no remote copies, remote signals or barrier semaphores. Data moves between devices by JAX's collectives and lax.ppermute only.
A program may use at most 704 MiB of HBM per device.

```python
import math
import jax
import jax.numpy as jnp
import numpy as np
from jax import lax

D = 768
HEAD = 64
FF = 2048
NEXP = 8
VOCAB = 65536
PROMPT = 512
CLEN = 128
NCONT = 4
NPAIR = 4
ADAM_STEP = 5
TOK = 1024
CAP = 320
GROUPS = 32


def draw_rank_pairs(key, part):
    key = jax.random.fold_in(key, 7)
    lead_key, offset_key = jax.random.split(key)
    leading = jax.random.randint(lead_key, (GROUPS, NPAIR), 0, NCONT)
    offset = jax.random.randint(offset_key, (GROUPS, NPAIR), 1, NCONT)
    return jnp.stack([leading, (leading + offset) % NCONT], -1).astype(jnp.int32)


def place_ends(array, stream_key, low, largest):
    shape = array.shape
    place = [jax.random.randint(jax.random.fold_in(stream_key, axis), (), 0, shape[axis]) for axis in range(len(shape))]
    array = array.at[tuple(place)].set(low)
    longest = shape.index(max(shape))
    place[longest] = (place[longest] + 1) % shape[longest]
    return array.at[tuple(place)].set(largest)


def steps_of(own_key, extent, pieces, least, top_value):
    factor_of, own = 1.0, jax.random.fold_in(own_key, 6)
    for dim, blocks in pieces:
        steps = jnp.exp(jax.random.uniform(jax.random.fold_in(own, dim), (blocks,), jnp.float32, least / len(pieces), top_value / len(pieces)))
        factor_of = factor_of * jnp.repeat(steps, extent[dim] // blocks).reshape([-1 if axis == dim else 1 for axis in range(len(extent))])
    return factor_of


def rank_table(number_of, lean):
    weights = [(1 << 20) // math.isqrt(grade ** lean) + 1 for grade in range(1, number_of + 1)]
    scale = 1 + sum(weights) // (1 << 30)
    return np.cumsum(np.array([max(1, weight // scale) for weight in weights]))


def ranked_ids(key, shape, amount, skew):
    grid = rank_table(amount, skew)
    pick = jax.random.randint(jax.random.fold_in(key, 1), shape, 0, int(grid[amount - 1]))
    grade = jnp.searchsorted(jnp.asarray(grid, jnp.int32), pick, side="right")
    return jax.random.permutation(jax.random.fold_in(key, 2), amount)[grade].astype(jnp.int32)


def deal_out(stream_key, own, number, rows, count, top, limit, slope):
    ranking = jax.random.permutation(stream_key, count)
    packed, common = portions_of(count, rows * top, limit, slope, True), portions_of(count, rows * top, limit, slope, False)
    places = jnp.arange(count)

    def named(lengths, rotation):
        used = int((lengths > 0).sum())
        fixed = max(1, used // 4)
        shifted = fixed + (places - fixed + rotation * (used - fixed)) % max(1, count - fixed)
        return jnp.zeros((count,), jnp.int32).at[ranking[jnp.where(places < fixed, places, shifted)]].set(jnp.asarray(lengths, jnp.int32))

    lengths = jnp.where(number % 4 == 0, named(packed, number // 4), named(common, number - number // 4 - 1))
    mixed = jax.random.permutation(jax.random.fold_in(own, 3), count)
    giver, receiver = mixed[0:count // 2 * 2:2], mixed[1:count // 2 * 2:2]
    room = jnp.minimum(lengths[giver] - 1, limit - lengths[receiver]) // 2
    room = jnp.where((giver == ranking[0]) | (receiver == ranking[0]) | (lengths[receiver] == 0), 0, jnp.maximum(room, 0))
    shifted = jax.random.randint(jax.random.fold_in(own, 4), (count // 2,), 0, 1 << 20) % (room + 1)
    lengths = lengths.at[giver].add(-shifted).at[receiver].add(shifted)
    items = jnp.searchsorted(jnp.cumsum(lengths), jnp.arange(rows * top), side="right").astype(jnp.int32)
    listing = items.reshape(top, rows).T
    listing = listing[jax.random.permutation(jax.random.fold_in(own, 1), rows)]
    rotation = jax.random.randint(jax.random.fold_in(own, 2), (rows, 1), 0, top)
    return jnp.take_along_axis(listing, (jnp.arange(top)[None, :] + rotation) % top, axis=1)


def portions_of(count, total, most, slope, full):
    portions = [(1 << 20) // math.isqrt(rank ** slope) + 1 for rank in range(1, count + 1)]
    largest = most if full else min(most, max(-(-total // count), total * portions[0] // sum(portions)))
    least = 1 if total - largest >= count - 1 else 0
    counts, spare = [largest] + [least] * (count - 1), total - largest - least * (count - 1)
    while spare > 0:
        candidates = [i for i in range(1, count) if counts[i] < largest] or [i for i in range(1, count) if counts[i] < most]
        pool, remaining = sum([portions[i] for i in candidates]), spare
        for i in candidates:
            more = min(most - counts[i], max(1, remaining * portions[i] // pool), spare)
            counts[i] = counts[i] + more
            spare = spare - more
    return np.array(counts)


def centred(rng, extent, scale, bound, pieces=(), dtype=jnp.bfloat16):
    level = steps_of(rng, extent, pieces, -0.22, 0.18) if pieces else 1.0
    array = jax.random.normal(rng, extent, jnp.float32) * scale * level
    return jnp.minimum(jnp.maximum(array, -bound), bound).astype(dtype)


def setup_inputs(seed: int = 0) -> dict:
    splits = jax.random.split(jax.random.key(seed), 32)
    token_ids = place_ends(ranked_ids(splits[0], (GROUPS, TOK), VOCAB, 2), jax.random.fold_in(splits[0], 3), 0, VOCAB - 1).astype(jnp.int32)
    routes_keys = jax.random.split(jax.random.fold_in(splits[1], 1), GROUPS * TOK // TOK)
    routes_turns = jax.random.permutation(jax.random.fold_in(splits[1], 3), GROUPS * TOK // TOK)
    routes = jax.vmap(lambda own, number: deal_out(jax.random.fold_in(splits[1], 2), own, number, TOK, NEXP + 4, 2, CAP, 1))(routes_keys, routes_turns).reshape((GROUPS, TOK, 2))
    last_valid = place_ends(jax.random.randint(splits[2], (GROUPS, NCONT), 0, CLEN), jax.random.fold_in(splits[2], 1), 0, CLEN - 1).astype(jnp.int32)
    rank_pairs = draw_rank_pairs(jax.random.fold_in(splits[31], 71), 0)
    embedding = centred(splits[4], (VOCAB, D), 1.0, 6.0, ((0, 8),), jnp.float32)
    embedding_first = centred(splits[5], (VOCAB, D), (0.002 * (VOCAB * D) ** -0.5), 1.6689300537109375e-06, ((0, 8),), jnp.float32)
    embedding_second = jnp.clip(jnp.exp(math.log(3.178914379994846e-13) - 1.3862944 * jax.random.uniform(splits[6], (VOCAB, D), jnp.float32) ** steps_of(splits[6], (VOCAB, D), ((0, 8),), -0.2, 0.2)), 7.947285949987115e-14, 3.178914379994846e-13)
    attend_in = centred(splits[7], (D, 3 * D), D ** -0.5, 0.21875, ((0, 8),), jnp.float32)
    attend_in_first = centred(splits[8], (D, 3 * D), (0.01 * (3 * D * D) ** -0.5), 4.57763671875e-05, ((0, 8),), jnp.float32)
    attend_in_second = jnp.clip(jnp.exp(math.log(2.2605613214654596e-10) - 1.3862944 * jax.random.uniform(splits[9], (D, 3 * D), jnp.float32) ** steps_of(splits[9], (D, 3 * D), ((0, 8),), -0.2, 0.2)), 5.651403303663649e-11, 2.2605613214654596e-10)
    attend_out = centred(splits[10], (D, D), (D * 16 // PROMPT) ** -0.5, 1.25, ((0, 8),), jnp.float32)
    attend_out_first = centred(splits[11], (D, D), (0.01 * (D * D) ** -0.5), 7.62939453125e-05, ((0, 8),), jnp.float32)
    attend_out_second = jnp.clip(jnp.exp(math.log(6.781684103174257e-10) - 1.3862944 * jax.random.uniform(splits[12], (D, D), jnp.float32) ** steps_of(splits[12], (D, D), ((0, 8),), -0.2, 0.2)), 1.6954210257935642e-10, 6.781684103174257e-10)
    expert_in = centred(splits[13], (NEXP, D, 2 * FF), D ** -0.5, 0.21875, ((0, 4), (1, 8)), jnp.float32)
    expert_in_first = centred(splits[14], (NEXP, D, 2 * FF), (0.02 * (NEXP * D * 2 * FF) ** -0.5), 2.288818359375e-05, ((0, 4), (1, 8)), jnp.float32)
    expert_in_second = jnp.clip(jnp.exp(math.log(6.357828846725866e-11) - 1.3862944 * jax.random.uniform(splits[15], (NEXP, D, 2 * FF), jnp.float32) ** steps_of(splits[15], (NEXP, D, 2 * FF), ((0, 4), (1, 8)), -0.2, 0.2)), 1.5894572116814665e-11, 6.357828846725866e-11)
    expert_out = centred(splits[16], (NEXP, FF, D), (FF // 64) ** -0.5, 1.0, ((0, 4), (1, 8)), jnp.float32)
    expert_out_first = centred(splits[17], (NEXP, FF, D), (0.02 * (NEXP * FF * D) ** -0.5), 3.0517578125e-05, ((0, 4), (1, 8)), jnp.float32)
    expert_out_second = jnp.clip(jnp.exp(math.log(1.2715657693451732e-10) - 1.3862944 * jax.random.uniform(splits[18], (NEXP, FF, D), jnp.float32) ** steps_of(splits[18], (NEXP, FF, D), ((0, 4), (1, 8)), -0.2, 0.2)), 3.178914423362933e-11, 1.2715657693451732e-10)
    router = centred(splits[19], (D, NEXP + 8), (2 * D) ** -0.5, 0.15625, (), jnp.float32)
    router_first = centred(splits[20], (D, NEXP + 8), (0.001 * D ** -0.5), 0.00021362305, (), jnp.float32)
    router_second = jnp.clip(jnp.exp(jax.random.uniform(splits[21], (D, NEXP + 8), jnp.float32, math.log(1.302083330045889e-09), math.log(5.208333320183556e-09))), 1.302083330045889e-09, 5.208333320183556e-09)
    norm_gains = jnp.clip(1.0 + 0.1 * jax.random.normal(splits[22], (3, D), jnp.float32), 0.5, 1.5)
    norm_gains_first = centred(splits[23], (3, D), (0.03 * D ** -1), 0.00024414062, (), jnp.float32)
    norm_gains_second = jnp.clip(jnp.exp(jax.random.uniform(splits[24], (3, D), jnp.float32, math.log(1.5258788677030566e-09), math.log(6.103515470812226e-09))), 1.5258788677030566e-09, 6.103515470812226e-09)
    const_vectors = centred(splits[25], (2, D), 1.0, 6.0, (), jnp.float32)
    const_vectors_first = centred(splits[26], (2, D), (0.001 * D ** -1), 7.62939453125e-06, (), jnp.float32)
    const_vectors_second = jnp.clip(jnp.exp(jax.random.uniform(splits[27], (2, D), jnp.float32, math.log(1.6954210388039903e-12), math.log(6.781684155215961e-12))), 1.6954210388039903e-12, 6.781684155215961e-12)
    score_head = centred(splits[28], (D,), D ** -0.5, 0.21875, (), jnp.float32)
    score_head_first = centred(splits[29], (D,), (0.03 * D ** -0.5), 0.0068359375, (), jnp.float32)
    score_head_second = jnp.clip(jnp.exp(jax.random.uniform(splits[30], (D,), jnp.float32, math.log(1.1718750556610757e-06), math.log(4.687500222644303e-06))), 1.1718750556610757e-06, 4.687500222644303e-06)
    return {"token_ids": token_ids, "routes": routes, "last_valid": last_valid, "rank_pairs": rank_pairs, "embedding": embedding, "embedding_first": embedding_first, "embedding_second": embedding_second, "attend_in": attend_in, "attend_in_first": attend_in_first, "attend_in_second": attend_in_second, "attend_out": attend_out, "attend_out_first": attend_out_first, "attend_out_second": attend_out_second, "expert_in": expert_in, "expert_in_first": expert_in_first, "expert_in_second": expert_in_second, "expert_out": expert_out, "expert_out_first": expert_out_first, "expert_out_second": expert_out_second, "router": router, "router_first": router_first, "router_second": router_second, "norm_gains": norm_gains, "norm_gains_first": norm_gains_first, "norm_gains_second": norm_gains_second, "const_vectors": const_vectors, "const_vectors_first": const_vectors_first, "const_vectors_second": const_vectors_second, "score_head": score_head, "score_head_first": score_head_first, "score_head_second": score_head_second}


HIGH = lax.Precision.HIGHEST
EPS_NORM = 1e-05
THRESH = 0.05
BETA_ONE = 0.5
BETA_TWO = 0.5
ADAM_EPS = 1e-08
ROPE_BASE = 10000.0
DECAYS = (0.1, 0.1, 0.1, 0.1, 0.1, 0.1, 0.0, 0.0, 0.0)

@jax.custom_vjp
def low(v):
    return lax.optimization_barrier(v.astype(jnp.bfloat16)).astype(jnp.float32)

@jax.custom_vjp
def low_back(v):
    return v

def low_keep(v):
    return (low(v), None)

def low_pass(kept, grad):
    return (grad,)

def back_keep(v):
    return (v, None)

def back_low(kept, grad):
    return (low(grad),)
low.defvjp(low_keep, low_pass)
low_back.defvjp(back_keep, back_low)

def learn_rates():
    return (1.0, D ** (-0.5), (D * 16 // PROMPT) ** (-0.5), D ** (-0.5), (FF // 64) ** (-0.5), (2 * D) ** (-0.5), 0.5, 1.0, D ** (-0.5))

def matmul(left, right):
    return jnp.dot(left, right, precision=HIGH, preferred_element_type=jnp.float32)

def rms_norm(values, gain):
    return values * lax.rsqrt(lax.optimization_barrier(jnp.mean(values * values, -1, keepdims=True)) + EPS_NORM) * gain

def rope_tables(tokens, prompt, span, half):
    places = jnp.arange(tokens)
    position = jnp.where(places < prompt, places, prompt + (places - prompt) % span).astype(jnp.float32)
    freq = ROPE_BASE ** (-jnp.arange(half).astype(jnp.float32) / half)
    angle = position[:, None] * freq[None, :]
    return (jnp.cos(angle), jnp.sin(angle))

def rotate(values, cosine, sine):
    half = cosine.shape[1]
    former, latter = (values[..., :half], values[..., half:])
    cosine, sine = (cosine[:, None, :], sine[:, None, :])
    return jnp.concatenate([former * cosine - latter * sine, latter * cosine + former * sine], -1)

def visible(row_pos, col_pos, prompt, span):
    row_seg = jnp.where(row_pos < prompt, 0, (row_pos - prompt) // span + 1)
    col_seg = jnp.where(col_pos < prompt, 0, (col_pos - prompt) // span + 1)
    before = col_pos[None, :] <= row_pos[:, None]
    from_prompt = (col_seg == 0)[None, :] & ((row_seg > 0)[:, None] | before)
    own_cont = (col_seg[None, :] == row_seg[:, None]) & before
    return from_prompt | own_cont

def group_loss(lowered, gains, const_vectors, score_head, ids, picks, last, pair):
    embed_low, attend_in_low, attend_out_low, expert_in_low, expert_out_low, router_low = lowered
    tokens = ids.shape[0]
    width = embed_low.shape[1]
    heads = width // HEAD
    experts = expert_in_low.shape[0]
    routed = experts + 4
    hidden_units = expert_in_low.shape[2] // 2
    start_x = embed_low[ids]
    normed = rms_norm(start_x, gains[0])
    proj = low_back(matmul(low(normed), attend_in_low))
    cosine, sine = rope_tables(tokens, PROMPT, CLEN, HEAD // 2)
    shaped = proj.reshape(tokens, 3, heads, HEAD)
    queries = low(rotate(shaped[:, 0], cosine, sine))
    keys = low(rotate(shaped[:, 1], cosine, sine))
    values = low(shaped[:, 2])
    scores = low_back(jnp.einsum('thd,shd->hts', queries, keys, precision=HIGH) * HEAD ** (-0.5))
    places = jnp.arange(tokens)
    scores = jnp.where(visible(places, places, PROMPT, CLEN)[None], scores, -1e+30)
    probs = low(jax.nn.softmax(scores, -1))
    mixed = jnp.einsum('hts,shd->thd', probs, values, precision=HIGH).reshape(tokens, width)
    after_attn = start_x + low_back(matmul(low(low_back(mixed)), attend_out_low))
    normed_two = rms_norm(after_attn, gains[1])
    normed_low = low(normed_two)
    logits = matmul(normed_low, router_low)
    gate_probs = jax.nn.softmax(logits[:, :routed], -1)
    alphas = [jax.nn.softmax(logits[:, routed + 2 * which:routed + 2 * which + 2], -1) for which in range(2)]
    flat = picks.reshape(-1)
    onehot = (flat[:, None] == jnp.arange(routed)[None, :]).astype(jnp.int32)
    slots = lax.optimization_barrier(jnp.sum((jnp.cumsum(onehot, 0) - onehot) * onehot, 1))
    target = jnp.where(flat < experts, flat * CAP + slots, experts * CAP).astype(jnp.int32)
    sources = (jnp.arange(flat.shape[0]) // 2).astype(jnp.int32)
    sent_rows = low_back(normed_low[sources])
    buffer = jnp.zeros((experts * CAP, width), jnp.float32).at[target].add(sent_rows, mode='drop')
    buffer = buffer.reshape(experts, CAP, width)
    inner = low_back(jnp.einsum('ecd,edf->ecf', buffer, expert_in_low, precision=HIGH))
    active = low(jax.nn.silu(inner[..., :hidden_units]) * inner[..., hidden_units:])
    result = low(low_back(jnp.einsum('ecf,efd->ecd', active, expert_out_low, precision=HIGH)))
    fetched = result.reshape(experts * CAP, width).at[target].get(mode='fill', fill_value=0.0)
    fetched = fetched.reshape(tokens, 2, width)
    gate_pick = jnp.take_along_axis(gate_probs, picks, 1)
    is_copy = (picks == experts + 1).astype(jnp.float32)[..., None]
    branch = fetched + is_copy * normed_two[:, None, :]
    for which in range(2):
        chosen = (picks == experts + 2 + which).astype(jnp.float32)[..., None]
        constant = alphas[which][:, None, 0:1] * normed_two[:, None, :] + alphas[which][:, None, 1:2] * const_vectors[which]
        branch = branch + chosen * constant
    after_ffn = after_attn + lax.optimization_barrier(jnp.sum(gate_pick[..., None] * branch, 1))
    final = rms_norm(after_ffn, gains[2])
    score = jnp.dot(final, score_head, precision=HIGH)
    spots = PROMPT + jnp.arange(NCONT) * CLEN + last
    picked = score[spots]
    margin = picked[pair[:, 0]] - picked[pair[:, 1]]
    return jnp.sum(jax.nn.softplus(-margin))

def adam_update(weight, first, second, grad, rate, decay):
    first = BETA_ONE * first + (1.0 - BETA_ONE) * grad
    second = BETA_TWO * second + (1.0 - BETA_TWO) * grad * grad
    step_dir = first / (1.0 - BETA_ONE ** ADAM_STEP) / (jnp.sqrt(second / (1.0 - BETA_TWO ** ADAM_STEP)) + ADAM_EPS)
    return (weight - rate * (step_dir + decay * weight), first, second)

def reference(token_ids, routes, last_valid, rank_pairs, embedding, embedding_first, embedding_second, attend_in, attend_in_first, attend_in_second, attend_out, attend_out_first, attend_out_second, expert_in, expert_in_first, expert_in_second, expert_out, expert_out_first, expert_out_second, router, router_first, router_second, norm_gains, norm_gains_first, norm_gains_second, const_vectors, const_vectors_first, const_vectors_second, score_head, score_head_first, score_head_second):
    weights = (embedding, attend_in, attend_out, expert_in, expert_out, router, norm_gains, const_vectors, score_head)
    firsts = (embedding_first, attend_in_first, attend_out_first, expert_in_first, expert_out_first, router_first, norm_gains_first, const_vectors_first, score_head_first)
    seconds = (embedding_second, attend_in_second, attend_out_second, expert_in_second, expert_out_second, router_second, norm_gains_second, const_vectors_second, score_head_second)

    def total_loss(params):
        lowered = tuple((low(member) for member in params[:6]))
        checked = jax.checkpoint(group_loss)

        def one_group(accum, group):
            return (accum + checked(lowered, params[6], params[7], params[8], *group), None)
        total, _ = lax.scan(one_group, jnp.float32(0.0), (token_ids, routes, last_valid, rank_pairs))
        return total
    loss_total, pull = jax.vjp(total_loss, weights)
    grads = pull(jnp.float32(1.0 / (GROUPS * NPAIR)))[0]
    square = jnp.float32(0.0)
    for member in grads:
        square = square + jnp.sum(member * member)
    norm_total = jnp.sqrt(square)
    factor = THRESH / jnp.maximum(norm_total, THRESH)
    rates = learn_rates()
    made = [adam_update(weights[which], firsts[which], seconds[which], grads[which] * factor, rates[which], DECAYS[which]) for which in range(9)]
    return (made[0][0], made[0][1], made[0][2], made[1][0], made[1][1], made[1][2], made[2][0], made[2][1], made[2][2], made[3][0], made[3][1], made[3][2], made[4][0], made[4][1], made[4][2], made[5][0], made[5][1], made[5][2], made[6][0], made[6][1], made[6][2], made[7][0], made[7][1], made[7][2], made[8][0], made[8][1], made[8][2], loss_total, norm_total)
```

```python
import functools

import jax
import jax.numpy as jnp
import ml_dtypes
import numpy as np
from jax import lax
from jax.experimental import pallas as pl
from jax.experimental.pallas import tpu as pltpu
from jax.sharding import PartitionSpec as P

D = 768
HEAD = 64
FF = 2048
PROMPT = 512
CLEN = 128
NCONT = 4
NPAIR = 4
ADAM_STEP = 5
TOK = PROMPT + NCONT * CLEN
SPAN = PROMPT + CLEN
HALF = HEAD // 2
QUAD = 4
TILE = 256
ROWS = 256
WINDOW = 1024
KEEP = 65536
TOK_BITS = TOK.bit_length() - 1
CLEN_BITS = CLEN.bit_length() - 1
LANES = 128

HIGH = lax.Precision.HIGHEST
EPS_NORM = 1e-05
THRESH = 0.05
BETA_ONE = 0.5
BETA_TWO = 0.5
ADAM_EPS = 1e-08
ROPE_BASE = 10000.0
DECAYS = (0.1, 0.1, 0.1, 0.1, 0.1, 0.1, 0.0, 0.0, 0.0)
BFLOAT = jnp.bfloat16
FLOAT = jnp.float32
BOTH = ("dp", "expert")
SCALE = HEAD ** (-0.5)
FAR = -1e30
VMEM_LIMIT = 62 * 1024 * 1024


def learn_rates():
    return (
        1.0,
        D ** (-0.5),
        (D * 16 // PROMPT) ** (-0.5),
        D ** (-0.5),
        (FF // 64) ** (-0.5),
        (2 * D) ** (-0.5),
        0.5,
        1.0,
        D ** (-0.5),
    )


def rms_forward(values, gain):
    factor = lax.rsqrt(jnp.mean(values * values, -1, keepdims=True) + EPS_NORM)
    return (values * factor * gain, factor)


def rms_backward(values, factor, gain, upstream):
    weighted = upstream * gain
    inner = jnp.mean(weighted * values, -1, keepdims=True)
    return (
        factor * weighted - values * factor * factor * factor * inner,
        jnp.sum(upstream * values * factor, 0),
    )


def adam_update(weight, first, second, grad, rate, decay):
    first = BETA_ONE * first + (1.0 - BETA_ONE) * grad
    second = BETA_TWO * second + (1.0 - BETA_TWO) * grad * grad
    step_dir = (
        first
        / (1.0 - BETA_ONE**ADAM_STEP)
        / (jnp.sqrt(second / (1.0 - BETA_TWO**ADAM_STEP)) + ADAM_EPS)
    )
    return (weight - rate * (step_dir + decay * weight), first, second)


def rope_constants():
    freq = np.float32(ROPE_BASE) ** (-np.arange(HALF, dtype=np.float32) / np.float32(HALF))
    angle = np.arange(SPAN, dtype=np.float32)[:, None] * freq.astype(np.float32)[None, :]
    angle = angle.astype(np.float64)
    return np.cos(angle).astype(np.float32), np.sin(angle).astype(np.float32)


def rope_split():
    parts = []
    for table in rope_constants():
        high = table.astype(ml_dtypes.bfloat16)
        low = (table - high.astype(np.float32)).astype(ml_dtypes.bfloat16)
        parts += [np.tile(high, (1, QUAD)), np.tile(low, (1, QUAD))]
    return np.concatenate(parts, 1)


def spread(array, axes):
    count = lax.axis_size(axes)
    return lax.all_to_all(
        jnp.broadcast_to(array[None], (count,) + array.shape), axes, 0, 0, tiled=True
    )


def swap(array, axes):
    return lax.all_to_all(array, axes, 0, 0, tiled=True)


def contract(left, right, dims):
    return lax.dot_general(left, right, (dims, ((), ())), preferred_element_type=FLOAT)


NN = ((1,), (0,))
NT = ((1,), (1,))
TN = ((0,), (0,))


def tile_tokens(key_row, token_bits):
    real = key_row >= 0
    local = lax.shift_right_arithmetic(key_row, token_bits)
    place = key_row & (TOK - 1)
    group = lax.shift_right_arithmetic(key_row & ((1 << token_bits) - 1), TOK_BITS)
    late = place - PROMPT
    seg = lax.shift_right_arithmetic(late, CLEN_BITS) + 1
    code = group * 8 + jnp.where(late < 0, 0, seg)
    spot = jnp.where(late < 0, place, PROMPT + (late & (CLEN - 1)))
    return jnp.where(real, local, -1), jnp.where(real, code, -1), spot


def to_column(row):
    return jnp.transpose(jnp.broadcast_to(row.astype(FLOAT), (8, TILE)))[:, 0:1].astype(jnp.int32)


def one_hot(matches):
    return matches.astype(FLOAT).astype(BFLOAT)


def tile_rows(id_col, low, high, embed_ref, start_ref):
    limit = embed_ref.shape[0]
    window = min(WINDOW, limit)
    align = 16
    origin = lax.div(low, align) * align
    lanes = lax.broadcasted_iota(jnp.int32, (TILE, window), 1)

    def pick(turn):
        least = origin + turn * window
        base = pl.multiple_of(jnp.minimum(least, limit - window), align)
        wanted = jnp.where(id_col >= least, id_col - base, -1)
        return contract(one_hot(wanted == lanes), embed_ref[pl.ds(base, window), :], NN)

    start_ref[...] = pick(0)

    def more(turn, carry):
        start_ref[...] += pick(turn)
        return carry

    lax.fori_loop(1, lax.div(high - origin, window) + 1, more, 0)
    return start_ref[...]


def tile_rope(pos_col, table_ref):
    spots = lax.broadcasted_iota(jnp.int32, (TILE, SPAN), 1)
    both = contract(one_hot(pos_col == spots), table_ref[...], NN)
    cosine = both[:, :LANES] + both[:, LANES : 2 * LANES]
    sine = both[:, 2 * LANES : 3 * LANES] + both[:, 3 * LANES :]
    return cosine, sine


def forward_kernel(
    token_bits,
    count_ref,
    first_ref,
    last_ref,
    info_ref,
    embed_ref,
    gain_ref,
    keys_w_ref,
    values_w_ref,
    table_ref,
    query_ref,
    own_ref,
    base_ref,
    out_ref,
    peak_ref,
    total_ref,
    *rest,
):
    kept = len(rest) > 1
    start_ref = rest[2] if kept else rest[0]
    out_ref[...] = jnp.zeros_like(out_ref)
    peak_ref[...] = jnp.full_like(peak_ref, FAR)
    total_ref[...] = jnp.zeros_like(total_ref)

    def saves(step):
        start_out, rope_out, _, start_buf, rope_buf, sems = rest
        slot = lax.rem(step, 2)
        place = pl.ds(pl.multiple_of(step * TILE, TILE), TILE)
        return (
            pltpu.make_async_copy(start_buf.at[slot], start_out.at[place], sems.at[0, slot]),
            pltpu.make_async_copy(rope_buf.at[slot], rope_out.at[place], sems.at[1, slot]),
        )

    def body(step, carry):
        id_row, code_row, pos_row = tile_tokens(info_ref[step], token_bits)
        id_col, pos_col = to_column(id_row), to_column(pos_row)
        start = tile_rows(id_col, first_ref[step], last_ref[step], embed_ref, start_ref)
        factor = lax.rsqrt(jnp.mean(start * start, -1, keepdims=True) + EPS_NORM)
        normed = (start * factor * gain_ref[...]).astype(BFLOAT)
        cosine, sine = tile_rope(pos_col, table_ref)
        if kept:

            @pl.when(step >= 2)
            def _():
                for copy in saves(step - 2):
                    copy.wait()

            slot = lax.rem(step, 2)
            rest[3][slot] = start.astype(BFLOAT)
            rest[4][slot] = jnp.concatenate([cosine, sine], 1)
            for copy in saves(step):
                copy.start()
        raw = contract(normed, keys_w_ref[...], NN)
        former, latter = raw[:, :LANES], raw[:, LANES:]
        keys = jnp.concatenate(
            [former * cosine - latter * sine, latter * cosine + former * sine], 1
        ).astype(BFLOAT)
        values = contract(normed, values_w_ref[...], NN).astype(BFLOAT)
        scores = contract(query_ref[...], keys, NT)
        seen = (own_ref[...] == code_row) | (base_ref[...] == code_row)
        scores = jnp.where(seen, scores, FAR)
        peak = peak_ref[...]
        newer = jnp.maximum(peak, jnp.max(scores, 1, keepdims=True))
        expos = jnp.where(seen, jnp.exp(scores - newer[:, 0:1]), 0.0)
        shrink = jnp.exp(peak - newer)
        peak_ref[...] = newer
        total_ref[...] = total_ref[...] * shrink + jnp.sum(expos, 1, keepdims=True)
        out_ref[...] = out_ref[...] * shrink[:, 0:1] + contract(
            expos.astype(BFLOAT), values, NN
        )
        return carry

    count = count_ref[0]
    lax.fori_loop(0, count, body, 0)
    if kept:
        for back in (2, 1):

            @pl.when(count >= back)
            def _():
                for copy in saves(count - back):
                    copy.wait()


def backward_kernel(
    kept,
    chunks,
    blocks,
    token_bits,
    steps_ref,
    owner_ref,
    first_ref,
    last_ref,
    scored_ref,
    info_ref,
    start_in_ref,
    rope_in_ref,
    gain_ref,
    keys_w_ref,
    values_w_ref,
    back_w_ref,
    query_ref,
    query_t_ref,
    upper_in_ref,
    upper_t_in_ref,
    mixed_t_ref,
    level_ref,
    own_ref,
    base_ref,
    grad_embed_ref,
    grad_w_ref,
    grad_query_ref,
    grad_gain_ref,
    met_ref,
    square_ref,
    sum_ref,
    sum_b_ref,
    upper_ref,
    upper_t_ref,
    inner_ref,
    lowered_ref,
    grad_kv_ref,
    start_ref,
    grad_keys_ref,
    grad_values_ref,
    copy_sem,
    *loaded,
):
    wide = 2 * LANES
    limit = sum_ref.shape[0]
    count = steps_ref[0]

    def loads(step):
        start_buf, rope_buf, sems = loaded
        slot = lax.rem(step, 2)
        place = pl.ds(pl.multiple_of(step * TILE, TILE), TILE)
        return (
            pltpu.make_async_copy(start_in_ref.at[place], start_buf.at[slot], sems.at[0, slot]),
            pltpu.make_async_copy(rope_in_ref.at[place], rope_buf.at[slot], sems.at[1, slot]),
        )

    if kept:

        @pl.when(count > 0)
        def _():
            for copy in loads(0):
                copy.start()

    def clear(block, carry):
        place = pl.ds(pl.multiple_of(block * ROWS, ROWS), ROWS)
        sum_ref[place, :] = jnp.zeros((ROWS, sum_ref.shape[1]), FLOAT)
        return carry

    lax.fori_loop(0, limit // ROWS, clear, 0)
    grad_w_ref[...] = jnp.zeros_like(grad_w_ref)
    grad_query_ref[...] = jnp.zeros_like(grad_query_ref)
    grad_gain_ref[...] = jnp.zeros_like(grad_gain_ref)
    owner = owner_ref[0]
    mine = pl.ds(pl.multiple_of(owner * LANES, LANES), LANES)
    part = grad_w_ref.shape[1]
    mine_kv = pl.ds(pl.multiple_of(owner * part, LANES), part)
    lane_head = lax.broadcasted_iota(jnp.int32, (LANES, wide), 1)
    row_head = lax.broadcasted_iota(jnp.int32, (wide, LANES), 0)

    def unfold(chunk, carry):
        for block in range(blocks):
            place = slice(block * wide, (block + 1) * wide)
            upper = upper_in_ref[chunk, :, place].astype(FLOAT)
            upper_t = upper_t_in_ref[chunk, place, :].astype(FLOAT)
            joint = upper_t * mixed_t_ref[chunk, place, :].astype(FLOAT)
            for head in range(QUAD):
                low, high = head * HEAD, (head + 1) * HEAD
                cut = slice(head * LANES, (head + 1) * LANES)
                kept_lanes = (lane_head >= low) & (lane_head < high)
                kept_rows = (row_head >= low) & (row_head < high)
                upper_ref[chunk, block, cut, :] = jnp.where(kept_lanes, upper, 0.0).astype(BFLOAT)
                upper_t_ref[chunk, block, :, cut] = jnp.where(kept_rows, upper_t, 0.0).astype(
                    BFLOAT
                )
                inner_ref[chunk, block, :, cut] = jnp.sum(joint[low:high], 0, keepdims=True)
        return carry

    lax.fori_loop(0, chunks, unfold, 0)

    def body(step, carry):
        tile_step(step)
        return carry

    def tile_step(step):
        if kept:
            key_row = info_ref[step]
        else:
            slab_buf, slab_sem = loaded
            copy = pltpu.make_async_copy(info_ref.at[step], slab_buf, slab_sem)
            copy.start()
            copy.wait()
            key_row = slab_buf[...]
        id_row, code_row, pos_row = tile_tokens(key_row, token_bits)
        code_col = to_column(code_row)
        if kept:

            @pl.when(step + 1 < count)
            def _():
                for copy in loads(step + 1):
                    copy.start()

            for copy in loads(step):
                copy.wait()
            slot = lax.rem(step, 2)
            start = loaded[0][slot].astype(FLOAT)
            cosine, sine = loaded[1][slot, :, :LANES], loaded[1][slot, :, LANES:]
        else:
            id_col, pos_col = to_column(id_row), to_column(pos_row)
            start = tile_rows(id_col, first_ref[step], last_ref[step], start_in_ref, start_ref)
            cosine, sine = tile_rope(pos_col, rope_in_ref)
        factor = lax.rsqrt(jnp.mean(start * start, -1, keepdims=True) + EPS_NORM)
        normed = (start * factor * gain_ref[...]).astype(BFLOAT)
        raw = contract(normed, keys_w_ref[...], NN)
        values = contract(normed, values_w_ref[...], NN).astype(BFLOAT)
        keys = []
        for block in range(blocks):
            former = raw[:, block * wide : block * wide + LANES]
            latter = raw[:, block * wide + LANES : (block + 1) * wide]
            keys.append(
                jnp.concatenate(
                    [former * cosine - latter * sine, latter * cosine + former * sine], 1
                ).astype(BFLOAT)
            )
        if chunks > 1:
            grad_keys_ref[...] = jnp.zeros_like(grad_keys_ref)
            grad_values_ref[...] = jnp.zeros_like(grad_values_ref)

        def attend(chunk):
            seen = (code_col == own_ref[chunk]) | (code_col == base_ref[chunk])
            hidden = jnp.where(seen, 0.0, FAR)
            hidden = jnp.concatenate([hidden] * QUAD, 1)
            for block in range(blocks):
                place = pl.ds(block * wide, wide)
                scores = contract(keys[block], query_t_ref[chunk, block], NN)
                weights = jnp.exp(scores - level_ref[chunk, block] + hidden)
                slopes = contract(
                    values[:, block * wide : (block + 1) * wide], upper_t_ref[chunk, block], NN
                )
                lowered = (weights * (slopes - inner_ref[chunk, block])).astype(BFLOAT)
                lowered_ref[...] = lowered
                grad_query_ref[chunk, block] += contract(keys[block], lowered_ref[:, mine], TN)
                grad_k = contract(lowered, query_ref[chunk, block], NN)
                grad_v = contract(weights.astype(BFLOAT), upper_ref[chunk, block], NN)
                if chunks > 1:
                    grad_keys_ref[:, place] += grad_k
                    grad_values_ref[:, place] += grad_v
                else:
                    grad_keys_ref[:, place] = grad_k
                    grad_values_ref[:, place] = grad_v

        if chunks > 1:
            lax.fori_loop(0, chunks, lambda chunk, c: (attend(chunk), c)[1], 0)
        else:
            attend(0)
        pieces = []
        for block in range(blocks):
            former = grad_keys_ref[:, pl.ds(block * wide, LANES)]
            latter = grad_keys_ref[:, pl.ds(block * wide + LANES, LANES)]
            pieces.append((former * cosine + latter * sine).astype(BFLOAT))
            pieces.append((latter * cosine - former * sine).astype(BFLOAT))
        grad_kv = jnp.concatenate(pieces + [grad_values_ref[...].astype(BFLOAT)], 1)
        grad_kv_ref[...] = grad_kv
        grad_w_ref[...] += contract(normed, grad_kv_ref[:, mine_kv], TN)
        grad_normed = contract(grad_kv, back_w_ref[...], NN)
        scaled = start * factor
        grad_gain_ref[...] += jnp.sum(grad_normed * scaled, 0, keepdims=True)
        weighted = grad_normed * gain_ref[...]
        inner = jnp.mean(weighted * scaled, -1, keepdims=True)
        grad_start = (factor * (weighted - scaled * inner)).astype(BFLOAT)
        rows = lax.broadcasted_iota(jnp.int32, (ROWS, TILE), 0)

        def put(block, carry):
            base = pl.multiple_of(block * ROWS, ROWS)
            sum_ref[pl.ds(base, ROWS), :] += contract(one_hot(id_row == rows + base), grad_start, NN)
            return carry

        lax.fori_loop(
            lax.div(first_ref[step], ROWS), lax.div(last_ref[step], ROWS) + 1, put, 0
        )

    lax.fori_loop(0, count, body, 0)

    def out_copy(base):
        place = pl.ds(base, ROWS)
        return pltpu.make_async_copy(sum_b_ref.at[place], grad_embed_ref.at[place], copy_sem)

    def send(block, total):
        base = pl.multiple_of(block * ROWS, ROWS)
        part = sum_ref[pl.ds(base, ROWS), :]
        sum_b_ref[pl.ds(base, ROWS), :] = part.astype(BFLOAT)
        out_copy(base).start()
        return total + jnp.sum((part * part).reshape(ROWS // 8, 8, -1), 0)

    square_ref[...] = lax.fori_loop(
        0, limit // ROWS, send, jnp.zeros(square_ref.shape, FLOAT)
    )

    def meet(spot, carry):
        met_ref[pl.ds(spot, 1), :] = sum_ref[pl.ds(scored_ref[spot], 1), :]
        return carry

    lax.fori_loop(0, met_ref.shape[0], meet, 0)
    pltpu.make_async_copy(sum_b_ref, grad_embed_ref, copy_sem).wait()


def pick_kernel(rows_ref, source_ref, picked_ref, copy_sem):
    count = picked_ref.shape[0]

    def fetch(spot, carry):
        pltpu.make_async_copy(
            source_ref.at[pl.ds(rows_ref[spot], 1)], picked_ref.at[pl.ds(spot, 1)], copy_sem
        ).start()
        return carry

    lax.fori_loop(0, count, fetch, 0)
    pltpu.make_async_copy(source_ref.at[pl.ds(0, count)], picked_ref, copy_sem).wait()


def adam_kernel(
    rate,
    decay,
    factor_ref,
    ids_ref,
    extra_ref,
    weight_ref,
    first_ref,
    second_ref,
    grad_ref,
    weight_out,
    first_out,
    second_out,
):
    rows = weight_ref.shape[0]
    base = pl.program_id(0) * rows
    spots = lax.broadcasted_iota(jnp.int32, (rows, ids_ref.shape[1]), 0) + base
    chosen = (ids_ref[...] == spots).astype(FLOAT).astype(BFLOAT)
    extra = contract(chosen, extra_ref[...], NN)
    grad = (grad_ref[...].astype(FLOAT) + extra) * factor_ref[0]
    made = adam_update(weight_ref[...], first_ref[...], second_ref[...], grad, rate, decay)
    weight_out[...], first_out[...], second_out[...] = made


VMEM_SPEC = pl.BlockSpec(memory_space=pltpu.VMEM)
SMEM_SPEC = pl.BlockSpec(memory_space=pltpu.SMEM)


def matrix_adam_kernel(
    rate, decay, factor_ref, weight_ref, first_ref, second_ref, grad_ref, weight_out, first_out, second_out
):
    units = grad_ref.shape[3]
    for source in range(grad_ref.shape[0]):
        place = slice(source * units, (source + 1) * units)
        grad = grad_ref[source, 0].astype(FLOAT) * factor_ref[0]
        made = adam_update(
            weight_ref[0, :, place], first_ref[0, :, place], second_ref[0, :, place], grad, rate, decay
        )
        weight_out[0, :, place], first_out[0, :, place], second_out[0, :, place] = made


def split_float(values):
    high = lax.reduce_precision(values, 8, 7)
    return jnp.concatenate([high, values - high], -1).astype(BFLOAT)


def join_float(parts):
    half = parts.shape[-1] // 2
    parts = parts.astype(FLOAT)
    return parts[..., :half] + parts[..., half:]


def shards(
    token_ids,
    routes,
    last_valid,
    rank_pairs,
    embedding,
    embedding_first,
    embedding_second,
    attend_in,
    attend_in_first,
    attend_in_second,
    attend_out,
    attend_out_first,
    attend_out_second,
    expert_in,
    expert_in_first,
    expert_in_second,
    expert_out,
    expert_out_first,
    expert_out_second,
    router,
    router_first,
    router_second,
    norm_gains,
    norm_gains_first,
    norm_gains_second,
    const_vectors,
    const_vectors_first,
    const_vectors_second,
    score_head,
    score_head_first,
    score_head_second,
):
    shard_count = lax.axis_size("dp")
    owners = lax.axis_size("expert")
    groups = shard_count * owners
    my_shard = lax.axis_index("dp")
    my_owner = lax.axis_index("expert")
    width = embedding.shape[1]
    heads = width // HEAD
    blocks = heads // QUAD
    per_owner = heads // owners
    local_experts = expert_in.shape[0]
    experts = local_experts * owners
    routed = experts + 4
    hidden_units = expert_in.shape[2] // 2
    shard_rows = embedding.shape[0]
    slice_rows = attend_in.shape[0]
    queries = groups * NCONT
    everything = groups * TOK
    far_key = jnp.iinfo(jnp.int32).max
    gain_row = norm_gains[0:1]

    packed = jnp.concatenate(
        [token_ids[0], last_valid[0], jnp.zeros(LANES - NCONT, jnp.int32)]
    )
    known = spread(packed, BOTH)

    shaped_in = attend_in.astype(BFLOAT).reshape(slice_rows, 3, per_owner, owners, HEAD)
    mine_in = lax.dynamic_index_in_dim(shaped_in, my_owner, 3, keepdims=False)
    mine_in, known = lax.optimization_barrier((mine_in, known))
    weights_e = spread(mine_in.reshape(slice_rows, 3 * per_owner * HEAD), "dp").reshape(
        width, 3, per_owner, HEAD
    )

    ids, last = known[:, :TOK], known[:, TOK : TOK + NCONT]

    def paired(part):
        cut = part.reshape(width, per_owner, 2, HALF)
        cut = jnp.pad(cut, ((0, 0), (0, QUAD - per_owner), (0, 0), (0, 0)))
        return cut.transpose(0, 2, 1, 3).reshape(width, 2 * QUAD * HALF)

    query_w_e, key_w_e = paired(weights_e[:, 0]), paired(weights_e[:, 1])
    value_w_e = jnp.pad(
        weights_e[:, 2].reshape(width, per_owner * HEAD),
        ((0, 0), (0, (QUAD - per_owner) * HEAD)),
    )

    places = jnp.arange(TOK, dtype=jnp.int32)
    offsets = jnp.arange(CLEN, dtype=jnp.int32)
    seen_late = (offsets[None, None, :] <= last[:, :, None]).reshape(groups, NCONT * CLEN)
    seen = jnp.concatenate([jnp.ones((groups, PROMPT), bool), seen_late], 1)
    local = ids - my_shard * shard_rows
    here = seen & (local >= 0) & (local < shard_rows)
    index = jnp.arange(everything, dtype=jnp.int32).reshape(groups, TOK)
    key = jnp.where(here, local * everything + index, far_key)
    ordered = lax.sort(key.reshape(-1))
    tile_count = (jnp.sum(here.astype(jnp.int32)) + TILE - 1) // TILE
    ordered = jnp.where(ordered == far_key, -1, ordered)
    info = ordered.reshape(everything // TILE, 1, TILE)
    token_bits = everything.bit_length() - 1
    rows_of = jnp.maximum(lax.shift_right_arithmetic(ordered, token_bits), 0)
    rows_of = rows_of.reshape(everything // TILE, TILE)
    first_row = rows_of[:, 0]
    last_row = jnp.max(rows_of, 1)
    tile_count = tile_count.reshape(1)

    at_last = (offsets[None, None, :] == last[:, :, None]).astype(jnp.int32)
    scored_ids = jnp.sum(ids[:, PROMPT:].reshape(groups, NCONT, CLEN) * at_last, 2)
    scored_local = scored_ids.reshape(-1) - my_shard * shard_rows
    scored_here = (scored_local >= 0) & (scored_local < shard_rows)
    scored_row = jnp.clip(scored_local, 0, shard_rows - 1)
    scored_row = scored_row.astype(jnp.int32)
    scored_start = pl.pallas_call(
        pick_kernel,
        out_shape=jax.ShapeDtypeStruct((queries, width), FLOAT),
        in_specs=[SMEM_SPEC, pl.BlockSpec(memory_space=pl.ANY)],
        out_specs=VMEM_SPEC,
        scratch_shapes=[pltpu.SemaphoreType.DMA],
    )(scored_row, embedding)
    scored_start = jnp.where(scored_here[:, None], scored_start, 0.0)
    scored_start = lax.reduce_precision(scored_start, 8, 7)
    scored_normed = rms_forward(scored_start, norm_gains[0])[0].astype(BFLOAT)
    cos_table, sin_table = rope_constants()
    late_cos, late_sin = jnp.asarray(cos_table[PROMPT:]), jnp.asarray(sin_table[PROMPT:])
    at_late = (offsets[None, :] == last.reshape(-1)[:, None]).astype(FLOAT)
    scored_cos = jnp.dot(at_late, late_cos, precision=HIGH)
    scored_sin = jnp.dot(at_late, late_sin, precision=HIGH)
    cos_wide, sin_wide = jnp.tile(scored_cos, (1, QUAD)), jnp.tile(scored_sin, (1, QUAD))
    raw = jnp.dot(scored_normed, query_w_e, preferred_element_type=FLOAT)
    former, latter = raw[:, :LANES], raw[:, LANES:]
    query_part = jnp.concatenate(
        [former * cos_wide - latter * sin_wide, latter * cos_wide + former * sin_wide], 1
    ).astype(BFLOAT)
    embed_late, query_part = lax.optimization_barrier((embedding, query_part))
    embed_b = embed_late.astype(BFLOAT)
    query_e = jnp.sum(spread(query_part, "dp").astype(FLOAT), 0)

    units = hidden_units // shard_count
    cut_in = expert_in.astype(BFLOAT).reshape(
        local_experts, slice_rows, 2, shard_count, units
    )
    cut_in, query_e = lax.optimization_barrier((cut_in.transpose(3, 0, 1, 2, 4), query_e))
    got_in = swap(cut_in, "dp")
    in_w = got_in.transpose(1, 0, 2, 3, 4).reshape(local_experts, width, 2 * units)

    lane_head = (jnp.arange(2 * LANES) % LANES) // HALF
    head_lanes = (lane_head[None, :] == jnp.arange(per_owner)[:, None]).astype(FLOAT)
    query_rows = (query_e[None] * SCALE * head_lanes[:, None, :]).astype(BFLOAT)
    query_rows = query_rows.reshape(per_owner * queries, 2 * LANES)
    base_code = (jnp.arange(queries, dtype=jnp.int32) // NCONT) * 8
    own_code = base_code + jnp.arange(queries, dtype=jnp.int32) % NCONT + 1
    table = jnp.asarray(rope_split())
    kept = everything <= KEEP
    any_spec = pl.BlockSpec(memory_space=pl.ANY)
    query_count = per_owner * queries
    kept_shapes = (
        jax.ShapeDtypeStruct((everything, width), BFLOAT),
        jax.ShapeDtypeStruct((everything, 2 * LANES), FLOAT),
    )
    attended, peaks, totals, *saved = pl.pallas_call(
        functools.partial(forward_kernel, token_bits),
        in_specs=[SMEM_SPEC] * 3 + [VMEM_SPEC] * 9,
        out_specs=(VMEM_SPEC,) * 3 + (any_spec,) * (2 * kept),
        scratch_shapes=[pltpu.VMEM((TILE, width), FLOAT)]
        + [
            pltpu.VMEM((2, TILE, width), BFLOAT),
            pltpu.VMEM((2, TILE, 2 * LANES), FLOAT),
            pltpu.SemaphoreType.DMA((2, 2)),
        ]
        * kept,
        out_shape=(
            jax.ShapeDtypeStruct((query_count, 2 * LANES), FLOAT),
            jax.ShapeDtypeStruct((query_count, LANES), FLOAT),
            jax.ShapeDtypeStruct((query_count, LANES), FLOAT),
        )
        + kept_shapes * kept,
        compiler_params=pltpu.CompilerParams(vmem_limit_bytes=VMEM_LIMIT),
        cost_estimate=pl.CostEstimate(
            flops=30_000_000_000, bytes_accessed=20_000_000, transcendentals=2_000_000
        ),
    )(
        tile_count,
        first_row,
        last_row,
        info,
        embed_b,
        gain_row,
        key_w_e,
        value_w_e,
        table,
        query_rows,
        jnp.tile(own_code, per_owner)[:, None],
        jnp.tile(base_code, per_owner)[:, None],
    )
    attended = attended.reshape(per_owner, queries, 2 * LANES)
    attended = jnp.stack(
        [attended[h, :, h * HEAD : (h + 1) * HEAD] for h in range(per_owner)], 1
    ).reshape(queries, per_owner * HEAD)
    peaks = peaks[:, 0].reshape(per_owner, queries).T
    totals = totals[:, 0].reshape(per_owner, queries).T
    start_cut = lax.dynamic_slice_in_dim(
        scored_start, my_owner * (width // owners), width // owners, 1
    )
    part = per_owner * HEAD
    filler = jnp.zeros((queries, LANES - 2 * per_owner), FLOAT)
    sent = jnp.concatenate([attended, start_cut, peaks, totals, filler], 1)
    sent, in_w = lax.optimization_barrier((sent, in_w))
    got = swap(sent.reshape(groups, NCONT, -1), BOTH)
    got = got.reshape(shard_count, owners, NCONT, -1)
    got_out = got[..., :part].reshape(shard_count, owners, NCONT, per_owner, HEAD)
    got_start = got[..., part : 2 * part]
    got_peak = got[..., 2 * part : 2 * part + per_owner]
    got_total = got[..., 2 * part + per_owner : 2 * part + 2 * per_owner]
    peak = jnp.max(got_peak, 0)
    share = jnp.exp(got_peak - peak[None])
    total = jnp.sum(share * got_total, 0)
    mixed = jnp.sum(share[..., None] * got_out, 0) / total[..., None]
    mixed = mixed.transpose(1, 2, 0, 3).reshape(NCONT, width)
    level = (peak + jnp.log(total)).transpose(1, 2, 0).reshape(NCONT, heads)
    start_x = jnp.sum(got_start, 0).transpose(1, 0, 2).reshape(NCONT, width)

    piece = slice_rows // owners
    out_w = lax.all_gather(
        lax.dynamic_slice_in_dim(attend_out.astype(BFLOAT), my_owner * piece, piece, 0),
        BOTH,
        tiled=True,
    )
    router_b = router.astype(BFLOAT)
    after_attn = start_x + jnp.dot(mixed.astype(BFLOAT), out_w, preferred_element_type=FLOAT)
    normed_two, factor_two = rms_forward(after_attn, norm_gains[1])
    normed_two_b = normed_two.astype(BFLOAT)
    logits = jnp.dot(normed_two_b, router_b, preferred_element_type=FLOAT)
    gate_probs = jax.nn.softmax(logits[:, :routed], -1)
    alphas = [
        jax.nn.softmax(logits[:, routed + 2 * which : routed + 2 * which + 2], -1)
        for which in range(2)
    ]
    own_last = last_valid[0]
    own_pick = (offsets[None, :] == own_last[:, None]).astype(jnp.int32)
    route_row = jnp.sum(
        routes[0, PROMPT:].reshape(NCONT, CLEN, 2) * own_pick[..., None], 1
    )
    pick_table = (route_row[:, :, None] == jnp.arange(routed)[None, None, :]).astype(FLOAT)
    gate_pick = jnp.sum(pick_table * gate_probs[:, None, :], -1)
    gate_full = jnp.sum(pick_table * gate_pick[..., None], 1)[:, :experts]
    fine = split_float(jnp.concatenate([level, gate_full], 1))
    tail = jnp.zeros((NCONT, LANES - 2 * (heads + experts)), BFLOAT)
    told = spread(
        jnp.concatenate(
            [normed_two_b, start_x.astype(BFLOAT), mixed.astype(BFLOAT), fine, tail], 1
        ),
        BOTH,
    ).reshape(queries, -1)
    all_normed_b = told[:, :width]
    all_start = told[:, width : 2 * width].astype(FLOAT)
    all_mixed_b = told[:, 2 * width : 3 * width]
    all_fine = join_float(told[:, 3 * width : 3 * width + 2 * (heads + experts)])
    all_level, all_gates = all_fine[:, :heads], all_fine[:, heads:]
    own_gates = lax.dynamic_slice_in_dim(all_gates, my_owner * local_experts, local_experts, 1)

    down_w = expert_out.astype(BFLOAT)
    inner_all, active_all, result_all = [], [], []
    for which in range(local_experts):
        inner = jnp.dot(all_normed_b, in_w[which], preferred_element_type=FLOAT)
        active = (jax.nn.silu(inner[:, :units]) * inner[:, units:]).astype(BFLOAT)
        inner_all.append(inner)
        active_all.append(active)
        result_all.append(jnp.dot(active, down_w[which], preferred_element_type=FLOAT))
    combined = sum(own_gates[:, w : w + 1] * result_all[w] for w in range(local_experts))
    fetched = jnp.sum(swap(combined.reshape(groups, NCONT, width), BOTH), 0)

    is_copy = (route_row == experts + 1).astype(FLOAT)[..., None]
    chosen = [(route_row == experts + 2 + which).astype(FLOAT)[..., None] for which in range(2)]
    branch = is_copy * normed_two[:, None, :]
    for which in range(2):
        constant = (
            alphas[which][:, None, 0:1] * normed_two[:, None, :]
            + alphas[which][:, None, 1:2] * const_vectors[which]
        )
        branch = branch + chosen[which] * constant
    after_ffn = after_attn + fetched + jnp.sum(gate_pick[..., None] * branch, 1)
    final, factor_three = rms_forward(after_ffn, norm_gains[2])
    picked = jnp.sum(final * score_head[None, :], -1)
    pair_rows = rank_pairs[0]
    lead = (pair_rows[:, 0:1] == jnp.arange(NCONT)[None, :]).astype(FLOAT)
    other = (pair_rows[:, 1:2] == jnp.arange(NCONT)[None, :]).astype(FLOAT)
    sides = lead - other
    margin = jnp.sum(sides * picked[None, :], 1)
    loss_part = jnp.sum(jax.nn.softplus(-margin))
    grad_margin = -jax.nn.sigmoid(-margin) * (1.0 / (groups * NPAIR))
    grad_picked = jnp.sum(sides * grad_margin[:, None], 0)
    grad_head = jnp.sum(grad_picked[:, None] * final, 0)
    grad_ffn, grad_gain_final = rms_backward(
        after_ffn, factor_three, norm_gains[2], grad_picked[:, None] * score_head[None, :]
    )
    all_ffn = spread(grad_ffn, BOTH).reshape(queries, width)

    grad_in, grad_out, back, dots = [], [], 0.0, []
    for which in range(local_experts):
        gate_half, up_half = inner_all[which][:, :units], inner_all[which][:, units:]
        grad_result = (own_gates[:, which : which + 1] * all_ffn).astype(BFLOAT)
        dots.append(jnp.sum(all_ffn * result_all[which], -1))
        grad_active = contract(grad_result, down_w[which], NT)
        grad_out.append(contract(active_all[which], grad_result, TN))
        sigma = jax.nn.sigmoid(gate_half)
        grad_gate = grad_active * up_half * sigma * (1.0 + gate_half * (1.0 - sigma))
        grad_up = grad_active * gate_half * sigma
        grad_inner = jnp.concatenate([grad_gate, grad_up], -1).astype(BFLOAT)
        grad_in.append(contract(all_normed_b, grad_inner, TN))
        back = back + contract(grad_inner, in_w[which], NT)
    grad_expert_out = jnp.stack(grad_out)
    grad_in = jnp.stack(grad_in)
    dots = jnp.stack(dots, 1)
    wide_dots = jnp.zeros((queries, LANES), FLOAT)
    wide_dots = lax.dynamic_update_slice_in_dim(wide_dots, dots, my_owner * local_experts, 1)
    returned = jnp.sum(
        swap(jnp.concatenate([back, wide_dots], 1).reshape(groups, NCONT, -1), BOTH), 0
    )
    returned_grad, returned_dots = returned[:, :width], returned[:, width : width + experts]
    grad_pick = jnp.sum(grad_ffn[:, None, :] * branch, -1) + jnp.sum(
        pick_table[:, :, :experts] * returned_dots[:, None, :], -1
    )
    grad_branch = gate_pick[..., None] * grad_ffn[:, None, :]
    grad_normed_two = returned_grad + jnp.sum(grad_branch * is_copy, 1)
    grad_vectors = []
    grad_alpha_parts = []
    for which in range(2):
        masked = jnp.sum(chosen[which] * grad_branch, 1)
        grad_vectors.append(jnp.sum(masked * alphas[which][:, 1:2], 0))
        grad_alpha = jnp.stack(
            [jnp.sum(masked * normed_two, -1), jnp.sum(masked * const_vectors[which], -1)], -1
        )
        grad_alpha_parts.append(
            alphas[which] * (grad_alpha - jnp.sum(alphas[which] * grad_alpha, -1, keepdims=True))
        )
        grad_normed_two = grad_normed_two + masked * alphas[which][:, 0:1]
    grad_probs = jnp.sum(pick_table * grad_pick[..., None], 1)
    grad_main = gate_probs * (grad_probs - jnp.sum(gate_probs * grad_probs, -1, keepdims=True))
    grad_logits = jnp.concatenate([grad_main] + grad_alpha_parts, -1)
    grad_normed_two = grad_normed_two + jnp.einsum(
        "tc,dc->td", grad_logits, router_b.astype(FLOAT), precision=HIGH
    )
    grad_attn_part, grad_gain_ffn = rms_backward(
        after_attn, factor_two, norm_gains[1], grad_normed_two
    )
    grad_after_attn = grad_ffn + grad_attn_part
    columns = grad_logits.shape[1]
    misc = jnp.concatenate(
        [
            grad_logits.reshape(-1),
            split_float(loss_part[None]).astype(FLOAT),
        ]
    )
    grad_attn_b = spread(grad_after_attn.astype(BFLOAT), BOTH).reshape(queries, width)

    cut_grad = grad_in.reshape(local_experts, shard_count, slice_rows, 2 * units)
    cut_grad = cut_grad.transpose(1, 0, 2, 3).astype(BFLOAT)
    cut_grad, grad_attn_b = lax.optimization_barrier((cut_grad, grad_attn_b))
    sum_expert_in = swap(cut_grad, "dp")

    weights_all = lax.all_gather(weights_e.reshape(width, 3 * per_owner * HEAD), "expert")
    weights_all = weights_all.reshape(owners, width, 3, per_owner, HEAD)
    weights_all = weights_all.transpose(2, 1, 3, 0, 4)
    query_w, key_w, value_w = weights_all.reshape(3, width, width)

    def folded(array):
        lead = array.shape[:-1]
        cut = array.reshape(lead + (blocks, QUAD, 2, HALF))
        return jnp.swapaxes(cut, -3, -2).reshape(lead + (width,))

    def unfolded(array):
        lead = array.shape[:-1]
        cut = array.reshape(lead + (blocks, 2, QUAD, HALF))
        return jnp.swapaxes(cut, -3, -2).reshape(lead + (width,))

    key_w_f = folded(key_w)
    all_normed_one = rms_forward(all_start, norm_gains[0])[0].astype(BFLOAT)
    raw = jnp.dot(all_normed_one, query_w, preferred_element_type=FLOAT)
    raw = raw.reshape(queries, heads, 2, HALF)
    cos_one, sin_one = scored_cos[:, None, :], scored_sin[:, None, :]
    all_query = jnp.stack(
        [
            raw[:, :, 0] * cos_one - raw[:, :, 1] * sin_one,
            raw[:, :, 1] * cos_one + raw[:, :, 0] * sin_one,
        ],
        2,
    ).astype(BFLOAT)
    all_query = folded(all_query.reshape(queries, width))
    chunk = min(queries, LANES)
    chunks = queries // chunk

    def by_head(array, lane_owner):
        cut = array.reshape(chunks, 1, chunk, blocks, 2 * LANES).transpose(0, 3, 1, 2, 4)
        keep = (lane_owner[None, :] == jnp.arange(QUAD)[:, None]).astype(array.dtype)
        cut = cut * keep[None, None, :, None, :]
        return cut.reshape(chunks, blocks, QUAD * chunk, 2 * LANES)

    def by_row(array):
        cut = array.reshape(chunks, chunk, blocks, QUAD).transpose(0, 2, 3, 1)
        return cut.reshape(chunks, blocks, 1, QUAD * chunk)

    grad_mixed = contract(grad_attn_b, out_w, NT).astype(BFLOAT)
    sum_attend_out = contract(
        lax.dynamic_slice_in_dim(all_mixed_b, my_shard * slice_rows, slice_rows, 1),
        grad_attn_b,
        TN,
    )
    query_blocks = by_head(all_query * jnp.asarray(SCALE, BFLOAT), lane_head)
    uppers = grad_mixed.reshape(chunks, chunk, width)
    mixed_t = jnp.swapaxes(all_mixed_b.reshape(chunks, chunk, width), 1, 2)
    side = QUAD * chunk
    quarter = 2 * width // owners
    grad_embed, grad_kv, grad_query, grad_gain, met, embed_square = pl.pallas_call(
        functools.partial(backward_kernel, kept, chunks, blocks, token_bits),
        in_specs=[SMEM_SPEC] * 5
        + ([VMEM_SPEC] + [any_spec] * 2 if kept else [any_spec] + [VMEM_SPEC] * 2)
        + [VMEM_SPEC] * 12,
        out_specs=(any_spec,) + (VMEM_SPEC,) * 5,
        scratch_shapes=[
            pltpu.VMEM((shard_rows, width), FLOAT),
            pltpu.VMEM((shard_rows, width), BFLOAT),
            pltpu.VMEM((chunks, blocks, side, 2 * LANES), BFLOAT),
            pltpu.VMEM((chunks, blocks, 2 * LANES, side), BFLOAT),
            pltpu.VMEM((chunks, blocks, 1, side), FLOAT),
            pltpu.VMEM((TILE, side), BFLOAT),
            pltpu.VMEM((TILE, 2 * width), BFLOAT),
            pltpu.VMEM((TILE, width), FLOAT),
            pltpu.VMEM((TILE, width), FLOAT),
            pltpu.VMEM((TILE, width), FLOAT),
            pltpu.SemaphoreType.DMA,
        ]
        + (
            [
                pltpu.VMEM((2, TILE, width), BFLOAT),
                pltpu.VMEM((2, TILE, 2 * LANES), FLOAT),
                pltpu.SemaphoreType.DMA((2, 2)),
            ]
            if kept
            else [pltpu.VMEM((1, TILE), jnp.int32), pltpu.SemaphoreType.DMA]
        ),
        out_shape=(
            jax.ShapeDtypeStruct((shard_rows, width), BFLOAT),
            jax.ShapeDtypeStruct((width, quarter), FLOAT),
            jax.ShapeDtypeStruct((chunks, blocks, 2 * LANES, chunk), FLOAT),
            jax.ShapeDtypeStruct((1, width), FLOAT),
            jax.ShapeDtypeStruct((queries, width), FLOAT),
            jax.ShapeDtypeStruct((8, width), FLOAT),
        ),
        compiler_params=pltpu.CompilerParams(vmem_limit_bytes=VMEM_LIMIT),
        cost_estimate=pl.CostEstimate(
            flops=60_000_000_000, bytes_accessed=60_000_000, transcendentals=6_000_000
        ),
    )(
        tile_count,
        my_owner.astype(jnp.int32).reshape(1),
        first_row,
        last_row,
        scored_row,
        info,
        saved[0] if kept else embed_b,
        saved[1] if kept else table,
        gain_row,
        key_w_f,
        value_w,
        jnp.concatenate([key_w_f, value_w], 1).T,
        query_blocks,
        jnp.swapaxes(query_blocks, 2, 3),
        uppers,
        jnp.swapaxes(uppers, 1, 2),
        mixed_t,
        by_row(all_level),
        own_code.reshape(chunks, 1, chunk),
        base_code.reshape(chunks, 1, chunk),
    )

    pieces = grad_query.reshape(chunks, blocks, 2, QUAD, HALF, chunk)
    pieces = lax.dynamic_index_in_dim(pieces, my_owner, 3, keepdims=False)
    pieces = pieces.transpose(0, 4, 1, 2, 3).reshape(groups, NCONT, part) * SCALE
    met = jnp.where(scored_here[:, None], met, 0.0)
    met = lax.dynamic_slice_in_dim(met, my_owner * part, part, 1).reshape(groups, NCONT, part)
    thin = width // groups
    sent = jnp.concatenate(
        [
            grad_kv.astype(BFLOAT).reshape(groups, thin, quarter),
            split_float(pieces),
            split_float(met),
        ],
        1,
    )
    sent, sum_expert_in = lax.optimization_barrier((sent, sum_expert_in))
    got = swap(sent, BOTH).reshape(shard_count, owners, thin + 2 * NCONT, quarter)
    sum_kv = jnp.sum(got[:, :, :thin].astype(FLOAT), 0).transpose(1, 0, 2)
    sum_kv = sum_kv.reshape(thin, 2 * width)
    met = jnp.sum(join_float(got[:, :, thin + NCONT :]), 0).transpose(1, 0, 2)
    met = met.reshape(NCONT, width)
    got = jnp.sum(join_float(got[:, :, thin : thin + NCONT]), 0)
    got = got.reshape(owners, NCONT, per_owner, HEAD)
    turned = got.transpose(1, 2, 0, 3).reshape(NCONT, heads, 2, HALF)
    own_late = (offsets[None, :] == own_last[:, None]).astype(FLOAT)
    own_cos = jnp.dot(own_late, late_cos, precision=HIGH)[:, None, :]
    own_sin = jnp.dot(own_late, late_sin, precision=HIGH)[:, None, :]
    own_grad_query = jnp.stack(
        [
            turned[:, :, 0] * own_cos + turned[:, :, 1] * own_sin,
            turned[:, :, 1] * own_cos - turned[:, :, 0] * own_sin,
        ],
        2,
    ).reshape(NCONT, width)
    own_grad_query = own_grad_query.astype(BFLOAT)
    grad_normed_one = contract(own_grad_query, query_w, NT)
    factor_one = rms_forward(start_x, norm_gains[0])[1]
    grad_start_part, grad_gain_query = rms_backward(
        start_x, factor_one, norm_gains[0], grad_normed_one
    )
    own_extra = lax.reduce_precision(grad_after_attn + grad_start_part, 8, 7)
    leader = (my_owner == 0).astype(FLOAT)
    local_square = (
        jnp.sum(grad_in * grad_in)
        + jnp.sum(grad_expert_out * grad_expert_out)
        + jnp.sum(sum_kv * sum_kv)
        + 2.0 * jnp.sum(met * own_extra)
        + leader * (jnp.sum(embed_square) + jnp.sum(sum_attend_out * sum_attend_out))
    )
    misc = jnp.concatenate([misc, split_float(local_square[None]).astype(FLOAT)])
    misc = jnp.pad(misc, (0, width - misc.shape[0]))
    gain_part = grad_gain_query + grad_gain[0] * (1.0 / owners)
    rows = [gain_part, grad_gain_ffn, grad_gain_final] + grad_vectors + [grad_head, misc, 0.0 * misc]
    told = spread(
        jnp.concatenate(
            [own_extra, own_grad_query.astype(FLOAT), jnp.stack(rows)]
        ).astype(BFLOAT),
        BOTH,
    )
    all_extra_b = told[:, :NCONT].reshape(queries, width)
    all_extra = all_extra_b.astype(FLOAT)
    all_grad_query = told[:, NCONT : 2 * NCONT].reshape(queries, width)
    small = jnp.sum(told[:, 2 * NCONT : 2 * NCONT + 6].astype(FLOAT), 0)
    sum_gains, sum_vectors, sum_head = small[:3], small[3:5], small[5]
    all_misc = told[:, 2 * NCONT + 6].astype(FLOAT)
    all_logits = all_misc[:, : NCONT * columns].reshape(queries, columns)
    totals = jnp.sum(all_misc[:, NCONT * columns : NCONT * columns + 4], 0)
    loss_total, spread_square = totals[0] + totals[1], totals[2] + totals[3]
    sum_router = jnp.einsum(
        "td,tc->dc", all_normed_b.astype(FLOAT), all_logits, precision=HIGH
    )
    sum_query_w = contract(
        lax.dynamic_slice_in_dim(all_normed_one, my_shard * slice_rows, slice_rows, 1),
        all_grad_query,
        TN,
    )

    same = (scored_ids.reshape(-1, 1) == scored_ids.reshape(1, -1)).astype(FLOAT)
    query_square = contract(all_normed_one, all_normed_one, NT) * contract(
        all_grad_query, all_grad_query, NT
    )
    small_square = (
        jnp.sum(contract(all_extra_b, all_extra_b, NT) * same)
        + jnp.sum(query_square)
        + jnp.sum(sum_router * sum_router)
        + jnp.sum(sum_gains * sum_gains)
        + jnp.sum(sum_vectors * sum_vectors)
        + jnp.sum(sum_head * sum_head)
    )
    norm_total = jnp.sqrt(spread_square + small_square)
    factor = THRESH / jnp.maximum(norm_total, THRESH)
    sum_kv, factor = lax.optimization_barrier((sum_kv, factor))
    all_kv = spread(sum_kv, "expert").reshape(slice_rows, 2 * width)
    sum_attend_in = jnp.concatenate(
        [sum_query_w, unfolded(all_kv[:, :width]), all_kv[:, width:]], 1
    )

    rates = learn_rates()
    block_rows = min(4 * ROWS, shard_rows)
    row_spec = pl.BlockSpec((block_rows, width), lambda i: (i, 0))
    whole_spec = pl.BlockSpec((queries, width), lambda i: (0, 0))
    made_embedding = pl.pallas_call(
        functools.partial(adam_kernel, rates[0], DECAYS[0]),
        grid=(shard_rows // block_rows,),
        out_shape=(jax.ShapeDtypeStruct((shard_rows, width), FLOAT),) * 3,
        in_specs=[
            SMEM_SPEC,
            pl.BlockSpec((1, queries), lambda i: (0, 0)),
            whole_spec,
        ]
        + [row_spec] * 4,
        out_specs=(row_spec,) * 3,
        compiler_params=pltpu.CompilerParams(vmem_limit_bytes=VMEM_LIMIT),
        cost_estimate=pl.CostEstimate(
            flops=4_000_000_000, bytes_accessed=176_000_000, transcendentals=12_000_000
        ),
    )(
        factor.reshape(1),
        jnp.where(scored_here, scored_local, -1)[None],
        all_extra_b,
        embedding,
        embedding_first,
        embedding_second,
        grad_embed,
    )
    cut_rows = 32
    cells = pl.BlockSpec((1, cut_rows, hidden_units), lambda l, h, r: (l, r, h))
    cut_spec = pl.BlockSpec((shard_count, 1, cut_rows, units), lambda l, h, r: (0, l, r, h))
    if units % LANES == 0 and slice_rows % cut_rows == 0:
        made_in = pl.pallas_call(
            functools.partial(matrix_adam_kernel, rates[3], DECAYS[3]),
            grid=(local_experts, 2, slice_rows // cut_rows),
            out_shape=(jax.ShapeDtypeStruct(expert_in.shape, FLOAT),) * 3,
            in_specs=[SMEM_SPEC] + [cells] * 3 + [cut_spec],
            out_specs=(cells,) * 3,
            compiler_params=pltpu.CompilerParams(vmem_limit_bytes=VMEM_LIMIT),
            cost_estimate=pl.CostEstimate(
                flops=100_000_000, bytes_accessed=20_000_000, transcendentals=1_600_000
            ),
        )(factor.reshape(1), expert_in, expert_in_first, expert_in_second, sum_expert_in)
    else:
        whole_in = sum_expert_in.astype(FLOAT).reshape(
            shard_count, local_experts, slice_rows, 2, units
        )
        whole_in = whole_in.transpose(1, 2, 3, 0, 4).reshape(expert_in.shape)
        made_in = adam_update(
            expert_in, expert_in_first, expert_in_second, whole_in * factor, rates[3], DECAYS[3]
        )
    weights = (
        attend_in,
        attend_out,
        None,
        expert_out,
        router,
        norm_gains,
        const_vectors,
        score_head,
    )
    firsts = (
        attend_in_first,
        attend_out_first,
        None,
        expert_out_first,
        router_first,
        norm_gains_first,
        const_vectors_first,
        score_head_first,
    )
    seconds = (
        attend_in_second,
        attend_out_second,
        None,
        expert_out_second,
        router_second,
        norm_gains_second,
        const_vectors_second,
        score_head_second,
    )
    summed = (
        sum_attend_in,
        sum_attend_out,
        None,
        grad_expert_out,
        sum_router,
        sum_gains,
        sum_vectors,
        sum_head,
    )
    made = list(made_embedding)
    for which in range(8):
        made += made_in if which == 2 else adam_update(
            weights[which],
            firsts[which],
            seconds[which],
            summed[which] * factor,
            rates[which + 1],
            DECAYS[which + 1],
        )
    return tuple(made) + (loss_total, norm_total)


def solution(mesh):
    pair = P(BOTH, None)
    triple = P(BOTH, None, None)
    rows = P("dp", None)
    cells = P("expert", "dp", None)
    placed = (pair, triple, pair, triple) + (rows,) * 9 + (cells,) * 6 + (P(),) * 12
    return jax.shard_map(
        shards,
        mesh=mesh,
        in_specs=placed,
        out_specs=(rows,) * 9 + (cells,) * 6 + (P(),) * 14,
        check_vma=False,
    )
```

```python
import functools

import jax
import jax.numpy as jnp
import ml_dtypes
import numpy as np
from jax import lax
from jax.experimental import pallas as pl
from jax.experimental.pallas import tpu as pltpu
from jax.sharding import PartitionSpec as P

D = 768
HEAD = 64
FF = 2048
PROMPT = 512
CLEN = 128
NCONT = 4
NPAIR = 4
ADAM_STEP = 5
TOK = PROMPT + NCONT * CLEN
SPAN = PROMPT + CLEN
HALF = HEAD // 2
QUAD = 4
TILE = 512
TILE_SMALL = 256
ROWS = 256
WINDOW = 1536
KEEP = 65536
TOK_BITS = TOK.bit_length() - 1
CLEN_BITS = CLEN.bit_length() - 1
HALF_BITS = HALF.bit_length() - 1
LANES = 128

HIGH = lax.Precision.HIGHEST
EPS_NORM = 1e-05
THRESH = 0.05
BETA_ONE = 0.5
BETA_TWO = 0.5
ADAM_EPS = 1e-08
ROPE_BASE = 10000.0
DECAYS = (0.1, 0.1, 0.1, 0.1, 0.1, 0.1, 0.0, 0.0, 0.0)
BFLOAT = jnp.bfloat16
FLOAT = jnp.float32
BOTH = ("dp", "expert")
SCALE = HEAD ** (-0.5)
FAR = -1e30
VMEM_LIMIT = 127 * 512 * 1024
SMALL_LIMIT = 16 * 1024 * 1024
FORWARD_LIMIT = 40 * 1024 * 1024


VMEM_SPEC = pl.BlockSpec(memory_space=pltpu.VMEM)
SMEM_SPEC = pl.BlockSpec(memory_space=pltpu.SMEM)


def learn_rates():
    return (
        1.0,
        D ** (-0.5),
        (D * 16 // PROMPT) ** (-0.5),
        D ** (-0.5),
        (FF // 64) ** (-0.5),
        (2 * D) ** (-0.5),
        0.5,
        1.0,
        D ** (-0.5),
    )


def rms_forward(values, gain):
    factor = lax.rsqrt(jnp.mean(values * values, -1, keepdims=True) + EPS_NORM)
    return (values * factor * gain, factor)


def rms_backward(values, factor, gain, upstream):
    weighted = upstream * gain
    inner = jnp.mean(weighted * values, -1, keepdims=True)
    return (
        factor * weighted - values * factor * factor * factor * inner,
        jnp.sum(upstream * values * factor, 0),
    )


def adam_update(weight, first, second, grad, rate, decay):
    first = BETA_ONE * first + (1.0 - BETA_ONE) * grad
    second = BETA_TWO * second + (1.0 - BETA_TWO) * grad * grad
    step_dir = (
        first
        / (1.0 - BETA_ONE**ADAM_STEP)
        / (jnp.sqrt(second / (1.0 - BETA_TWO**ADAM_STEP)) + ADAM_EPS)
    )
    return (weight - rate * (step_dir + decay * weight), first, second)


def rope_constants():
    freq = np.float32(ROPE_BASE) ** (-np.arange(HALF, dtype=np.float32) / np.float32(HALF))
    angle = np.arange(SPAN, dtype=np.float32)[:, None] * freq.astype(np.float32)[None, :]
    angle = angle.astype(np.float64)
    return np.cos(angle).astype(np.float32), np.sin(angle).astype(np.float32)


def rope_split():
    parts = []
    for table in rope_constants():
        high = table.astype(ml_dtypes.bfloat16)
        low = (table - high.astype(np.float32)).astype(ml_dtypes.bfloat16)
        parts += [np.tile(high, (1, QUAD)), np.tile(low, (1, QUAD))]
    return np.concatenate(parts, 1)


def spread(array, axes):
    count = lax.axis_size(axes)
    return lax.all_to_all(
        jnp.broadcast_to(array[None], (count,) + array.shape), axes, 0, 0, tiled=True
    )


def spread_made(copies, axes):
    return lax.all_to_all(copies, axes, 0, 0, tiled=True)


def swap(array, axes):
    return lax.all_to_all(array, axes, 0, 0, tiled=True)


def contract(left, right, dims):
    return lax.dot_general(left, right, (dims, ((), ())), preferred_element_type=FLOAT)


NN = ((1,), (0,))
NT = ((1,), (1,))
TN = ((0,), (0,))


def tile_tokens(key_row, token_bits):
    real = key_row >= 0
    local = lax.shift_right_arithmetic(key_row, token_bits)
    place = key_row & (TOK - 1)
    group = lax.shift_right_arithmetic(key_row & ((1 << token_bits) - 1), TOK_BITS)
    late = place - PROMPT
    seg = lax.shift_right_arithmetic(late, CLEN_BITS) + 1
    code = group * 8 + jnp.where(late < 0, 0, seg)
    spot = jnp.where(late < 0, place, PROMPT + (late & (CLEN - 1)))
    return jnp.where(real, local, -1), jnp.where(real, code, -1), spot


def to_column(row):
    return jnp.transpose(jnp.broadcast_to(row.astype(FLOAT), (8, row.shape[1])))[:, 0:1].astype(jnp.int32)


def one_hot(matches):
    return matches.astype(FLOAT).astype(BFLOAT)


def tile_rows(id_col, low, high, embed_ref, start_ref):
    limit = embed_ref.shape[0]
    window = min(WINDOW, limit)
    align = 16
    origin = lax.div(low, align) * align
    lanes = lax.broadcasted_iota(jnp.int32, (id_col.shape[0], window), 1)

    def pick(turn):
        least = origin + turn * window
        base = pl.multiple_of(jnp.minimum(least, limit - window), align)
        wanted = jnp.where(id_col >= least, id_col - base, -1)
        return contract(one_hot(wanted == lanes), embed_ref[pl.ds(base, window), :], NN)

    start_ref[...] = pick(0)

    def more(turn, carry):
        start_ref[...] += pick(turn)
        return carry

    lax.fori_loop(1, lax.div(high - origin, window) + 1, more, 0)
    return start_ref[...]


def tile_rope(pos_col, table_ref):
    spots = lax.broadcasted_iota(jnp.int32, (pos_col.shape[0], SPAN), 1)
    both = contract(one_hot(pos_col == spots), table_ref[...], NN)
    cosine = both[:, :LANES] + both[:, LANES : 2 * LANES]
    sine = both[:, 2 * LANES : 3 * LANES] + both[:, 3 * LANES :]
    return cosine, sine


def forward_kernel(
    token_bits,
    count_ref,
    first_ref,
    last_ref,
    info_ref,
    embed_ref,
    gain_ref,
    weights_ref,
    table_ref,
    query_ref,
    own_ref,
    base_ref,
    scored_ref,
    sent_ref,
    *rest,
):
    kept = len(rest) > 4
    *rest, out_ref, peak_ref, total_ref, start_ref = rest
    tile = info_ref.shape[2]
    if kept:
        *rest, embed_buf, whole_ref, embed_sems = rest
        slots, piece = embed_buf.shape[:2]
        pieces = whole_ref.shape[0] // piece

        def fetch(part):
            slot = lax.rem(part, slots)
            place = pl.ds(pl.multiple_of(part * piece, piece), piece)
            return pltpu.make_async_copy(
                embed_ref.at[place], embed_buf.at[slot], embed_sems.at[slot]
            )

        for part in range(min(slots, pieces)):
            fetch(part).start()

        def take(part, carry):
            fetch(part).wait()
            place = pl.ds(pl.multiple_of(part * piece, piece), piece)
            whole_ref[place, :] = embed_buf[lax.rem(part, slots)].astype(BFLOAT)

            @pl.when(part + slots < pieces)
            def _():
                fetch(part + slots).start()

            return carry

    else:
        whole_ref = embed_ref
    wide = 2 * LANES
    out_ref[...] = jnp.zeros_like(out_ref)
    peak_ref[...] = jnp.full_like(peak_ref, FAR)
    total_ref[...] = jnp.zeros_like(total_ref)

    def saves(step):
        start_out, rope_out, start_buf, rope_buf, sems = rest
        slot = lax.rem(step, 2)
        place = pl.ds(pl.multiple_of(step * tile, tile), tile)
        return (
            pltpu.make_async_copy(start_buf.at[slot], start_out.at[place], sems.at[0, slot]),
            pltpu.make_async_copy(rope_buf.at[slot], rope_out.at[place], sems.at[1, slot]),
        )

    def body(step, carry):
        id_row, code_row, pos_row = tile_tokens(info_ref[step], token_bits)
        id_col, pos_col = to_column(id_row), to_column(pos_row)
        low, high = first_ref[step], last_ref[step]
        taken = carry
        if kept:
            limit = whole_ref.shape[0]
            needed = jnp.minimum(limit, high + min(WINDOW, limit))
            wanted = lax.div(needed + piece - 1, piece)
            lax.fori_loop(taken, wanted, take, 0)
            taken = jnp.maximum(taken, wanted)
        start = tile_rows(id_col, low, high, whole_ref, start_ref)
        factor = lax.rsqrt(jnp.mean(start * start, -1, keepdims=True) + EPS_NORM)
        normed = (start * factor * gain_ref[...]).astype(BFLOAT)
        cosine, sine = tile_rope(pos_col, table_ref)
        if kept:

            @pl.when(step >= 2)
            def _():
                for copy in saves(step - 2):
                    copy.wait()

            slot = lax.rem(step, 2)
            rest[2][slot] = start.astype(BFLOAT)
            rest[3][slot] = jnp.concatenate([cosine, sine], 1)
            for copy in saves(step):
                copy.start()
        raw = contract(normed, weights_ref[:, wide : 2 * wide], NN)
        former, latter = raw[:, :LANES], raw[:, LANES:]
        keys = jnp.concatenate(
            [former * cosine - latter * sine, latter * cosine + former * sine], 1
        ).astype(BFLOAT)
        values = contract(normed, weights_ref[:, 2 * wide :], NN).astype(BFLOAT)
        scores = contract(query_ref[...], keys, NT)
        seen = (own_ref[...] == code_row) | (base_ref[...] == code_row)
        scores = jnp.where(seen, scores, FAR)
        peak = peak_ref[...]
        newer = jnp.maximum(peak, jnp.max(scores, 1, keepdims=True))
        expos = jnp.where(seen, jnp.exp(scores - newer[:, 0:1]), 0.0)
        shrink = jnp.exp(peak - newer)
        peak_ref[...] = newer
        total_ref[...] = total_ref[...] * shrink + jnp.sum(expos, 1, keepdims=True)
        out_ref[...] = out_ref[...] * shrink[:, 0:1] + contract(
            expos.astype(BFLOAT), values, NN
        )
        return taken

    count = count_ref[0]
    taken = lax.fori_loop(0, count, body, jnp.int32(0))
    if kept:
        lax.fori_loop(taken, pieces, take, 0)
    if kept:
        for back in (2, 1):

            @pl.when(count >= back)
            def _():
                for copy in saves(count - back):
                    copy.wait()

    queries, part = scored_ref.shape
    per_owner = part // HEAD
    cuts = [slice(head * queries, (head + 1) * queries) for head in range(per_owner)]
    mixed = [out_ref[cuts[h], h * HEAD : (h + 1) * HEAD] for h in range(per_owner)]
    fine = [peak_ref[cuts[h], 0:1] for h in range(per_owner)]
    fine += [total_ref[cuts[h], 0:1] for h in range(per_owner)]
    coarse = [value.astype(BFLOAT).astype(FLOAT) for value in fine]
    rest_of = [value - high for value, high in zip(fine, coarse)]
    filler = jnp.zeros((queries, sent_ref.shape[1] - 2 * part - 4 * per_owner), FLOAT)
    sent_ref[...] = jnp.concatenate(
        mixed + [scored_ref[...]] + coarse + rest_of + [filler], 1
    ).astype(BFLOAT)


def backward_kernel(
    kept,
    chunks,
    blocks,
    token_bits,
    fine_gap,
    steps_ref,
    owner_ref,
    first_ref,
    last_ref,
    scored_ref,
    info_ref,
    start_in_ref,
    rope_in_ref,
    gain_ref,
    both_ref,
    fold_ref,
    told_ref,
    upper_in_ref,
    cosine_ref,
    sine_ref,
    own_ref,
    base_ref,
    grad_embed_ref,
    grad_w_ref,
    grad_turned_ref,
    grad_gain_ref,
    met_ref,
    square_ref,
    sum_ref,
    stage_ref,
    both_w_ref,
    query_ref,
    query_t_ref,
    upper_ref,
    upper_t_ref,
    level_ref,
    inner_ref,
    lowered_ref,
    grad_query_ref,
    grad_kv_ref,
    start_ref,
    grad_keys_ref,
    grad_values_ref,
    copy_sem,
    *loaded,
):
    wide = 2 * LANES
    tile = info_ref.shape[2]
    limit = sum_ref.shape[0]
    count = steps_ref[0]

    def loads(step):
        start_buf, rope_buf, sems = loaded
        slot = lax.rem(step, 2)
        place = pl.ds(pl.multiple_of(step * tile, tile), tile)
        return (
            pltpu.make_async_copy(start_in_ref.at[place], start_buf.at[slot], sems.at[0, slot]),
            pltpu.make_async_copy(rope_in_ref.at[place], rope_buf.at[slot], sems.at[1, slot]),
        )

    if kept:

        @pl.when(count > 0)
        def _():
            for copy in loads(0):
                copy.start()

    def clear(block, carry):
        place = pl.ds(pl.multiple_of(block * ROWS, ROWS), ROWS)
        sum_ref[place, :] = jnp.zeros((ROWS, sum_ref.shape[1]), FLOAT)
        return carry

    lax.fori_loop(0, limit // ROWS, clear, 0)
    grad_w_ref[...] = jnp.zeros_like(grad_w_ref)
    grad_query_ref[...] = jnp.zeros_like(grad_query_ref)
    grad_gain_ref[...] = jnp.zeros_like(grad_gain_ref)
    owner = owner_ref[0]
    mine = pl.ds(pl.multiple_of(owner * LANES, LANES), LANES)
    part = grad_w_ref.shape[1]
    mine_kv = pl.ds(pl.multiple_of(owner * part, LANES), part)
    lane_head = lax.broadcasted_iota(jnp.int32, (LANES, wide), 1)
    row_head = lax.broadcasted_iota(jnp.int32, (wide, LANES), 0)

    width = gain_ref.shape[1]
    heads = blocks * QUAD
    query_w = contract(both_ref[:, :width], fold_ref[...], NN).astype(BFLOAT)
    both_w_ref[:, :width] = contract(both_ref[:, width : 2 * width], fold_ref[...], NN).astype(
        BFLOAT
    )
    both_w_ref[:, width:] = both_ref[:, 2 * width : 3 * width]

    def unfold(chunk, carry):
        begin = told_ref[chunk, :, width : 2 * width].astype(FLOAT)
        scale = lax.rsqrt(jnp.mean(begin * begin, -1, keepdims=True) + EPS_NORM)
        raw = contract((begin * scale * gain_ref[...]).astype(BFLOAT), query_w, NN)
        cos_one, sin_one = cosine_ref[chunk] * SCALE, sine_ref[chunk] * SCALE
        fine = told_ref[chunk, :, 3 * width :].astype(FLOAT)
        level = jnp.transpose(fine)
        upper_all = contract(upper_in_ref[chunk], both_ref[:, 3 * width :], NT)
        upper_all = upper_all.astype(BFLOAT).astype(FLOAT)
        joint_all = upper_all * told_ref[chunk, :, 2 * width : 3 * width].astype(FLOAT)
        for block in range(blocks):
            place = slice(block * wide, (block + 1) * wide)
            former = raw[:, block * wide : block * wide + LANES]
            latter = raw[:, block * wide + LANES : (block + 1) * wide]
            query = jnp.concatenate(
                [former * cos_one - latter * sin_one, latter * cos_one + former * sin_one], 1
            )
            upper = upper_all[:, place]
            query_t, upper_t = jnp.transpose(query), jnp.transpose(upper)
            joint = jnp.transpose(joint_all[:, place])
            for head in range(QUAD):
                low, high = head * HEAD, (head + 1) * HEAD
                cut = slice(head * LANES, (head + 1) * LANES)
                kept_lanes = (lane_head >= low) & (lane_head < high)
                kept_rows = (row_head >= low) & (row_head < high)
                upper_ref[chunk, block, cut, :] = jnp.where(kept_lanes, upper, 0.0).astype(BFLOAT)
                upper_t_ref[chunk, block, :, cut] = jnp.where(kept_rows, upper_t, 0.0).astype(
                    BFLOAT
                )
                inner_ref[chunk, block, :, cut] = jnp.sum(joint[low:high], 0, keepdims=True)
                row = block * QUAD + head
                fine_row = heads + fine_gap + row
                level_ref[chunk, block, :, cut] = (
                    level[row : row + 1] + level[fine_row : fine_row + 1]
                )
                kept_lanes = lax.shift_right_arithmetic(lane_head & (LANES - 1), HALF_BITS) == head
                kept_rows = lax.shift_right_arithmetic(row_head & (LANES - 1), HALF_BITS) == head
                query_ref[chunk, block, cut, :] = jnp.where(kept_lanes, query, 0.0).astype(BFLOAT)
                query_t_ref[chunk, block, :, cut] = jnp.where(kept_rows, query_t, 0.0).astype(
                    BFLOAT
                )
        return carry

    lax.fori_loop(0, chunks, unfold, 0)

    def body(step, carry):
        tile_step(step)
        return carry

    def tile_step(step):
        if kept:
            key_row = info_ref[step]
        else:
            slab_buf, slab_sem = loaded
            copy = pltpu.make_async_copy(info_ref.at[step], slab_buf, slab_sem)
            copy.start()
            copy.wait()
            key_row = slab_buf[...]
        id_row, code_row, pos_row = tile_tokens(key_row, token_bits)
        code_col = to_column(code_row)
        if kept:

            @pl.when(step + 1 < count)
            def _():
                for copy in loads(step + 1):
                    copy.start()

            for copy in loads(step):
                copy.wait()
            slot = lax.rem(step, 2)
            start = loaded[0][slot].astype(FLOAT)
            cosine, sine = loaded[1][slot, :, :LANES], loaded[1][slot, :, LANES:]
        else:
            id_col, pos_col = to_column(id_row), to_column(pos_row)
            start = tile_rows(id_col, first_ref[step], last_ref[step], start_in_ref, start_ref)
            cosine, sine = tile_rope(pos_col, rope_in_ref)
        factor = lax.rsqrt(jnp.mean(start * start, -1, keepdims=True) + EPS_NORM)
        normed = (start * factor * gain_ref[...]).astype(BFLOAT)
        raw = contract(normed, both_w_ref[:, :width], NN)
        values = contract(normed, both_w_ref[:, width:], NN).astype(BFLOAT)
        keys = []
        for block in range(blocks):
            former = raw[:, block * wide : block * wide + LANES]
            latter = raw[:, block * wide + LANES : (block + 1) * wide]
            keys.append(
                jnp.concatenate(
                    [former * cosine - latter * sine, latter * cosine + former * sine], 1
                ).astype(BFLOAT)
            )
        if chunks > 1:
            grad_keys_ref[...] = jnp.zeros_like(grad_keys_ref)
            grad_values_ref[...] = jnp.zeros_like(grad_values_ref)

        def attend(chunk):
            seen = (code_col == own_ref[chunk]) | (code_col == base_ref[chunk])
            hidden = jnp.where(seen, 0.0, FAR)
            hidden = jnp.concatenate([hidden] * QUAD, 1)
            for block in range(blocks):
                place = pl.ds(block * wide, wide)
                scores = contract(keys[block], query_t_ref[chunk, block], NN)
                weights = jnp.exp(scores - level_ref[chunk, block] + hidden)
                slopes = contract(
                    values[:, block * wide : (block + 1) * wide], upper_t_ref[chunk, block], NN
                )
                lowered = (weights * (slopes - inner_ref[chunk, block])).astype(BFLOAT)
                lowered_ref[...] = lowered
                grad_query_ref[chunk, block] += contract(keys[block], lowered_ref[:, mine], TN)
                grad_k = contract(lowered, query_ref[chunk, block], NN)
                grad_v = contract(weights.astype(BFLOAT), upper_ref[chunk, block], NN)
                if chunks > 1:
                    grad_keys_ref[:, place] += grad_k
                    grad_values_ref[:, place] += grad_v
                else:
                    grad_keys_ref[:, place] = grad_k
                    grad_values_ref[:, place] = grad_v

        if chunks > 1:
            lax.fori_loop(0, chunks, lambda chunk, c: (attend(chunk), c)[1], 0)
        else:
            attend(0)
        pieces = []
        for block in range(blocks):
            former = grad_keys_ref[:, pl.ds(block * wide, LANES)]
            latter = grad_keys_ref[:, pl.ds(block * wide + LANES, LANES)]
            pieces.append((former * cosine + latter * sine).astype(BFLOAT))
            pieces.append((latter * cosine - former * sine).astype(BFLOAT))
        grad_kv = jnp.concatenate(pieces + [grad_values_ref[...].astype(BFLOAT)], 1)
        grad_kv_ref[...] = grad_kv
        grad_w_ref[...] += contract(normed, grad_kv_ref[:, mine_kv], TN)
        grad_normed = contract(grad_kv, both_w_ref[...], NT)
        scaled = start * factor
        grad_gain_ref[...] += jnp.sum(grad_normed * scaled, 0, keepdims=True)
        weighted = grad_normed * gain_ref[...]
        inner = jnp.mean(weighted * scaled, -1, keepdims=True)
        grad_start = (factor * (weighted - scaled * inner)).astype(BFLOAT)
        rows = lax.broadcasted_iota(jnp.int32, (ROWS, tile), 0)

        def put(block, carry):
            base = pl.multiple_of(block * ROWS, ROWS)
            sum_ref[pl.ds(base, ROWS), :] += contract(one_hot(id_row == rows + base), grad_start, NN)
            return carry

        lax.fori_loop(
            lax.div(first_ref[step], ROWS), lax.div(last_ref[step], ROWS) + 1, put, 0
        )

    lax.fori_loop(0, count, body, 0)
    for half in range(2):
        place = pl.ds(pl.multiple_of(half * LANES + owner * HALF, HALF), HALF)
        grad_turned_ref[:, :, half] = grad_query_ref[:, :, place, :] * SCALE

    slots = stage_ref.shape[0]
    parts = limit // ROWS

    def out_copy(block):
        slot = lax.rem(block, slots)
        place = pl.ds(pl.multiple_of(block * ROWS, ROWS), ROWS)
        return pltpu.make_async_copy(
            stage_ref.at[slot], grad_embed_ref.at[place], copy_sem.at[slot]
        )

    def send(block, total):
        @pl.when(block >= slots)
        def _():
            out_copy(block - slots).wait()

        part = sum_ref[pl.ds(pl.multiple_of(block * ROWS, ROWS), ROWS), :]
        stage_ref[lax.rem(block, slots)] = part.astype(BFLOAT)
        out_copy(block).start()
        return total + jnp.sum((part * part).reshape(ROWS // 8, 8, -1), 0)

    square_ref[...] = lax.fori_loop(0, parts, send, jnp.zeros(square_ref.shape, FLOAT))

    def meet(spot, carry):
        met_ref[pl.ds(spot, 1), :] = sum_ref[pl.ds(scored_ref[spot], 1), :]
        return carry

    lax.fori_loop(0, met_ref.shape[0], meet, 0)
    for block in range(max(parts - slots, 0), parts):
        out_copy(block).wait()


def owner_kernel(
    owners,
    thin,
    misc_lane,
    rest_ref,
    leader_ref,
    got_ref,
    query_w_ref,
    start_ref,
    after_ref,
    cosine_ref,
    sine_ref,
    gain_ref,
    gain_part_ref,
    square_ref,
    rows_ref,
    told_ref,
    kv_ref,
):
    groups, _, quarter = got_ref.shape
    part = quarter // 2
    per_owner = part // HEAD
    cosine, sine = cosine_ref[...], sine_ref[...]
    square, turned, met = 0.0, {}, []
    for owner in range(owners):

        def add(shard, total):
            return total + got_ref[shard * owners + owner].astype(FLOAT)

        total = lax.fori_loop(
            0, groups // owners, add, jnp.zeros((thin + 2 * NCONT, quarter), FLOAT)
        )
        rows = total[:thin]
        kv_ref[:, owner * quarter : (owner + 1) * quarter] = rows
        square += jnp.sum(rows * rows)
        near = total[thin : thin + NCONT]
        near = near[:, :part] + near[:, part:]
        for slot in range(per_owner):
            former = near[:, slot * HEAD : slot * HEAD + HALF]
            latter = near[:, slot * HEAD + HALF : (slot + 1) * HEAD]
            turned[slot * owners + owner] = [
                former * cosine + latter * sine,
                latter * cosine - former * sine,
            ]
        far = total[thin + NCONT :]
        met.append(far[:, :part] + far[:, part:])
    met = jnp.concatenate(met, 1)
    grad_query = jnp.concatenate(sum([turned[head] for head in range(len(turned))], []), 1)
    grad_query = grad_query.astype(BFLOAT)
    upstream = contract(grad_query, query_w_ref[...], NT)
    start = start_ref[...]
    factor = lax.rsqrt(jnp.mean(start * start, -1, keepdims=True) + EPS_NORM)
    scaled = start * factor
    weighted = upstream * gain_ref[...]
    inner = jnp.mean(weighted * scaled, -1, keepdims=True)
    extra = after_ref[...] + factor * (weighted - scaled * inner)
    extra = extra.astype(BFLOAT).astype(FLOAT)
    gain = jnp.sum(upstream * scaled, 0, keepdims=True) + gain_part_ref[...] * (1.0 / owners)
    square += rest_ref[0] + 2.0 * jnp.sum(met * extra)
    square += leader_ref[0] * jnp.sum(square_ref[...])
    rows = rows_ref[...]
    line = lax.broadcasted_iota(jnp.int32, rows.shape, 0)
    lane = lax.broadcasted_iota(jnp.int32, rows.shape, 1)
    whole = jnp.full(rows.shape, square, FLOAT)
    high = whole.astype(BFLOAT).astype(FLOAT)
    rows = jnp.where(line == 0, gain, rows)
    rows = jnp.where((line == 6) & (lane == misc_lane), high, rows)
    rows = jnp.where((line == 6) & (lane == misc_lane + 1), whole - high, rows)
    payload = jnp.concatenate([extra, grad_query.astype(FLOAT), rows], 0).astype(BFLOAT)

    def put(group, carry):
        told_ref[group] = payload
        return carry

    lax.fori_loop(0, groups, put, 0)


def finish_kernel(rates, decays, columns, told_ref, id_col_ref, id_row_ref, gram_ref, *refs):
    normed_ref, slice_ref, *refs = refs
    sources, refs = refs[:12], refs[12:]
    extra_ref, query_ref, scalar_ref, *made_refs = refs
    count = extra_ref.shape[0]
    chunk = min(count, LANES)
    span = 16 * chunk // NCONT
    row = lax.broadcasted_iota(jnp.int32, (chunk, span), 0)
    col = lax.broadcasted_iota(jnp.int32, (chunk, span), 1)
    spot = 16 * lax.shift_right_arithmetic(row, 2)
    place = row & (NCONT - 1)
    line = lax.broadcasted_iota(jnp.int32, (8, span), 0)
    side = lax.broadcasted_iota(jnp.int32, (8, span), 1)
    which = lax.broadcasted_iota(jnp.int32, (chunk, columns), 0) & (NCONT - 1)
    sums, extra, query, logits = 0.0, [], [], []
    for begin in range(0, count, chunk):
        told = told_ref[begin // NCONT * 16 : begin // NCONT * 16 + span, :]
        extra.append(contract(one_hot(col == spot + place), told, NN).astype(BFLOAT))
        query.append(contract(one_hot(col == spot + place + NCONT), told, NN).astype(BFLOAT))
        misc = contract(one_hot(col == spot + 14), told[:, :LANES], NN)
        own = jnp.zeros((chunk, columns), FLOAT)
        for turn in range(NCONT):
            own = jnp.where(which == turn, misc[:, turn * columns : (turn + 1) * columns], own)
        logits.append(own.astype(BFLOAT))
        sums = sums + contract(one_hot((side & 15) == line + 8), told, NN)
    extra, query, logits = (jnp.concatenate(parts, 0) for parts in (extra, query, logits))
    extra_ref[...] = extra
    query_ref[...] = contract(slice_ref[...], query, TN)
    same = id_col_ref[...] == id_row_ref[...]
    square = jnp.sum(jnp.where(same, contract(extra, extra, NT), 0.0))
    square += jnp.sum(gram_ref[...] * contract(query, query, NT))
    grad_router = contract(logits, normed_ref[...], TN)
    gains, vectors, head = sums[0:3], sums[3:5], sums[5:6]
    misc = sums[6:7, NCONT * columns : NCONT * columns + 4]
    loss = jnp.sum(misc[:, 0:2])
    square += jnp.sum(misc[:, 2:4]) + jnp.sum(grad_router * grad_router)
    square += jnp.sum(sums[0:6] * sums[0:6])
    norm = jnp.sqrt(jnp.full((8, LANES), square, FLOAT))
    factor = THRESH / jnp.maximum(norm, THRESH)
    lane = lax.broadcasted_iota(jnp.int32, (8, LANES), 1)
    scalar_ref[...] = jnp.where(lane == 0, loss, jnp.where(lane == 1, norm, factor))
    factor = factor[0:1, 0:1]
    for index, grad in enumerate((grad_router, gains, vectors, head)):
        state = [sources[3 * index + part][...] for part in range(3)]
        made = adam_update(*state, grad * factor, rates[index], decays[index])
        for part in range(3):
            made_refs[3 * index + part][...] = made[part]


def expert_kernel(
    experts,
    owner_ref,
    told_ref,
    gates_ref,
    inner_ref,
    result_ref,
    down_ref,
    in_ref,
    sent_ref,
    grad_result_ref,
    grad_inner_ref,
    upstream_ref,
    back_ref,
):
    count, width = upstream_ref.shape
    local, units = down_ref.shape[0], down_ref.shape[1]

    def gather(pair, carry):
        rows = [told_ref[2 * pair + side].astype(FLOAT) for side in range(2)]
        place = pl.ds(pl.multiple_of(pair * 2 * NCONT, 2 * NCONT), 2 * NCONT)
        upstream_ref[place, :] = jnp.concatenate(rows, 0)
        return carry

    lax.fori_loop(0, count // (2 * NCONT), gather, 0)
    upstream = upstream_ref[...]
    owner = owner_ref[0]
    lane = lax.broadcasted_iota(jnp.int32, (count, LANES), 1)
    tail = jnp.zeros((count, LANES), FLOAT)
    back = 0.0
    for which in range(local):
        result = result_ref[which]
        dots = jnp.sum(upstream * result, -1, keepdims=True)
        high = dots.astype(BFLOAT).astype(FLOAT)
        spot = owner * local + which
        tail = jnp.where(lane == spot, high, tail)
        tail = jnp.where(lane == spot + experts, dots - high, tail)
        grad_result = (gates_ref[:, which : which + 1] * upstream).astype(BFLOAT)
        grad_result_ref[which] = grad_result
        grad_active = contract(grad_result, down_ref[which], NT)
        gate_half, up_half = inner_ref[which, :, :units], inner_ref[which, :, units:]
        sigma = lax.logistic(gate_half)
        grad_gate = grad_active * up_half * sigma * (1.0 + gate_half * (1.0 - sigma))
        grad_up = grad_active * gate_half * sigma
        grad_inner = jnp.concatenate([grad_gate, grad_up], 1).astype(BFLOAT)
        grad_inner_ref[which] = grad_inner
        back += contract(grad_inner, in_ref[which], NT)
    back_ref[...] = jnp.concatenate([back, tail], 1)

    def scatter(pair, carry):
        place = pl.ds(pl.multiple_of(pair * 2 * NCONT, 2 * NCONT), 2 * NCONT)
        rows = back_ref[place, :]
        for side in range(2):
            sent_ref[2 * pair + side] = rows[side * NCONT : (side + 1) * NCONT].astype(BFLOAT)
        return carry

    lax.fori_loop(0, count // (2 * NCONT), scatter, 0)


def pick_kernel(rows_ref, source_ref, picked_ref, copy_sem):
    count = picked_ref.shape[0]

    def fetch(spot, carry):
        pltpu.make_async_copy(
            source_ref.at[pl.ds(rows_ref[spot], 1)], picked_ref.at[pl.ds(spot, 1)], copy_sem
        ).start()
        return carry

    lax.fori_loop(0, count, fetch, 0)
    pltpu.make_async_copy(source_ref.at[pl.ds(0, count)], picked_ref, copy_sem).wait()


def adam_kernel(
    rate,
    decay,
    factor_ref,
    ids_ref,
    extra_ref,
    weight_ref,
    first_ref,
    second_ref,
    grad_ref,
    weight_out,
    first_out,
    second_out,
):
    rows = weight_out.shape[0]
    base = pl.program_id(0) * rows
    spots = lax.broadcasted_iota(jnp.int32, (rows, ids_ref.shape[1]), 0) + base
    extra = contract(one_hot(ids_ref[...] == spots), extra_ref[...], NN)
    grad = (grad_ref[...].astype(FLOAT) + extra) * factor_ref[0]
    weight, first, second = (
        ref[...].astype(FLOAT) for ref in (weight_ref, first_ref, second_ref)
    )
    made = adam_update(weight, first, second, grad, rate, decay)
    weight_out[...], first_out[...], second_out[...] = made


def matrix_adam_kernel(
    rate, decay, factor_ref, weight_ref, first_ref, second_ref, grad_ref, weight_out, first_out, second_out
):
    units = grad_ref.shape[3]
    for source in range(grad_ref.shape[0]):
        place = slice(source * units, (source + 1) * units)
        grad = grad_ref[source, 0].astype(FLOAT) * factor_ref[0]
        made = adam_update(
            weight_ref[0, :, place], first_ref[0, :, place], second_ref[0, :, place], grad, rate, decay
        )
        weight_out[0, :, place], first_out[0, :, place], second_out[0, :, place] = made


def split_float(values):
    high = lax.reduce_precision(values, 8, 7)
    return jnp.concatenate([high, values - high], -1).astype(BFLOAT)


def join_float(parts):
    half = parts.shape[-1] // 2
    parts = parts.astype(FLOAT)
    return parts[..., :half] + parts[..., half:]


def shards(
    token_ids,
    routes,
    last_valid,
    rank_pairs,
    embedding,
    embedding_first,
    embedding_second,
    attend_in,
    attend_in_first,
    attend_in_second,
    attend_out,
    attend_out_first,
    attend_out_second,
    expert_in,
    expert_in_first,
    expert_in_second,
    expert_out,
    expert_out_first,
    expert_out_second,
    router,
    router_first,
    router_second,
    norm_gains,
    norm_gains_first,
    norm_gains_second,
    const_vectors,
    const_vectors_first,
    const_vectors_second,
    score_head,
    score_head_first,
    score_head_second,
):
    shard_count = lax.axis_size("dp")
    owners = lax.axis_size("expert")
    groups = shard_count * owners
    my_shard = lax.axis_index("dp")
    my_owner = lax.axis_index("expert")
    width = embedding.shape[1]
    heads = width // HEAD
    blocks = heads // QUAD
    per_owner = heads // owners
    local_experts = expert_in.shape[0]
    experts = local_experts * owners
    routed = experts + 4
    hidden_units = expert_in.shape[2] // 2
    shard_rows = embedding.shape[0]
    slice_rows = attend_in.shape[0]
    queries = groups * NCONT
    everything = groups * TOK
    tile = TILE if everything <= KEEP else TILE_SMALL
    far_key = jnp.iinfo(jnp.int32).max
    gain_row = norm_gains[0:1]

    packed = jnp.concatenate(
        [token_ids[0], last_valid[0], jnp.zeros(LANES - NCONT, jnp.int32)]
    )
    known = spread(packed, BOTH)

    attend_b = attend_in.astype(BFLOAT)
    into = jnp.arange(3 * 2 * LANES, dtype=jnp.int32)
    which_part, spot = into // (2 * LANES), into % (2 * LANES)
    folded_head, folded_dim = spot % LANES // HALF, spot // LANES * HALF + spot % HALF
    is_value = which_part == 2
    head_slot = jnp.where(is_value, spot // HEAD, folded_head)
    dim = jnp.where(is_value, spot % HEAD, folded_dim)
    origin = which_part * width + (head_slot * owners + my_owner) * HEAD + dim
    origin = jnp.where(head_slot < per_owner, origin, -1)
    select = (jnp.arange(3 * width, dtype=jnp.int32)[:, None] == origin[None, :]).astype(BFLOAT)
    mine_in = jnp.dot(attend_b, select, preferred_element_type=FLOAT).astype(BFLOAT)
    weights_e = lax.all_gather(mine_in, "dp", tiled=True)
    piece = slice_rows // owners
    both_b = jnp.concatenate([attend_b, attend_out.astype(BFLOAT)], 1)
    both_b = lax.dynamic_slice_in_dim(both_b, my_owner * piece, piece, 0)

    units = hidden_units // shard_count
    cut_in = expert_in.astype(BFLOAT).reshape(
        local_experts, slice_rows, 2, shard_count, units
    )
    cut_in, known = lax.optimization_barrier((cut_in.transpose(3, 0, 1, 2, 4), known))
    ids, last = known[:, :TOK], known[:, TOK : TOK + NCONT]
    got_in = swap(cut_in, "dp")

    places = jnp.arange(TOK, dtype=jnp.int32)
    offsets = jnp.arange(CLEN, dtype=jnp.int32)
    seen_late = (offsets[None, None, :] <= last[:, :, None]).reshape(groups, NCONT * CLEN)
    seen = jnp.concatenate([jnp.ones((groups, PROMPT), bool), seen_late], 1)
    local = ids - my_shard * shard_rows
    here = seen & (local >= 0) & (local < shard_rows)
    index = jnp.arange(everything, dtype=jnp.int32).reshape(groups, TOK)
    key = jnp.where(here, local * everything + index, far_key)
    ordered = lax.sort(key.reshape(-1))
    tile_count = (jnp.sum(here.astype(jnp.int32)) + tile - 1) // tile
    ordered = jnp.where(ordered == far_key, -1, ordered)
    info = ordered.reshape(everything // tile, 1, tile)
    token_bits = everything.bit_length() - 1
    rows_of = jnp.maximum(lax.shift_right_arithmetic(ordered, token_bits), 0)
    rows_of = rows_of.reshape(everything // tile, tile)
    first_row = rows_of[:, 0]
    last_row = jnp.max(rows_of, 1)
    tile_count = tile_count.reshape(1)

    at_last = (offsets[None, None, :] == last[:, :, None]).astype(jnp.int32)
    scored_ids = jnp.sum(ids[:, PROMPT:].reshape(groups, NCONT, CLEN) * at_last, 2)
    scored_local = scored_ids.reshape(-1) - my_shard * shard_rows
    scored_here = (scored_local >= 0) & (scored_local < shard_rows)
    scored_row = jnp.clip(scored_local, 0, shard_rows - 1)
    scored_row = scored_row.astype(jnp.int32)
    scored_start = pl.pallas_call(
        pick_kernel,
        out_shape=jax.ShapeDtypeStruct((queries, width), FLOAT),
        in_specs=[SMEM_SPEC, pl.BlockSpec(memory_space=pl.ANY)],
        out_specs=VMEM_SPEC,
        scratch_shapes=[pltpu.SemaphoreType.DMA],
    )(scored_row, embedding)
    scored_start = jnp.where(scored_here[:, None], scored_start, 0.0)
    scored_start = lax.reduce_precision(scored_start, 8, 7)
    scored_normed = rms_forward(scored_start, norm_gains[0])[0].astype(BFLOAT)
    weights_e, both_b, info, scored_normed = lax.optimization_barrier(
        (weights_e, both_b, info, scored_normed)
    )
    query_w_e = weights_e[:, : 2 * LANES]
    both_w = lax.all_gather(both_b, BOTH, tiled=True)
    query_w, out_w = both_w[:, :width], both_w[:, 3 * width :]
    cos_table, sin_table = rope_constants()
    late_cos, late_sin = jnp.asarray(cos_table[PROMPT:]), jnp.asarray(sin_table[PROMPT:])
    at_late = (offsets[None, :] == last.reshape(-1)[:, None]).astype(FLOAT)
    scored_cos = jnp.dot(at_late, late_cos, precision=HIGH)
    scored_sin = jnp.dot(at_late, late_sin, precision=HIGH)
    cos_wide, sin_wide = jnp.tile(scored_cos, (1, QUAD)), jnp.tile(scored_sin, (1, QUAD))
    raw = jnp.dot(scored_normed, query_w_e, preferred_element_type=FLOAT)
    former, latter = raw[:, :LANES], raw[:, LANES:]
    query_part = jnp.concatenate(
        [former * cos_wide - latter * sin_wide, latter * cos_wide + former * sin_wide], 1
    ).astype(BFLOAT)
    kept = everything <= KEEP
    embed_b = embedding if kept else embedding.astype(BFLOAT)
    query_e = jnp.sum(spread(query_part, "dp").astype(FLOAT), 0)

    lane_head = (jnp.arange(2 * LANES) % LANES) // HALF
    head_lanes = (lane_head[None, :] == jnp.arange(per_owner)[:, None]).astype(FLOAT)
    query_rows = (query_e[None] * SCALE * head_lanes[:, None, :]).astype(BFLOAT)
    query_rows = query_rows.reshape(per_owner * queries, 2 * LANES)
    base_code = (jnp.arange(queries, dtype=jnp.int32) // NCONT) * 8
    own_code = base_code + jnp.arange(queries, dtype=jnp.int32) % NCONT + 1
    table = jnp.asarray(rope_split())
    any_spec = pl.BlockSpec(memory_space=pl.ANY)
    part = per_owner * HEAD
    start_cut = lax.dynamic_slice_in_dim(scored_start, my_owner * part, part, 1)
    sent_lanes = 2 * part + LANES
    query_count = per_owner * queries
    kept_shapes = (
        jax.ShapeDtypeStruct((everything, width), BFLOAT),
        jax.ShapeDtypeStruct((everything, 2 * LANES), FLOAT),
    )
    sent, *saved = pl.pallas_call(
        functools.partial(forward_kernel, token_bits),
        in_specs=[SMEM_SPEC] * 3
        + [VMEM_SPEC, any_spec if kept else VMEM_SPEC]
        + [VMEM_SPEC] * 7,
        out_specs=(VMEM_SPEC,) + (any_spec,) * (2 * kept),
        scratch_shapes=[
            pltpu.VMEM((2, tile, width), BFLOAT),
            pltpu.VMEM((2, tile, 2 * LANES), FLOAT),
            pltpu.SemaphoreType.DMA((2, 2)),
            pltpu.VMEM((4, min(2 * ROWS, shard_rows), width), FLOAT),
            pltpu.VMEM((shard_rows, width), BFLOAT),
            pltpu.SemaphoreType.DMA((4,)),
        ]
        * kept
        + [
            pltpu.VMEM((query_count, 2 * LANES), FLOAT),
            pltpu.VMEM((query_count, LANES), FLOAT),
            pltpu.VMEM((query_count, LANES), FLOAT),
            pltpu.VMEM((tile, width), FLOAT),
        ],
        out_shape=(jax.ShapeDtypeStruct((queries, sent_lanes), BFLOAT),) + kept_shapes * kept,
        compiler_params=pltpu.CompilerParams(vmem_limit_bytes=FORWARD_LIMIT),
        cost_estimate=pl.CostEstimate(
            flops=30_000_000_000, bytes_accessed=20_000_000, transcendentals=2_000_000
        ),
    )(
        tile_count,
        first_row,
        last_row,
        info,
        embed_b,
        gain_row,
        weights_e,
        table,
        query_rows,
        jnp.tile(own_code, per_owner)[:, None],
        jnp.tile(base_code, per_owner)[:, None],
        start_cut,
    )
    sent, got_in = lax.optimization_barrier((sent, got_in))
    in_w = got_in.transpose(1, 0, 2, 3, 4).reshape(local_experts, width, 2 * units)
    got = swap(sent.reshape(groups, NCONT, -1), BOTH)
    got = got.reshape(shard_count, owners, NCONT, -1)
    got = got.astype(FLOAT)
    got_out = got[..., :part].reshape(shard_count, owners, NCONT, per_owner, HEAD)
    got_start = got[..., part : 2 * part]
    got_fine = join_float(got[..., 2 * part : 2 * part + 4 * per_owner])
    got_peak, got_total = got_fine[..., :per_owner], got_fine[..., per_owner:]
    peak = jnp.max(got_peak, 0)
    share = jnp.exp(got_peak - peak[None])
    total = jnp.sum(share * got_total, 0)
    mixed = jnp.sum(share[..., None] * got_out, 0) / total[..., None]
    mixed = mixed.transpose(1, 2, 0, 3).reshape(NCONT, width)
    level = (peak + jnp.log(total)).transpose(1, 2, 0).reshape(NCONT, heads)
    start_x = jnp.sum(got_start, 0).transpose(1, 0, 2).reshape(NCONT, width)

    router_b = router.astype(BFLOAT)
    after_attn = start_x + jnp.dot(mixed.astype(BFLOAT), out_w, preferred_element_type=FLOAT)
    normed_two, factor_two = rms_forward(after_attn, norm_gains[1])
    normed_two_b = normed_two.astype(BFLOAT)
    logits = jnp.dot(normed_two_b, router_b, preferred_element_type=FLOAT)
    gate_probs = jax.nn.softmax(logits[:, :routed], -1)
    alphas = [
        jax.nn.softmax(logits[:, routed + 2 * which : routed + 2 * which + 2], -1)
        for which in range(2)
    ]
    own_last = last_valid[0]
    own_pick = (offsets[None, :] == own_last[:, None]).astype(jnp.int32)
    route_row = jnp.sum(
        routes[0, PROMPT:].reshape(NCONT, CLEN, 2) * own_pick[..., None], 1
    )
    pick_table = (route_row[:, :, None] == jnp.arange(routed)[None, None, :]).astype(FLOAT)
    gate_pick = jnp.sum(pick_table * gate_probs[:, None, :], -1)
    gate_full = jnp.sum(pick_table * gate_pick[..., None], 1)[:, :experts]
    fine = split_float(jnp.concatenate([level, gate_full], 1))
    tail = jnp.zeros((NCONT, LANES - 2 * (heads + experts)), BFLOAT)
    told = jnp.concatenate(
        [normed_two_b, start_x.astype(BFLOAT), mixed.astype(BFLOAT), fine, tail], 1
    )
    told = all_told = spread(told, BOTH).reshape(queries, -1)
    all_normed_b = told[:, :width]
    all_start = told[:, width : 2 * width].astype(FLOAT)
    all_mixed_b = told[:, 2 * width : 3 * width]
    all_fine = join_float(told[:, 3 * width : 3 * width + 2 * (heads + experts)])
    all_level, all_gates = all_fine[:, :heads], all_fine[:, heads:]
    own_gates = lax.dynamic_slice_in_dim(all_gates, my_owner * local_experts, local_experts, 1)

    down_w = expert_out.astype(BFLOAT)
    inner_all, active_all, result_all = [], [], []
    for which in range(local_experts):
        inner = jnp.dot(all_normed_b, in_w[which], preferred_element_type=FLOAT)
        active = (jax.nn.silu(inner[:, :units]) * inner[:, units:]).astype(BFLOAT)
        inner_all.append(inner)
        active_all.append(active)
        result_all.append(jnp.dot(active, down_w[which], preferred_element_type=FLOAT))
    combined = sum(own_gates[:, w : w + 1] * result_all[w] for w in range(local_experts))
    combined = combined.astype(BFLOAT).reshape(groups, NCONT, width)
    fetched = jnp.sum(swap(combined, BOTH).astype(FLOAT), 0)

    is_copy = (route_row == experts + 1).astype(FLOAT)[..., None]
    chosen = [(route_row == experts + 2 + which).astype(FLOAT)[..., None] for which in range(2)]
    branch = is_copy * normed_two[:, None, :]
    for which in range(2):
        constant = (
            alphas[which][:, None, 0:1] * normed_two[:, None, :]
            + alphas[which][:, None, 1:2] * const_vectors[which]
        )
        branch = branch + chosen[which] * constant
    after_ffn = after_attn + fetched + jnp.sum(gate_pick[..., None] * branch, 1)
    final, factor_three = rms_forward(after_ffn, norm_gains[2])
    picked = jnp.sum(final * score_head[None, :], -1)
    pair_rows = rank_pairs[0]
    lead = (pair_rows[:, 0:1] == jnp.arange(NCONT)[None, :]).astype(FLOAT)
    other = (pair_rows[:, 1:2] == jnp.arange(NCONT)[None, :]).astype(FLOAT)
    sides = lead - other
    margin = jnp.sum(sides * picked[None, :], 1)
    loss_part = jnp.sum(jax.nn.softplus(-margin))
    grad_margin = -jax.nn.sigmoid(-margin) * (1.0 / (groups * NPAIR))
    grad_picked = jnp.sum(sides * grad_margin[:, None], 0)
    grad_head = jnp.sum(grad_picked[:, None] * final, 0)
    grad_ffn, grad_gain_final = rms_backward(
        after_ffn, factor_three, norm_gains[2], grad_picked[:, None] * score_head[None, :]
    )
    all_ffn = spread(grad_ffn.astype(BFLOAT), BOTH)

    returned, grad_result, grad_inner = pl.pallas_call(
        functools.partial(expert_kernel, experts),
        out_shape=(
            jax.ShapeDtypeStruct((groups, NCONT, width + LANES), BFLOAT),
            jax.ShapeDtypeStruct((local_experts, queries, width), BFLOAT),
            jax.ShapeDtypeStruct((local_experts, queries, 2 * units), BFLOAT),
        ),
        in_specs=[SMEM_SPEC] + [VMEM_SPEC] * 6,
        out_specs=(VMEM_SPEC,) * 3,
        scratch_shapes=[
            pltpu.VMEM((queries, width), FLOAT),
            pltpu.VMEM((queries, width + LANES), FLOAT),
        ],
        compiler_params=pltpu.CompilerParams(vmem_limit_bytes=VMEM_LIMIT),
    )(
        my_owner.astype(jnp.int32).reshape(1),
        all_ffn,
        own_gates,
        jnp.stack(inner_all),
        jnp.stack(result_all),
        down_w,
        in_w,
    )
    returned = jnp.sum(swap(returned, BOTH).astype(FLOAT), 0)
    returned_grad = returned[:, :width]
    returned_dots = join_float(returned[:, width : width + 2 * experts])
    grad_in = jnp.stack(
        [contract(all_normed_b, grad_inner[w], TN) for w in range(local_experts)]
    )
    grad_expert_out = jnp.stack(
        [contract(active_all[w], grad_result[w], TN) for w in range(local_experts)]
    )

    grad_pick = jnp.sum(grad_ffn[:, None, :] * branch, -1) + jnp.sum(
        pick_table[:, :, :experts] * returned_dots[:, None, :], -1
    )
    grad_branch = gate_pick[..., None] * grad_ffn[:, None, :]
    grad_normed_two = returned_grad + jnp.sum(grad_branch * is_copy, 1)
    grad_vectors = []
    grad_alpha_parts = []
    for which in range(2):
        masked = jnp.sum(chosen[which] * grad_branch, 1)
        grad_vectors.append(jnp.sum(masked * alphas[which][:, 1:2], 0))
        grad_alpha = jnp.stack(
            [jnp.sum(masked * normed_two, -1), jnp.sum(masked * const_vectors[which], -1)], -1
        )
        grad_alpha_parts.append(
            alphas[which] * (grad_alpha - jnp.sum(alphas[which] * grad_alpha, -1, keepdims=True))
        )
        grad_normed_two = grad_normed_two + masked * alphas[which][:, 0:1]
    grad_probs = jnp.sum(pick_table * grad_pick[..., None], 1)
    grad_main = gate_probs * (grad_probs - jnp.sum(gate_probs * grad_probs, -1, keepdims=True))
    grad_logits = jnp.concatenate([grad_main] + grad_alpha_parts, -1)
    grad_normed_two = grad_normed_two + jnp.einsum(
        "tc,dc->td", grad_logits, router_b.astype(FLOAT), precision=HIGH
    )
    grad_attn_part, grad_gain_ffn = rms_backward(
        after_attn, factor_two, norm_gains[1], grad_normed_two
    )
    grad_after_attn = grad_ffn + grad_attn_part
    columns = grad_logits.shape[1]
    misc = jnp.concatenate(
        [
            grad_logits.reshape(-1),
            split_float(loss_part[None]).astype(FLOAT),
        ]
    )
    grad_attn_b = spread(grad_after_attn.astype(BFLOAT), BOTH).reshape(queries, width)

    cut_grad = grad_in.reshape(local_experts, shard_count, slice_rows, 2 * units)
    cut_grad = cut_grad.transpose(1, 0, 2, 3).astype(BFLOAT)
    cut_grad, grad_attn_b = lax.optimization_barrier((cut_grad, grad_attn_b))
    sum_expert_in = swap(cut_grad, "dp")

    order = np.arange(width).reshape(blocks, QUAD, 2, HALF).swapaxes(1, 2).reshape(-1)
    fold = jnp.asarray((np.arange(width)[:, None] == order[None, :]).astype(ml_dtypes.bfloat16))
    all_normed_one = rms_forward(all_start, norm_gains[0])[0].astype(BFLOAT)
    chunk = min(queries, LANES)
    chunks = queries // chunk

    sum_attend_out = contract(
        lax.dynamic_slice_in_dim(all_mixed_b, my_shard * slice_rows, slice_rows, 1),
        grad_attn_b,
        TN,
    )
    side = QUAD * chunk
    quarter = 2 * width // owners
    grad_embed, grad_kv, grad_query, grad_gain, met, embed_square = pl.pallas_call(
        functools.partial(backward_kernel, kept, chunks, blocks, token_bits, experts),
        in_specs=[SMEM_SPEC] * 5
        + ([VMEM_SPEC] + [any_spec] * 2 if kept else [any_spec] + [VMEM_SPEC] * 2)
        + [VMEM_SPEC] * 9,
        out_specs=(any_spec,) + (VMEM_SPEC,) * 5,
        scratch_shapes=[
            pltpu.VMEM((shard_rows, width), FLOAT),
            pltpu.VMEM((4, ROWS, width), BFLOAT),
            pltpu.VMEM((width, 2 * width), BFLOAT),
            pltpu.VMEM((chunks, blocks, side, 2 * LANES), BFLOAT),
            pltpu.VMEM((chunks, blocks, 2 * LANES, side), BFLOAT),
            pltpu.VMEM((chunks, blocks, side, 2 * LANES), BFLOAT),
            pltpu.VMEM((chunks, blocks, 2 * LANES, side), BFLOAT),
            pltpu.VMEM((chunks, blocks, 1, side), FLOAT),
            pltpu.VMEM((chunks, blocks, 1, side), FLOAT),
            pltpu.VMEM((tile, side), BFLOAT),
            pltpu.VMEM((chunks, blocks, 2 * LANES, chunk), FLOAT),
            pltpu.VMEM((tile, 2 * width), BFLOAT),
            pltpu.VMEM((8 if kept else tile, width), FLOAT),
            pltpu.VMEM((tile, width), FLOAT),
            pltpu.VMEM((tile, width), FLOAT),
            pltpu.SemaphoreType.DMA((4,)),
        ]
        + (
            [
                pltpu.VMEM((2, tile, width), BFLOAT),
                pltpu.VMEM((2, tile, 2 * LANES), FLOAT),
                pltpu.SemaphoreType.DMA((2, 2)),
            ]
            if kept
            else [pltpu.VMEM((1, tile), jnp.int32), pltpu.SemaphoreType.DMA]
        ),
        out_shape=(
            jax.ShapeDtypeStruct((shard_rows, width), BFLOAT),
            jax.ShapeDtypeStruct((width, quarter), FLOAT),
            jax.ShapeDtypeStruct((chunks, blocks, 2, HALF, chunk), FLOAT),
            jax.ShapeDtypeStruct((1, width), FLOAT),
            jax.ShapeDtypeStruct((queries, width), FLOAT),
            jax.ShapeDtypeStruct((8, width), FLOAT),
        ),
        compiler_params=pltpu.CompilerParams(vmem_limit_bytes=VMEM_LIMIT),
        cost_estimate=pl.CostEstimate(
            flops=60_000_000_000, bytes_accessed=60_000_000, transcendentals=6_000_000
        ),
    )(
        tile_count,
        my_owner.astype(jnp.int32).reshape(1),
        first_row,
        last_row,
        scored_row,
        info,
        saved[0] if kept else embed_b,
        saved[1] if kept else table,
        gain_row,
        both_w,
        fold,
        all_told.reshape(chunks, chunk, -1),
        grad_attn_b.reshape(chunks, chunk, width),
        cos_wide.reshape(chunks, chunk, LANES),
        sin_wide.reshape(chunks, chunk, LANES),
        own_code.reshape(chunks, 1, chunk),
        base_code.reshape(chunks, 1, chunk),
    )

    pieces = grad_query.transpose(0, 4, 1, 2, 3).reshape(groups, NCONT, part)
    met = jnp.where(scored_here[:, None], met, 0.0)
    met = lax.dynamic_slice_in_dim(met, my_owner * part, part, 1).reshape(groups, NCONT, part)
    thin = width // groups
    sent = jnp.concatenate(
        [
            grad_kv.astype(BFLOAT).reshape(groups, thin, quarter),
            split_float(pieces),
            split_float(met),
        ],
        1,
    )
    sent, sum_expert_in = lax.optimization_barrier((sent, sum_expert_in))
    got = swap(sent, BOTH)
    own_late = (offsets[None, :] == own_last[:, None]).astype(FLOAT)
    own_cos = jnp.dot(own_late, late_cos, precision=HIGH)
    own_sin = jnp.dot(own_late, late_sin, precision=HIGH)
    leader = (my_owner == 0).astype(FLOAT)
    rest_square = (
        jnp.sum(grad_in * grad_in)
        + jnp.sum(grad_expert_out * grad_expert_out)
        + leader * jnp.sum(sum_attend_out * sum_attend_out)
    )
    misc_lane = misc.shape[0]
    misc = jnp.pad(misc, (0, width - misc_lane))
    blank = jnp.zeros((width,), FLOAT)
    rows = [blank, grad_gain_ffn, grad_gain_final] + grad_vectors + [grad_head, misc, blank]
    told, sum_kv = pl.pallas_call(
        functools.partial(owner_kernel, owners, thin, misc_lane),
        out_shape=(
            jax.ShapeDtypeStruct((groups, 16, width), BFLOAT),
            jax.ShapeDtypeStruct((thin, 2 * width), FLOAT),
        ),
        in_specs=[SMEM_SPEC] * 2 + [VMEM_SPEC] * 10,
        out_specs=(VMEM_SPEC,) * 2,
        compiler_params=pltpu.CompilerParams(vmem_limit_bytes=VMEM_LIMIT),
    )(
        rest_square.reshape(1),
        leader.reshape(1),
        got,
        query_w,
        start_x,
        grad_after_attn,
        own_cos,
        own_sin,
        gain_row,
        grad_gain,
        embed_square,
        jnp.stack(rows),
    )
    told = spread_made(told, BOTH).reshape(16 * groups, width)
    told, sum_kv = lax.optimization_barrier((told, sum_kv))
    all_kv = spread(sum_kv.astype(BFLOAT), "expert").reshape(slice_rows, 2 * width)
    rates = learn_rates()
    normed_slice = lax.dynamic_slice_in_dim(
        all_normed_one, my_shard * slice_rows, slice_rows, 1
    )
    small_states = (
        router.T,
        router_first.T,
        router_second.T,
        norm_gains,
        norm_gains_first,
        norm_gains_second,
        const_vectors,
        const_vectors_first,
        const_vectors_second,
        score_head[None],
        score_head_first[None],
        score_head_second[None],
    )
    all_extra_b, sum_query_w, scalars, *made_small = pl.pallas_call(
        functools.partial(finish_kernel, rates[5:], DECAYS[5:], columns),
        out_shape=(
            jax.ShapeDtypeStruct((queries, width), BFLOAT),
            jax.ShapeDtypeStruct((slice_rows, width), FLOAT),
            jax.ShapeDtypeStruct((8, LANES), FLOAT),
        )
        + tuple(jax.ShapeDtypeStruct(array.shape, FLOAT) for array in small_states),
        in_specs=[VMEM_SPEC] * 18,
        out_specs=(VMEM_SPEC,) * 15,
        compiler_params=pltpu.CompilerParams(vmem_limit_bytes=VMEM_LIMIT),
    )(
        told,
        scored_ids.reshape(-1, 1),
        scored_ids.reshape(1, -1),
        contract(all_normed_one, all_normed_one, NT),
        all_normed_b,
        normed_slice,
        *small_states,
    )
    loss_total, norm_total, factor = scalars[0, 0], scalars[0, 1], scalars[0, 2]
    key_grad = contract(all_kv[:, :width], fold, NT)
    sum_attend_in = jnp.concatenate(
        [sum_query_w, key_grad, all_kv[:, width:].astype(FLOAT)], 1
    )

    block_rows = min(4 * ROWS, shard_rows)
    row_spec = pl.BlockSpec((block_rows, width), lambda i: (i, 0))
    whole_spec = pl.BlockSpec((queries, width), lambda i: (0, 0))
    made_embedding = pl.pallas_call(
        functools.partial(adam_kernel, rates[0], DECAYS[0]),
        grid=(shard_rows // block_rows,),
        out_shape=(jax.ShapeDtypeStruct((shard_rows, width), FLOAT),) * 3,
        in_specs=[
            SMEM_SPEC,
            pl.BlockSpec((1, queries), lambda i: (0, 0)),
            whole_spec,
        ]
        + [row_spec] * 4,
        out_specs=(row_spec,) * 3,
        compiler_params=pltpu.CompilerParams(vmem_limit_bytes=VMEM_LIMIT),
        cost_estimate=pl.CostEstimate(
            flops=4_000_000_000, bytes_accessed=176_000_000, transcendentals=12_000_000
        ),
    )(
        factor.reshape(1),
        jnp.where(scored_here, scored_local, -1)[None],
        all_extra_b,
        embedding,
        embedding_first,
        embedding_second,
        grad_embed,
    )
    cut_rows = 32
    cells = pl.BlockSpec((1, cut_rows, hidden_units), lambda l, h, r: (l, r, h))
    cut_spec = pl.BlockSpec((shard_count, 1, cut_rows, units), lambda l, h, r: (0, l, r, h))
    if units % LANES == 0 and slice_rows % cut_rows == 0:
        made_in = pl.pallas_call(
            functools.partial(matrix_adam_kernel, rates[3], DECAYS[3]),
            grid=(local_experts, 2, slice_rows // cut_rows),
            out_shape=(jax.ShapeDtypeStruct(expert_in.shape, FLOAT),) * 3,
            in_specs=[SMEM_SPEC] + [cells] * 3 + [cut_spec],
            out_specs=(cells,) * 3,
            compiler_params=pltpu.CompilerParams(vmem_limit_bytes=SMALL_LIMIT),
            cost_estimate=pl.CostEstimate(
                flops=100_000_000, bytes_accessed=20_000_000, transcendentals=1_600_000
            ),
        )(factor.reshape(1), expert_in, expert_in_first, expert_in_second, sum_expert_in)
    else:
        whole_in = sum_expert_in.astype(FLOAT).reshape(
            shard_count, local_experts, slice_rows, 2, units
        )
        whole_in = whole_in.transpose(1, 2, 3, 0, 4).reshape(expert_in.shape)
        made_in = adam_update(
            expert_in, expert_in_first, expert_in_second, whole_in * factor, rates[3], DECAYS[3]
        )
    made = list(made_embedding)
    states = (
        (attend_in, attend_in_first, attend_in_second, sum_attend_in),
        (attend_out, attend_out_first, attend_out_second, sum_attend_out),
        None,
        (expert_out, expert_out_first, expert_out_second, grad_expert_out),
    )
    for which, state in enumerate(states):
        if state is None:
            made += made_in
            continue
        *state, grad = state
        made += adam_update(*state, grad * factor, rates[which + 1], DECAYS[which + 1])
    made += [array.T for array in made_small[:3]] + made_small[3:9]
    made += [array.reshape(-1) for array in made_small[9:]]
    return tuple(made) + (loss_total, norm_total)


def solution(mesh):
    pair = P(BOTH, None)
    triple = P(BOTH, None, None)
    rows = P("dp", None)
    cells = P("expert", "dp", None)
    placed = (pair, triple, pair, triple) + (rows,) * 9 + (cells,) * 6 + (P(),) * 12
    return jax.shard_map(
        shards,
        mesh=mesh,
        in_specs=placed,
        out_specs=(rows,) * 9 + (cells,) * 6 + (P(),) * 14,
        check_vma=False,
    )
```

```python
import functools

import jax
import jax.numpy as jnp
import ml_dtypes
import numpy as np
from jax import lax
from jax.experimental import pallas as pl
from jax.experimental.pallas import tpu as pltpu
from jax.sharding import PartitionSpec as P

D = 768
HEAD = 64
FF = 2048
PROMPT = 512
CLEN = 128
NCONT = 4
NPAIR = 4
ADAM_STEP = 5
TOK = PROMPT + NCONT * CLEN
SPAN = PROMPT + CLEN
HALF = HEAD // 2
QUAD = 4
TILE = 512
TILE_SMALL = 256
ROWS = 256
WINDOW = 1536
KEEP = 65536
TOK_BITS = TOK.bit_length() - 1
CLEN_BITS = CLEN.bit_length() - 1
HALF_BITS = HALF.bit_length() - 1
LANES = 128

HIGH = lax.Precision.HIGHEST
EPS_NORM = 1e-05
THRESH = 0.05
BETA_ONE = 0.5
BETA_TWO = 0.5
ADAM_EPS = 1e-08
ROPE_BASE = 10000.0
DECAYS = (0.1, 0.1, 0.1, 0.1, 0.1, 0.1, 0.0, 0.0, 0.0)
BFLOAT = jnp.bfloat16
FLOAT = jnp.float32
BOTH = ("dp", "expert")
SCALE = HEAD ** (-0.5)
FAR = -1e30
VMEM_LIMIT = 127 * 512 * 1024
SMALL_LIMIT = 16 * 1024 * 1024
FORWARD_LIMIT = 40 * 1024 * 1024


VMEM_SPEC = pl.BlockSpec(memory_space=pltpu.VMEM)
SMEM_SPEC = pl.BlockSpec(memory_space=pltpu.SMEM)


def learn_rates():
    return (
        1.0,
        D ** (-0.5),
        (D * 16 // PROMPT) ** (-0.5),
        D ** (-0.5),
        (FF // 64) ** (-0.5),
        (2 * D) ** (-0.5),
        0.5,
        1.0,
        D ** (-0.5),
    )


def rms_forward(values, gain):
    factor = lax.rsqrt(jnp.mean(values * values, -1, keepdims=True) + EPS_NORM)
    return (values * factor * gain, factor)


def rms_backward(values, factor, gain, upstream):
    weighted = upstream * gain
    inner = jnp.mean(weighted * values, -1, keepdims=True)
    return (
        factor * weighted - values * factor * factor * factor * inner,
        jnp.sum(upstream * values * factor, 0),
    )


def adam_update(weight, first, second, grad, rate, decay):
    first = BETA_ONE * first + (1.0 - BETA_ONE) * grad
    second = BETA_TWO * second + (1.0 - BETA_TWO) * grad * grad
    step_dir = (
        first
        / (1.0 - BETA_ONE**ADAM_STEP)
        / (jnp.sqrt(second / (1.0 - BETA_TWO**ADAM_STEP)) + ADAM_EPS)
    )
    return (weight - rate * (step_dir + decay * weight), first, second)


def rope_constants():
    freq = np.float32(ROPE_BASE) ** (-np.arange(HALF, dtype=np.float32) / np.float32(HALF))
    angle = np.arange(SPAN, dtype=np.float32)[:, None] * freq.astype(np.float32)[None, :]
    angle = angle.astype(np.float64)
    return np.cos(angle).astype(np.float32), np.sin(angle).astype(np.float32)


def rope_split():
    parts = []
    for table in rope_constants():
        high = table.astype(ml_dtypes.bfloat16)
        low = (table - high.astype(np.float32)).astype(ml_dtypes.bfloat16)
        parts += [np.tile(high, (1, QUAD)), np.tile(low, (1, QUAD))]
    return np.concatenate(parts, 1)


def spread(array, axes):
    count = lax.axis_size(axes)
    return lax.all_to_all(
        jnp.broadcast_to(array[None], (count,) + array.shape), axes, 0, 0, tiled=True
    )


def spread_made(copies, axes):
    return lax.all_to_all(copies, axes, 0, 0, tiled=True)


def swap(array, axes):
    return lax.all_to_all(array, axes, 0, 0, tiled=True)


def contract(left, right, dims):
    return lax.dot_general(left, right, (dims, ((), ())), preferred_element_type=FLOAT)


NN = ((1,), (0,))
NT = ((1,), (1,))
TN = ((0,), (0,))


def tile_tokens(key_row, token_bits):
    real = key_row >= 0
    local = lax.shift_right_arithmetic(key_row, token_bits)
    place = key_row & (TOK - 1)
    group = lax.shift_right_arithmetic(key_row & ((1 << token_bits) - 1), TOK_BITS)
    late = place - PROMPT
    seg = lax.shift_right_arithmetic(late, CLEN_BITS) + 1
    code = group * 8 + jnp.where(late < 0, 0, seg)
    spot = jnp.where(late < 0, place, PROMPT + (late & (CLEN - 1)))
    return jnp.where(real, local, -1), jnp.where(real, code, -1), spot


def to_column(row):
    return jnp.transpose(jnp.broadcast_to(row.astype(FLOAT), (8, row.shape[1])))[:, 0:1].astype(jnp.int32)


def one_hot(matches):
    return matches.astype(FLOAT).astype(BFLOAT)


def tile_rows(id_col, low, high, embed_ref, start_ref):
    limit = embed_ref.shape[0]
    window = min(WINDOW, limit)
    align = 16
    origin = lax.div(low, align) * align
    lanes = lax.broadcasted_iota(jnp.int32, (id_col.shape[0], window), 1)

    def pick(turn):
        least = origin + turn * window
        base = pl.multiple_of(jnp.minimum(least, limit - window), align)
        wanted = jnp.where(id_col >= least, id_col - base, -1)
        return contract(one_hot(wanted == lanes), embed_ref[pl.ds(base, window), :], NN)

    start_ref[...] = pick(0)

    def more(turn, carry):
        start_ref[...] += pick(turn)
        return carry

    lax.fori_loop(1, lax.div(high - origin, window) + 1, more, 0)
    return start_ref[...]


def tile_rope(pos_col, table_ref):
    spots = lax.broadcasted_iota(jnp.int32, (pos_col.shape[0], SPAN), 1)
    both = contract(one_hot(pos_col == spots), table_ref[...], NN)
    cosine = both[:, :LANES] + both[:, LANES : 2 * LANES]
    sine = both[:, 2 * LANES : 3 * LANES] + both[:, 3 * LANES :]
    return cosine, sine


def forward_kernel(
    token_bits,
    count_ref,
    first_ref,
    last_ref,
    info_ref,
    embed_ref,
    gain_ref,
    weights_ref,
    table_ref,
    query_ref,
    own_ref,
    base_ref,
    scored_ref,
    sent_ref,
    *rest,
):
    kept = len(rest) > 4
    *rest, out_ref, peak_ref, total_ref, start_ref = rest
    tile = info_ref.shape[2]
    if kept:
        *rest, embed_buf, whole_ref, embed_sems = rest
        slots, piece = embed_buf.shape[:2]
        pieces = whole_ref.shape[0] // piece

        def fetch(part):
            slot = lax.rem(part, slots)
            place = pl.ds(pl.multiple_of(part * piece, piece), piece)
            return pltpu.make_async_copy(
                embed_ref.at[place], embed_buf.at[slot], embed_sems.at[slot]
            )

        for part in range(min(slots, pieces)):
            fetch(part).start()

        def take(part, carry):
            fetch(part).wait()
            place = pl.ds(pl.multiple_of(part * piece, piece), piece)
            whole_ref[place, :] = embed_buf[lax.rem(part, slots)].astype(BFLOAT)

            @pl.when(part + slots < pieces)
            def _():
                fetch(part + slots).start()

            return carry

    else:
        whole_ref = embed_ref
    wide = 2 * LANES
    out_ref[...] = jnp.zeros_like(out_ref)
    peak_ref[...] = jnp.full_like(peak_ref, FAR)
    total_ref[...] = jnp.zeros_like(total_ref)

    def saves(step):
        start_out, rope_out, start_buf, rope_buf, sems = rest
        slot = lax.rem(step, 2)
        place = pl.ds(pl.multiple_of(step * tile, tile), tile)
        return (
            pltpu.make_async_copy(start_buf.at[slot], start_out.at[place], sems.at[0, slot]),
            pltpu.make_async_copy(rope_buf.at[slot], rope_out.at[place], sems.at[1, slot]),
        )

    def body(step, carry):
        id_row, code_row, pos_row = tile_tokens(info_ref[step], token_bits)
        id_col, pos_col = to_column(id_row), to_column(pos_row)
        low, high = first_ref[step], last_ref[step]
        taken = carry
        if kept:
            limit = whole_ref.shape[0]
            needed = jnp.minimum(limit, high + min(WINDOW, limit))
            wanted = lax.div(needed + piece - 1, piece)
            lax.fori_loop(taken, wanted, take, 0)
            taken = jnp.maximum(taken, wanted)
        start = tile_rows(id_col, low, high, whole_ref, start_ref)
        factor = lax.rsqrt(jnp.mean(start * start, -1, keepdims=True) + EPS_NORM)
        normed = (start * factor * gain_ref[...]).astype(BFLOAT)
        cosine, sine = tile_rope(pos_col, table_ref)
        if kept:

            @pl.when(step >= 2)
            def _():
                for copy in saves(step - 2):
                    copy.wait()

            slot = lax.rem(step, 2)
            rest[2][slot] = start.astype(BFLOAT)
            rest[3][slot] = jnp.concatenate([cosine, sine], 1)
            for copy in saves(step):
                copy.start()
        raw = contract(normed, weights_ref[:, wide : 2 * wide], NN)
        former, latter = raw[:, :LANES], raw[:, LANES:]
        keys = jnp.concatenate(
            [former * cosine - latter * sine, latter * cosine + former * sine], 1
        ).astype(BFLOAT)
        values = contract(normed, weights_ref[:, 2 * wide :], NN).astype(BFLOAT)
        scores = contract(query_ref[...], keys, NT)
        seen = (own_ref[...] == code_row) | (base_ref[...] == code_row)
        scores = jnp.where(seen, scores, FAR)
        peak = peak_ref[...]
        newer = jnp.maximum(peak, jnp.max(scores, 1, keepdims=True))
        expos = jnp.where(seen, jnp.exp(scores - newer[:, 0:1]), 0.0)
        shrink = jnp.exp(peak - newer)
        peak_ref[...] = newer
        total_ref[...] = total_ref[...] * shrink + jnp.sum(expos, 1, keepdims=True)
        out_ref[...] = out_ref[...] * shrink[:, 0:1] + contract(
            expos.astype(BFLOAT), values, NN
        )
        return taken

    count = count_ref[0]
    taken = lax.fori_loop(0, count, body, jnp.int32(0))
    if kept:
        lax.fori_loop(taken, pieces, take, 0)
    if kept:
        for back in (2, 1):

            @pl.when(count >= back)
            def _():
                for copy in saves(count - back):
                    copy.wait()

    queries, part = scored_ref.shape
    per_owner = part // HEAD
    cuts = [slice(head * queries, (head + 1) * queries) for head in range(per_owner)]
    mixed = [out_ref[cuts[h], h * HEAD : (h + 1) * HEAD] for h in range(per_owner)]
    fine = [peak_ref[cuts[h], 0:1] for h in range(per_owner)]
    fine += [total_ref[cuts[h], 0:1] for h in range(per_owner)]
    coarse = [value.astype(BFLOAT).astype(FLOAT) for value in fine]
    rest_of = [value - high for value, high in zip(fine, coarse)]
    filler = jnp.zeros((queries, sent_ref.shape[1] - 2 * part - 4 * per_owner), FLOAT)
    sent_ref[...] = jnp.concatenate(
        mixed + [scored_ref[...]] + coarse + rest_of + [filler], 1
    ).astype(BFLOAT)


def backward_kernel(
    kept,
    chunks,
    blocks,
    token_bits,
    fine_gap,
    steps_ref,
    owner_ref,
    first_ref,
    last_ref,
    scored_ref,
    info_ref,
    start_in_ref,
    rope_in_ref,
    gain_ref,
    both_ref,
    fold_ref,
    told_ref,
    upper_in_ref,
    cosine_ref,
    sine_ref,
    own_ref,
    base_ref,
    grad_embed_ref,
    grad_w_ref,
    grad_turned_ref,
    grad_gain_ref,
    met_ref,
    square_ref,
    carry_ref,
    row_buf,
    both_w_ref,
    query_ref,
    query_t_ref,
    upper_ref,
    upper_t_ref,
    level_ref,
    inner_ref,
    lowered_ref,
    grad_query_ref,
    grad_kv_ref,
    start_ref,
    grad_keys_ref,
    grad_values_ref,
    copy_sem,
    *loaded,
):
    wide = 2 * LANES
    tile = info_ref.shape[2]
    count = steps_ref[0]

    def loads(step):
        start_buf, rope_buf, sems = loaded
        slot = lax.rem(step, 2)
        place = pl.ds(pl.multiple_of(step * tile, tile), tile)
        return (
            pltpu.make_async_copy(start_in_ref.at[place], start_buf.at[slot], sems.at[0, slot]),
            pltpu.make_async_copy(rope_in_ref.at[place], rope_buf.at[slot], sems.at[1, slot]),
        )

    if kept:

        @pl.when(count > 0)
        def _():
            for copy in loads(0):
                copy.start()

    def row_copy(step):
        slot = lax.rem(step, 2)
        place = pl.ds(pl.multiple_of(step * tile, tile), tile)
        return pltpu.make_async_copy(
            row_buf.at[slot], grad_embed_ref.at[place], copy_sem.at[slot]
        )

    met_ref[...] = jnp.zeros_like(met_ref)
    carry_ref[...] = jnp.zeros_like(carry_ref)
    grad_w_ref[...] = jnp.zeros_like(grad_w_ref)
    grad_query_ref[...] = jnp.zeros_like(grad_query_ref)
    grad_gain_ref[...] = jnp.zeros_like(grad_gain_ref)
    owner = owner_ref[0]
    mine = pl.ds(pl.multiple_of(owner * LANES, LANES), LANES)
    part = grad_w_ref.shape[1]
    mine_kv = pl.ds(pl.multiple_of(owner * part, LANES), part)
    lane_head = lax.broadcasted_iota(jnp.int32, (LANES, wide), 1)
    row_head = lax.broadcasted_iota(jnp.int32, (wide, LANES), 0)

    width = gain_ref.shape[1]
    heads = blocks * QUAD
    query_w = contract(both_ref[:, :width], fold_ref[...], NN).astype(BFLOAT)
    both_w_ref[:, :width] = contract(both_ref[:, width : 2 * width], fold_ref[...], NN).astype(
        BFLOAT
    )
    both_w_ref[:, width:] = both_ref[:, 2 * width : 3 * width]

    def unfold(chunk, carry):
        begin = told_ref[chunk, :, width : 2 * width].astype(FLOAT)
        scale = lax.rsqrt(jnp.mean(begin * begin, -1, keepdims=True) + EPS_NORM)
        raw = contract((begin * scale * gain_ref[...]).astype(BFLOAT), query_w, NN)
        cos_one, sin_one = cosine_ref[chunk] * SCALE, sine_ref[chunk] * SCALE
        fine = told_ref[chunk, :, 3 * width :].astype(FLOAT)
        level = jnp.transpose(fine)
        upper_all = contract(upper_in_ref[chunk], both_ref[:, 3 * width :], NT)
        upper_all = upper_all.astype(BFLOAT).astype(FLOAT)
        joint_all = upper_all * told_ref[chunk, :, 2 * width : 3 * width].astype(FLOAT)
        for block in range(blocks):
            place = slice(block * wide, (block + 1) * wide)
            former = raw[:, block * wide : block * wide + LANES]
            latter = raw[:, block * wide + LANES : (block + 1) * wide]
            query = jnp.concatenate(
                [former * cos_one - latter * sin_one, latter * cos_one + former * sin_one], 1
            )
            upper = upper_all[:, place]
            query_t, upper_t = jnp.transpose(query), jnp.transpose(upper)
            joint = jnp.transpose(joint_all[:, place])
            for head in range(QUAD):
                low, high = head * HEAD, (head + 1) * HEAD
                cut = slice(head * LANES, (head + 1) * LANES)
                kept_lanes = (lane_head >= low) & (lane_head < high)
                kept_rows = (row_head >= low) & (row_head < high)
                upper_ref[chunk, block, cut, :] = jnp.where(kept_lanes, upper, 0.0).astype(BFLOAT)
                upper_t_ref[chunk, block, :, cut] = jnp.where(kept_rows, upper_t, 0.0).astype(
                    BFLOAT
                )
                inner_ref[chunk, block, :, cut] = jnp.sum(joint[low:high], 0, keepdims=True)
                row = block * QUAD + head
                fine_row = heads + fine_gap + row
                level_ref[chunk, block, :, cut] = (
                    level[row : row + 1] + level[fine_row : fine_row + 1]
                )
                kept_lanes = lax.shift_right_arithmetic(lane_head & (LANES - 1), HALF_BITS) == head
                kept_rows = lax.shift_right_arithmetic(row_head & (LANES - 1), HALF_BITS) == head
                query_ref[chunk, block, cut, :] = jnp.where(kept_lanes, query, 0.0).astype(BFLOAT)
                query_t_ref[chunk, block, :, cut] = jnp.where(kept_rows, query_t, 0.0).astype(
                    BFLOAT
                )
        return carry

    lax.fori_loop(0, chunks, unfold, 0)

    def body(step, square):
        return square + tile_step(step)

    def tile_step(step):
        if kept:
            key_row = info_ref[step]
        else:
            slab_buf, slab_sem = loaded
            copy = pltpu.make_async_copy(info_ref.at[step], slab_buf, slab_sem)
            copy.start()
            copy.wait()
            key_row = slab_buf[...]
        id_row, code_row, pos_row = tile_tokens(key_row, token_bits)
        code_col = to_column(code_row)
        if kept:

            @pl.when(step + 1 < count)
            def _():
                for copy in loads(step + 1):
                    copy.start()

            for copy in loads(step):
                copy.wait()
            slot = lax.rem(step, 2)
            start = loaded[0][slot].astype(FLOAT)
            cosine, sine = loaded[1][slot, :, :LANES], loaded[1][slot, :, LANES:]
        else:
            id_col, pos_col = to_column(id_row), to_column(pos_row)
            start = tile_rows(id_col, first_ref[step], last_ref[step], start_in_ref, start_ref)
            cosine, sine = tile_rope(pos_col, rope_in_ref)
        factor = lax.rsqrt(jnp.mean(start * start, -1, keepdims=True) + EPS_NORM)
        normed = (start * factor * gain_ref[...]).astype(BFLOAT)
        raw = contract(normed, both_w_ref[:, :width], NN)
        values = contract(normed, both_w_ref[:, width:], NN).astype(BFLOAT)
        keys = []
        for block in range(blocks):
            former = raw[:, block * wide : block * wide + LANES]
            latter = raw[:, block * wide + LANES : (block + 1) * wide]
            keys.append(
                jnp.concatenate(
                    [former * cosine - latter * sine, latter * cosine + former * sine], 1
                ).astype(BFLOAT)
            )
        if chunks > 1:
            grad_keys_ref[...] = jnp.zeros_like(grad_keys_ref)
            grad_values_ref[...] = jnp.zeros_like(grad_values_ref)

        def attend(chunk):
            seen = (code_col == own_ref[chunk]) | (code_col == base_ref[chunk])
            hidden = jnp.where(seen, 0.0, FAR)
            hidden = jnp.concatenate([hidden] * QUAD, 1)
            for block in range(blocks):
                place = pl.ds(block * wide, wide)
                scores = contract(keys[block], query_t_ref[chunk, block], NN)
                weights = jnp.exp(scores - level_ref[chunk, block] + hidden)
                slopes = contract(
                    values[:, block * wide : (block + 1) * wide], upper_t_ref[chunk, block], NN
                )
                lowered = (weights * (slopes - inner_ref[chunk, block])).astype(BFLOAT)
                lowered_ref[...] = lowered
                grad_query_ref[chunk, block] += contract(keys[block], lowered_ref[:, mine], TN)
                grad_k = contract(lowered, query_ref[chunk, block], NN)
                grad_v = contract(weights.astype(BFLOAT), upper_ref[chunk, block], NN)
                if chunks > 1:
                    grad_keys_ref[:, place] += grad_k
                    grad_values_ref[:, place] += grad_v
                else:
                    grad_keys_ref[:, place] = grad_k
                    grad_values_ref[:, place] = grad_v

        if chunks > 1:
            lax.fori_loop(0, chunks, lambda chunk, c: (attend(chunk), c)[1], 0)
        else:
            attend(0)
        pieces = []
        for block in range(blocks):
            former = grad_keys_ref[:, pl.ds(block * wide, LANES)]
            latter = grad_keys_ref[:, pl.ds(block * wide + LANES, LANES)]
            pieces.append((former * cosine + latter * sine).astype(BFLOAT))
            pieces.append((latter * cosine - former * sine).astype(BFLOAT))
        grad_kv = jnp.concatenate(pieces + [grad_values_ref[...].astype(BFLOAT)], 1)
        grad_kv_ref[...] = grad_kv
        grad_w_ref[...] += contract(normed, grad_kv_ref[:, mine_kv], TN)
        grad_normed = contract(grad_kv, both_w_ref[...], NT)
        scaled = start * factor
        grad_gain_ref[...] += jnp.sum(grad_normed * scaled, 0, keepdims=True)
        weighted = grad_normed * gain_ref[...]
        inner = jnp.mean(weighted * scaled, -1, keepdims=True)
        grad_start = (factor * (weighted - scaled * inner)).astype(BFLOAT)

        @pl.when(step >= 2)
        def _():
            row_copy(step - 2).wait()

        row_buf[lax.rem(step, 2)] = grad_start
        row_copy(step).start()
        met_ref[...] += contract(one_hot(scored_ref[...] == id_row), grad_start, NN)
        before = jnp.where(step > 0, last_ref[jnp.maximum(step - 1, 0)], -2)
        final = last_ref[step]
        line = lax.broadcasted_iota(jnp.int32, (8, tile), 0)
        edges = ((line == 0) & (id_row == before)) | ((line == 1) & (id_row == final))
        edges = contract(one_hot(edges), grad_start, NN)
        held = carry_ref[...]
        products = contract(grad_start, grad_start, NT)
        square = jnp.sum(jnp.where(to_column(id_row) == id_row, products, 0.0))
        square += 2.0 * jnp.sum(held * edges[0:1])
        carry_ref[...] = edges[1:2] + jnp.where(final == before, held, 0.0)
        return square

    square = lax.fori_loop(0, count, body, jnp.float32(0.0))
    line = lax.broadcasted_iota(jnp.int32, square_ref.shape, 0)
    lane = lax.broadcasted_iota(jnp.int32, square_ref.shape, 1)
    square_ref[...] = jnp.where((line == 0) & (lane == 0), square, 0.0)
    for back in (2, 1):

        @pl.when(count >= back)
        def _():
            row_copy(count - back).wait()

    for half in range(2):
        place = pl.ds(pl.multiple_of(half * LANES + owner * HALF, HALF), HALF)
        grad_turned_ref[:, :, half] = grad_query_ref[:, :, place, :] * SCALE


def owner_kernel(
    owners,
    thin,
    misc_lane,
    rest_ref,
    leader_ref,
    got_ref,
    query_w_ref,
    start_ref,
    after_ref,
    cosine_ref,
    sine_ref,
    gain_ref,
    gain_part_ref,
    square_ref,
    rows_ref,
    late_ref,
    told_ref,
    kv_ref,
):
    groups, _, quarter = got_ref.shape
    part = quarter // 2
    per_owner = part // HEAD
    cosine, sine = cosine_ref[...], sine_ref[...]
    square, turned, met = 0.0, {}, []
    for owner in range(owners):

        def add(shard, total):
            return total + got_ref[shard * owners + owner].astype(FLOAT)

        total = lax.fori_loop(
            0, groups // owners, add, jnp.zeros((thin + 2 * NCONT, quarter), FLOAT)
        )
        rows = total[:thin]
        kv_ref[:, owner * quarter : (owner + 1) * quarter] = rows
        square += jnp.sum(rows * rows)
        near = total[thin : thin + NCONT]
        near = near[:, :part] + near[:, part:]
        for slot in range(per_owner):
            former = near[:, slot * HEAD : slot * HEAD + HALF]
            latter = near[:, slot * HEAD + HALF : (slot + 1) * HEAD]
            turned[slot * owners + owner] = [
                former * cosine + latter * sine,
                latter * cosine - former * sine,
            ]
        far = total[thin + NCONT :]
        met.append(far[:, :part] + far[:, part:])
    met = jnp.concatenate(met, 1)
    grad_query = jnp.concatenate(sum([turned[head] for head in range(len(turned))], []), 1)
    grad_query = grad_query.astype(BFLOAT)
    upstream = contract(grad_query, query_w_ref[...], NT)
    start = start_ref[...]
    factor = lax.rsqrt(jnp.mean(start * start, -1, keepdims=True) + EPS_NORM)
    scaled = start * factor
    weighted = upstream * gain_ref[...]
    inner = jnp.mean(weighted * scaled, -1, keepdims=True)
    extra = after_ref[...] + factor * (weighted - scaled * inner)
    extra = extra.astype(BFLOAT).astype(FLOAT)
    gain = jnp.sum(upstream * scaled, 0, keepdims=True) + gain_part_ref[...] * (1.0 / owners)
    square += rest_ref[0] + 2.0 * jnp.sum(met * extra)
    square += leader_ref[0] * jnp.sum(square_ref[...])
    rows = rows_ref[...]
    line = lax.broadcasted_iota(jnp.int32, rows.shape, 0)
    lane = lax.broadcasted_iota(jnp.int32, rows.shape, 1)
    whole = jnp.full(rows.shape, square, FLOAT)
    high = whole.astype(BFLOAT).astype(FLOAT)
    rows = jnp.where(line == 0, gain, rows)
    rows = jnp.where((line == 6) & (lane == misc_lane), high, rows)
    rows = jnp.where((line == 6) & (lane == misc_lane + 1), whole - high, rows)
    payload = jnp.concatenate([extra, grad_query.astype(FLOAT), rows], 0).astype(BFLOAT)

    def put(group, carry):
        told_ref[group] = payload
        return carry

    lax.fori_loop(0, groups, put, 0)


def finish_kernel(rates, decays, columns, told_ref, id_col_ref, id_row_ref, gram_ref, *refs):
    normed_ref, slice_ref, *refs = refs
    sources, refs = refs[:12], refs[12:]
    extra_ref, query_ref, scalar_ref, *made_refs = refs
    count = extra_ref.shape[0]
    chunk = min(count, LANES)
    span = 16 * chunk // NCONT
    row = lax.broadcasted_iota(jnp.int32, (chunk, span), 0)
    col = lax.broadcasted_iota(jnp.int32, (chunk, span), 1)
    spot = 16 * lax.shift_right_arithmetic(row, 2)
    place = row & (NCONT - 1)
    line = lax.broadcasted_iota(jnp.int32, (8, span), 0)
    side = lax.broadcasted_iota(jnp.int32, (8, span), 1)
    which = lax.broadcasted_iota(jnp.int32, (chunk, columns), 0) & (NCONT - 1)
    sums, extra, query, logits = 0.0, [], [], []
    for begin in range(0, count, chunk):
        told = told_ref[begin // NCONT * 16 : begin // NCONT * 16 + span, :]
        extra.append(contract(one_hot(col == spot + place), told, NN).astype(BFLOAT))
        query.append(contract(one_hot(col == spot + place + NCONT), told, NN).astype(BFLOAT))
        misc = contract(one_hot(col == spot + 14), told[:, :LANES], NN)
        own = jnp.zeros((chunk, columns), FLOAT)
        for turn in range(NCONT):
            own = jnp.where(which == turn, misc[:, turn * columns : (turn + 1) * columns], own)
        logits.append(own.astype(BFLOAT))
        sums = sums + contract(one_hot((side & 15) == line + 8), told, NN)
    extra, query, logits = (jnp.concatenate(parts, 0) for parts in (extra, query, logits))
    extra_ref[...] = extra
    query_ref[...] = contract(slice_ref[...], query, TN)
    same = id_col_ref[...] == id_row_ref[...]
    square = jnp.sum(jnp.where(same, contract(extra, extra, NT), 0.0))
    square += jnp.sum(gram_ref[...] * contract(query, query, NT))
    grad_router = contract(logits, normed_ref[...], TN)
    gains, vectors, head = sums[0:3], sums[3:5], sums[5:6]
    misc = sums[6:7, NCONT * columns : NCONT * columns + 4]
    loss = jnp.sum(misc[:, 0:2])
    square += jnp.sum(misc[:, 2:4]) + jnp.sum(grad_router * grad_router)
    square += jnp.sum(sums[0:6] * sums[0:6])
    norm = jnp.sqrt(jnp.full((8, LANES), square, FLOAT))
    factor = THRESH / jnp.maximum(norm, THRESH)
    lane = lax.broadcasted_iota(jnp.int32, (8, LANES), 1)
    scalar_ref[...] = jnp.where(lane == 0, loss, jnp.where(lane == 1, norm, factor))
    factor = factor[0:1, 0:1]
    for index, grad in enumerate((grad_router, gains, vectors, head)):
        state = [sources[3 * index + part][...] for part in range(3)]
        made = adam_update(*state, grad * factor, rates[index], decays[index])
        for part in range(3):
            made_refs[3 * index + part][...] = made[part]


def expert_kernel(
    experts,
    owner_ref,
    told_ref,
    gates_ref,
    inner_ref,
    result_ref,
    down_ref,
    in_ref,
    sent_ref,
    grad_result_ref,
    grad_inner_ref,
    upstream_ref,
    back_ref,
):
    count, width = upstream_ref.shape
    local, units = down_ref.shape[0], down_ref.shape[1]

    def gather(pair, carry):
        rows = [told_ref[2 * pair + side].astype(FLOAT) for side in range(2)]
        place = pl.ds(pl.multiple_of(pair * 2 * NCONT, 2 * NCONT), 2 * NCONT)
        upstream_ref[place, :] = jnp.concatenate(rows, 0)
        return carry

    lax.fori_loop(0, count // (2 * NCONT), gather, 0)
    upstream = upstream_ref[...]
    owner = owner_ref[0]
    lane = lax.broadcasted_iota(jnp.int32, (count, LANES), 1)
    tail = jnp.zeros((count, LANES), FLOAT)
    back = 0.0
    for which in range(local):
        result = result_ref[which]
        dots = jnp.sum(upstream * result, -1, keepdims=True)
        high = dots.astype(BFLOAT).astype(FLOAT)
        spot = owner * local + which
        tail = jnp.where(lane == spot, high, tail)
        tail = jnp.where(lane == spot + experts, dots - high, tail)
        grad_result = (gates_ref[:, which : which + 1] * upstream).astype(BFLOAT)
        grad_result_ref[which] = grad_result
        grad_active = contract(grad_result, down_ref[which], NT)
        gate_half, up_half = inner_ref[which, :, :units], inner_ref[which, :, units:]
        sigma = lax.logistic(gate_half)
        grad_gate = grad_active * up_half * sigma * (1.0 + gate_half * (1.0 - sigma))
        grad_up = grad_active * gate_half * sigma
        grad_inner = jnp.concatenate([grad_gate, grad_up], 1).astype(BFLOAT)
        grad_inner_ref[which] = grad_inner
        back += contract(grad_inner, in_ref[which], NT)
    back_ref[...] = jnp.concatenate([back, tail], 1)

    def scatter(pair, carry):
        place = pl.ds(pl.multiple_of(pair * 2 * NCONT, 2 * NCONT), 2 * NCONT)
        rows = back_ref[place, :]
        for side in range(2):
            sent_ref[2 * pair + side] = rows[side * NCONT : (side + 1) * NCONT].astype(BFLOAT)
        return carry

    lax.fori_loop(0, count // (2 * NCONT), scatter, 0)


def pick_kernel(rows_ref, source_ref, picked_ref, copy_sem):
    count = picked_ref.shape[0]

    def fetch(spot, carry):
        pltpu.make_async_copy(
            source_ref.at[pl.ds(rows_ref[spot], 1)], picked_ref.at[pl.ds(spot, 1)], copy_sem
        ).start()
        return carry

    lax.fori_loop(0, count, fetch, 0)
    pltpu.make_async_copy(source_ref.at[pl.ds(0, count)], picked_ref, copy_sem).wait()


def gather_kernel(
    token_bits,
    base_ref,
    begin_ref,
    end_ref,
    order_ref,
    first_row_ref,
    last_row_ref,
    info_ref,
    rows_ref,
    late_ref,
    made_ref,
    grad_ref,
    row_buf,
    sems,
):
    rows = made_ref.shape[0]
    tile = info_ref.shape[2]
    block, blocks = pl.program_id(0), pl.num_programs(0)
    base = base_ref[0] + block * rows
    begin, end = begin_ref[block], end_ref[block]

    def fetch(step, turn):
        slot = lax.rem(turn, 2)
        place = pl.ds(pl.multiple_of(step * tile, tile), tile)
        return pltpu.make_async_copy(rows_ref.at[place], row_buf.at[slot], sems.at[slot])

    @pl.when(block == 0)
    def _():
        fetch(begin, order_ref[block]).start()

    grad_ref[...] = jnp.zeros_like(grad_ref)
    lines = lax.broadcasted_iota(jnp.int32, (ROWS, tile), 0)

    def gather(step, carry):
        turn = order_ref[block] + step - begin
        later = step + 1 < end
        following = jnp.where(later, step + 1, begin_ref[jnp.minimum(block + 1, blocks - 1)])

        @pl.when(later | (block + 1 < blocks))
        def _():
            fetch(following, turn + 1).start()

        fetch(step, turn).wait()
        key_row = info_ref[step]
        id_row = jnp.where(key_row >= 0, lax.shift_right_arithmetic(key_row, token_bits), -1)
        id_row = id_row - base
        slot = lax.rem(turn, 2)

        def put(part, inner):
            place = pl.multiple_of(part * ROWS, ROWS)
            grad_ref[pl.ds(place, ROWS), :] += contract(
                one_hot(id_row == lines + place), row_buf[slot], NN
            )
            return inner

        low = jnp.maximum(first_row_ref[step] - base, 0)
        high = jnp.minimum(last_row_ref[step] - base, rows - 1)
        reach = jnp.where(high >= low, lax.div(jnp.maximum(high, 0), ROWS) + 1, 0)
        lax.fori_loop(lax.div(low, ROWS), reach, put, 0)
        return carry

    lax.fori_loop(begin, end, gather, 0)
    made_ref[...] = grad_ref[...].astype(BFLOAT)


def adam_kernel(
    rate,
    decay,
    low_blocks,
    factor_ref,
    ids_ref,
    extra_ref,
    low_ref,
    high_ref,
    weight_ref,
    first_ref,
    second_ref,
    weight_out,
    first_out,
    second_out,
):
    rows = weight_out.shape[0]
    block = pl.program_id(0)
    spots = lax.broadcasted_iota(jnp.int32, (rows, ids_ref.shape[1]), 0) + block * rows
    extra = contract(one_hot(ids_ref[...] == spots), extra_ref[...], NN)
    chosen = (block < low_blocks).astype(FLOAT)
    grad = low_ref[...].astype(FLOAT) * chosen + high_ref[...].astype(FLOAT) * (1.0 - chosen)
    grad = (grad + extra) * factor_ref[0]
    made = adam_update(weight_ref[...], first_ref[...], second_ref[...], grad, rate, decay)
    weight_out[...], first_out[...], second_out[...] = made


def matrix_adam_kernel(
    rate, decay, factor_ref, weight_ref, first_ref, second_ref, grad_ref, weight_out, first_out, second_out
):
    units = grad_ref.shape[3]
    for source in range(grad_ref.shape[0]):
        place = slice(source * units, (source + 1) * units)
        grad = grad_ref[source, 0].astype(FLOAT) * factor_ref[0]
        made = adam_update(
            weight_ref[0, :, place], first_ref[0, :, place], second_ref[0, :, place], grad, rate, decay
        )
        weight_out[0, :, place], first_out[0, :, place], second_out[0, :, place] = made


def split_float(values):
    high = lax.reduce_precision(values, 8, 7)
    return jnp.concatenate([high, values - high], -1).astype(BFLOAT)


def join_float(parts):
    half = parts.shape[-1] // 2
    parts = parts.astype(FLOAT)
    return parts[..., :half] + parts[..., half:]


def shards(
    token_ids,
    routes,
    last_valid,
    rank_pairs,
    embedding,
    embedding_first,
    embedding_second,
    attend_in,
    attend_in_first,
    attend_in_second,
    attend_out,
    attend_out_first,
    attend_out_second,
    expert_in,
    expert_in_first,
    expert_in_second,
    expert_out,
    expert_out_first,
    expert_out_second,
    router,
    router_first,
    router_second,
    norm_gains,
    norm_gains_first,
    norm_gains_second,
    const_vectors,
    const_vectors_first,
    const_vectors_second,
    score_head,
    score_head_first,
    score_head_second,
):
    shard_count = lax.axis_size("dp")
    owners = lax.axis_size("expert")
    groups = shard_count * owners
    my_shard = lax.axis_index("dp")
    my_owner = lax.axis_index("expert")
    width = embedding.shape[1]
    heads = width // HEAD
    blocks = heads // QUAD
    per_owner = heads // owners
    local_experts = expert_in.shape[0]
    experts = local_experts * owners
    routed = experts + 4
    hidden_units = expert_in.shape[2] // 2
    shard_rows = embedding.shape[0]
    slice_rows = attend_in.shape[0]
    queries = groups * NCONT
    everything = groups * TOK
    tile = TILE if everything <= KEEP else TILE_SMALL
    far_key = jnp.iinfo(jnp.int32).max
    gain_row = norm_gains[0:1]

    packed = jnp.concatenate(
        [token_ids[0], last_valid[0], jnp.zeros(LANES - NCONT, jnp.int32)]
    )
    known = spread(packed, BOTH)

    attend_b = attend_in.astype(BFLOAT)
    into = jnp.arange(3 * 2 * LANES, dtype=jnp.int32)
    which_part, spot = into // (2 * LANES), into % (2 * LANES)
    folded_head, folded_dim = spot % LANES // HALF, spot // LANES * HALF + spot % HALF
    is_value = which_part == 2
    head_slot = jnp.where(is_value, spot // HEAD, folded_head)
    dim = jnp.where(is_value, spot % HEAD, folded_dim)
    origin = which_part * width + (head_slot * owners + my_owner) * HEAD + dim
    origin = jnp.where(head_slot < per_owner, origin, -1)
    select = (jnp.arange(3 * width, dtype=jnp.int32)[:, None] == origin[None, :]).astype(BFLOAT)
    mine_in = jnp.dot(attend_b, select, preferred_element_type=FLOAT).astype(BFLOAT)
    weights_e = lax.all_gather(mine_in, "dp", tiled=True)
    piece = slice_rows // owners
    both_b = jnp.concatenate([attend_b, attend_out.astype(BFLOAT)], 1)
    both_b = lax.dynamic_slice_in_dim(both_b, my_owner * piece, piece, 0)

    units = hidden_units // shard_count
    cut_in = expert_in.astype(BFLOAT).reshape(
        local_experts, slice_rows, 2, shard_count, units
    )
    cut_in = cut_in.transpose(3, 0, 1, 2, 4)
    cut_in = cut_in.reshape(shard_count, local_experts * slice_rows, 2 * units)
    cut_in, known = lax.optimization_barrier((cut_in, known))
    ids, last = known[:, :TOK], known[:, TOK : TOK + NCONT]
    got_in = swap(cut_in, "dp")

    places = jnp.arange(TOK, dtype=jnp.int32)
    offsets = jnp.arange(CLEN, dtype=jnp.int32)
    seen_late = (offsets[None, None, :] <= last[:, :, None]).reshape(groups, NCONT * CLEN)
    seen = jnp.concatenate([jnp.ones((groups, PROMPT), bool), seen_late], 1)
    local = ids - my_shard * shard_rows
    here = seen & (local >= 0) & (local < shard_rows)
    index = jnp.arange(everything, dtype=jnp.int32).reshape(groups, TOK)
    key = jnp.where(here, local * everything + index, far_key)
    ordered = lax.sort(key.reshape(-1))
    tile_count = (jnp.sum(here.astype(jnp.int32)) + tile - 1) // tile
    ordered = jnp.where(ordered == far_key, -1, ordered)
    info = ordered.reshape(everything // tile, 1, tile)
    token_bits = everything.bit_length() - 1
    rows_of = jnp.maximum(lax.shift_right_arithmetic(ordered, token_bits), 0)
    rows_of = rows_of.reshape(everything // tile, tile)
    first_row = rows_of[:, 0]
    last_row = jnp.max(rows_of, 1)
    tile_count = jnp.maximum(tile_count, 1).reshape(1)

    at_last = (offsets[None, None, :] == last[:, :, None]).astype(jnp.int32)
    scored_ids = jnp.sum(ids[:, PROMPT:].reshape(groups, NCONT, CLEN) * at_last, 2)
    scored_local = scored_ids.reshape(-1) - my_shard * shard_rows
    scored_here = (scored_local >= 0) & (scored_local < shard_rows)
    scored_row = jnp.clip(scored_local, 0, shard_rows - 1)
    scored_row = scored_row.astype(jnp.int32)
    scored_start = pl.pallas_call(
        pick_kernel,
        out_shape=jax.ShapeDtypeStruct((queries, width), FLOAT),
        in_specs=[SMEM_SPEC, pl.BlockSpec(memory_space=pl.ANY)],
        out_specs=VMEM_SPEC,
        scratch_shapes=[pltpu.SemaphoreType.DMA],
    )(scored_row, embedding)
    scored_start = jnp.where(scored_here[:, None], scored_start, 0.0)
    scored_start = lax.reduce_precision(scored_start, 8, 7)
    scored_normed = rms_forward(scored_start, norm_gains[0])[0].astype(BFLOAT)
    cos_table, sin_table = rope_constants()
    late_cos, late_sin = jnp.asarray(cos_table[PROMPT:]), jnp.asarray(sin_table[PROMPT:])
    at_late = (offsets[None, :] == last.reshape(-1)[:, None]).astype(FLOAT)
    scored_cos = jnp.dot(at_late, late_cos, precision=HIGH)
    scored_sin = jnp.dot(at_late, late_sin, precision=HIGH)
    own_late = (offsets[None, :] == last_valid[0][:, None]).astype(FLOAT)
    own_cos = jnp.dot(own_late, late_cos, precision=HIGH)
    own_sin = jnp.dot(own_late, late_sin, precision=HIGH)
    own_last = last_valid[0]
    own_pick = (offsets[None, :] == own_last[:, None]).astype(jnp.int32)
    route_row = jnp.sum(
        routes[0, PROMPT:].reshape(NCONT, CLEN, 2) * own_pick[..., None], 1
    )
    pick_table = (route_row[:, :, None] == jnp.arange(routed)[None, None, :]).astype(FLOAT)
    base_code = (jnp.arange(queries, dtype=jnp.int32) // NCONT) * 8
    own_code = base_code + jnp.arange(queries, dtype=jnp.int32) % NCONT + 1
    own_tall = jnp.tile(own_code, per_owner)[:, None]
    base_tall = jnp.tile(base_code, per_owner)[:, None]
    down_w = expert_out.astype(BFLOAT)
    head_states = (score_head[None], score_head_first[None], score_head_second[None])
    (
        weights_e,
        both_b,
        info,
        scored_normed,
        scored_cos,
        scored_sin,
        own_cos,
        own_sin,
        pick_table,
        own_tall,
        base_tall,
        down_w,
        tile_count,
        head_states,
    ) = lax.optimization_barrier(
        (
            weights_e,
            both_b,
            info,
            scored_normed,
            scored_cos,
            scored_sin,
            own_cos,
            own_sin,
            pick_table,
            own_tall,
            base_tall,
            down_w,
            tile_count,
            head_states,
        )
    )
    cos_wide, sin_wide = jnp.tile(scored_cos, (1, QUAD)), jnp.tile(scored_sin, (1, QUAD))
    query_w_e = weights_e[:, : 2 * LANES]
    both_w = lax.all_gather(both_b, BOTH, tiled=True)
    query_w, out_w = both_w[:, :width], both_w[:, 3 * width :]
    raw = jnp.dot(scored_normed, query_w_e, preferred_element_type=FLOAT)
    former, latter = raw[:, :LANES], raw[:, LANES:]
    query_part = jnp.concatenate(
        [former * cos_wide - latter * sin_wide, latter * cos_wide + former * sin_wide], 1
    ).astype(BFLOAT)
    kept = everything <= KEEP
    embed_b = embedding if kept else embedding.astype(BFLOAT)
    used = per_owner * HALF
    query_part = jnp.concatenate([query_part[:, :used], query_part[:, LANES : LANES + used]], 1)
    query_e = jnp.sum(spread(query_part, "dp").astype(FLOAT), 0)
    idle = jnp.zeros((queries, LANES - used), FLOAT)
    query_e = jnp.concatenate([query_e[:, :used], idle, query_e[:, used:], idle], 1)

    lane_head = (jnp.arange(2 * LANES) % LANES) // HALF
    head_lanes = (lane_head[None, :] == jnp.arange(per_owner)[:, None]).astype(FLOAT)
    query_rows = (query_e[None] * SCALE * head_lanes[:, None, :]).astype(BFLOAT)
    query_rows = query_rows.reshape(per_owner * queries, 2 * LANES)
    table = jnp.asarray(rope_split())
    any_spec = pl.BlockSpec(memory_space=pl.ANY)
    part = per_owner * HEAD
    start_cut = lax.dynamic_slice_in_dim(scored_start, my_owner * part, part, 1)
    sent_lanes = 2 * part + LANES
    query_count = per_owner * queries
    kept_shapes = (
        jax.ShapeDtypeStruct((everything, width), BFLOAT),
        jax.ShapeDtypeStruct((everything, 2 * LANES), FLOAT),
    )
    sent, *saved = pl.pallas_call(
        functools.partial(forward_kernel, token_bits),
        in_specs=[SMEM_SPEC] * 3
        + [VMEM_SPEC, any_spec if kept else VMEM_SPEC]
        + [VMEM_SPEC] * 7,
        out_specs=(VMEM_SPEC,) + (any_spec,) * (2 * kept),
        scratch_shapes=[
            pltpu.VMEM((2, tile, width), BFLOAT),
            pltpu.VMEM((2, tile, 2 * LANES), FLOAT),
            pltpu.SemaphoreType.DMA((2, 2)),
            pltpu.VMEM((4, min(2 * ROWS, shard_rows), width), FLOAT),
            pltpu.VMEM((shard_rows, width), BFLOAT),
            pltpu.SemaphoreType.DMA((4,)),
        ]
        * kept
        + [
            pltpu.VMEM((query_count, 2 * LANES), FLOAT),
            pltpu.VMEM((query_count, LANES), FLOAT),
            pltpu.VMEM((query_count, LANES), FLOAT),
            pltpu.VMEM((tile, width), FLOAT),
        ],
        out_shape=(jax.ShapeDtypeStruct((queries, sent_lanes), BFLOAT),) + kept_shapes * kept,
        compiler_params=pltpu.CompilerParams(vmem_limit_bytes=FORWARD_LIMIT),
        cost_estimate=pl.CostEstimate(
            flops=30_000_000_000, bytes_accessed=20_000_000, transcendentals=2_000_000
        ),
    )(
        tile_count,
        first_row,
        last_row,
        info,
        embed_b,
        gain_row,
        weights_e,
        table,
        query_rows,
        own_tall,
        base_tall,
        start_cut,
    )
    sent, got_in = lax.optimization_barrier((sent, got_in))
    in_w = got_in.reshape(shard_count, local_experts, slice_rows, 2 * units)
    in_w = in_w.transpose(1, 0, 2, 3).reshape(local_experts, width, 2 * units)
    got = swap(sent.reshape(groups, NCONT, -1), BOTH)
    got = got.reshape(shard_count, owners, NCONT, -1)
    got = got.astype(FLOAT)
    got_out = got[..., :part].reshape(shard_count, owners, NCONT, per_owner, HEAD)
    got_start = got[..., part : 2 * part]
    got_fine = join_float(got[..., 2 * part : 2 * part + 4 * per_owner])
    got_peak, got_total = got_fine[..., :per_owner], got_fine[..., per_owner:]
    peak = jnp.max(got_peak, 0)
    share = jnp.exp(got_peak - peak[None])
    total = jnp.sum(share * got_total, 0)
    mixed = jnp.sum(share[..., None] * got_out, 0) / total[..., None]
    mixed = mixed.transpose(1, 2, 0, 3).reshape(NCONT, width)
    level = (peak + jnp.log(total)).transpose(1, 2, 0).reshape(NCONT, heads)
    start_x = jnp.sum(got_start, 0).transpose(1, 0, 2).reshape(NCONT, width)

    router_b = router.astype(BFLOAT)
    after_attn = start_x + jnp.dot(mixed.astype(BFLOAT), out_w, preferred_element_type=FLOAT)
    normed_two, factor_two = rms_forward(after_attn, norm_gains[1])
    normed_two_b = normed_two.astype(BFLOAT)
    logits = jnp.dot(normed_two_b, router_b, preferred_element_type=FLOAT)
    gate_probs = jax.nn.softmax(logits[:, :routed], -1)
    alphas = [
        jax.nn.softmax(logits[:, routed + 2 * which : routed + 2 * which + 2], -1)
        for which in range(2)
    ]
    gate_pick = jnp.sum(pick_table * gate_probs[:, None, :], -1)
    gate_full = jnp.sum(pick_table * gate_pick[..., None], 1)[:, :experts]
    fine = split_float(jnp.concatenate([level, gate_full], 1))
    tail = jnp.zeros((NCONT, LANES - 2 * (heads + experts)), BFLOAT)
    told = jnp.concatenate(
        [normed_two_b, start_x.astype(BFLOAT), mixed.astype(BFLOAT), fine, tail], 1
    )
    told, first_late, last_late = lax.optimization_barrier((told, first_row, last_row))
    block_rows = min(4 * ROWS, shard_rows // 2)
    row_blocks = shard_rows // block_rows
    low_blocks = max(1, row_blocks * 3 // 8)
    bases = jnp.arange(0, shard_rows, block_rows, dtype=jnp.int32)[:, None]
    filled = (jnp.arange(everything // tile) < tile_count)[None, :]
    begins = jnp.sum((filled & (last_late[None, :] < bases)).astype(jnp.int32), 1)
    begins = jnp.minimum(begins, tile_count - 1)
    ends = jnp.sum((filled & (first_late[None, :] < bases + block_rows)).astype(jnp.int32), 1)
    ends = jnp.maximum(ends, begins + 1)
    earlier = np.arange(row_blocks)[:, None] > np.arange(row_blocks)[None, :]
    orders = jnp.sum((ends - begins)[None, :] * earlier.astype(np.int32), 1)
    told = all_told = spread(told, BOTH).reshape(queries, -1)
    all_normed_b = told[:, :width]
    all_start = told[:, width : 2 * width].astype(FLOAT)
    all_mixed_b = told[:, 2 * width : 3 * width]
    all_fine = join_float(told[:, 3 * width : 3 * width + 2 * (heads + experts)])
    all_level, all_gates = all_fine[:, :heads], all_fine[:, heads:]
    own_gates = lax.dynamic_slice_in_dim(all_gates, my_owner * local_experts, local_experts, 1)

    inner_all, active_all, result_all = [], [], []
    for which in range(local_experts):
        inner = jnp.dot(all_normed_b, in_w[which], preferred_element_type=FLOAT)
        active = (jax.nn.silu(inner[:, :units]) * inner[:, units:]).astype(BFLOAT)
        inner_all.append(inner)
        active_all.append(active)
        result_all.append(jnp.dot(active, down_w[which], preferred_element_type=FLOAT))
    combined = sum(own_gates[:, w : w + 1] * result_all[w] for w in range(local_experts))
    combined = combined.astype(BFLOAT).reshape(groups, NCONT, width)
    fetched = jnp.sum(swap(combined, BOTH).astype(FLOAT), 0)

    is_copy = (route_row == experts + 1).astype(FLOAT)[..., None]
    chosen = [(route_row == experts + 2 + which).astype(FLOAT)[..., None] for which in range(2)]
    branch = is_copy * normed_two[:, None, :]
    for which in range(2):
        constant = (
            alphas[which][:, None, 0:1] * normed_two[:, None, :]
            + alphas[which][:, None, 1:2] * const_vectors[which]
        )
        branch = branch + chosen[which] * constant
    after_ffn = after_attn + fetched + jnp.sum(gate_pick[..., None] * branch, 1)
    final, factor_three = rms_forward(after_ffn, norm_gains[2])
    picked = jnp.sum(final * score_head[None, :], -1)
    pair_rows = rank_pairs[0]
    lead = (pair_rows[:, 0:1] == jnp.arange(NCONT)[None, :]).astype(FLOAT)
    other = (pair_rows[:, 1:2] == jnp.arange(NCONT)[None, :]).astype(FLOAT)
    sides = lead - other
    margin = jnp.sum(sides * picked[None, :], 1)
    loss_part = jnp.sum(jax.nn.softplus(-margin))
    grad_margin = -jax.nn.sigmoid(-margin) * (1.0 / (groups * NPAIR))
    grad_picked = jnp.sum(sides * grad_margin[:, None], 0)
    grad_head = jnp.sum(grad_picked[:, None] * final, 0)
    grad_ffn, grad_gain_final = rms_backward(
        after_ffn, factor_three, norm_gains[2], grad_picked[:, None] * score_head[None, :]
    )
    all_ffn = spread(grad_ffn.astype(BFLOAT), BOTH)

    returned, grad_result, grad_inner = pl.pallas_call(
        functools.partial(expert_kernel, experts),
        out_shape=(
            jax.ShapeDtypeStruct((groups, NCONT, width + LANES), BFLOAT),
            jax.ShapeDtypeStruct((local_experts, queries, width), BFLOAT),
            jax.ShapeDtypeStruct((local_experts, queries, 2 * units), BFLOAT),
        ),
        in_specs=[SMEM_SPEC] + [VMEM_SPEC] * 6,
        out_specs=(VMEM_SPEC,) * 3,
        scratch_shapes=[
            pltpu.VMEM((queries, width), FLOAT),
            pltpu.VMEM((queries, width + LANES), FLOAT),
        ],
        compiler_params=pltpu.CompilerParams(vmem_limit_bytes=VMEM_LIMIT),
    )(
        my_owner.astype(jnp.int32).reshape(1),
        all_ffn,
        own_gates,
        jnp.stack(inner_all),
        jnp.stack(result_all),
        down_w,
        in_w,
    )
    returned = jnp.sum(swap(returned, BOTH).astype(FLOAT), 0)
    returned_grad = returned[:, :width]
    returned_dots = join_float(returned[:, width : width + 2 * experts])
    grad_in = jnp.stack(
        [contract(all_normed_b, grad_inner[w], TN) for w in range(local_experts)]
    )
    grad_expert_out = jnp.stack(
        [contract(active_all[w], grad_result[w], TN) for w in range(local_experts)]
    )

    grad_pick = jnp.sum(grad_ffn[:, None, :] * branch, -1) + jnp.sum(
        pick_table[:, :, :experts] * returned_dots[:, None, :], -1
    )
    grad_branch = gate_pick[..., None] * grad_ffn[:, None, :]
    grad_normed_two = returned_grad + jnp.sum(grad_branch * is_copy, 1)
    grad_vectors = []
    grad_alpha_parts = []
    for which in range(2):
        masked = jnp.sum(chosen[which] * grad_branch, 1)
        grad_vectors.append(jnp.sum(masked * alphas[which][:, 1:2], 0))
        grad_alpha = jnp.stack(
            [jnp.sum(masked * normed_two, -1), jnp.sum(masked * const_vectors[which], -1)], -1
        )
        grad_alpha_parts.append(
            alphas[which] * (grad_alpha - jnp.sum(alphas[which] * grad_alpha, -1, keepdims=True))
        )
        grad_normed_two = grad_normed_two + masked * alphas[which][:, 0:1]
    grad_probs = jnp.sum(pick_table * grad_pick[..., None], 1)
    grad_main = gate_probs * (grad_probs - jnp.sum(gate_probs * grad_probs, -1, keepdims=True))
    grad_logits = jnp.concatenate([grad_main] + grad_alpha_parts, -1)
    grad_normed_two = grad_normed_two + jnp.einsum(
        "tc,dc->td", grad_logits, router_b.astype(FLOAT), precision=HIGH
    )
    grad_attn_part, grad_gain_ffn = rms_backward(
        after_attn, factor_two, norm_gains[1], grad_normed_two
    )
    grad_after_attn = grad_ffn + grad_attn_part
    columns = grad_logits.shape[1]
    misc = jnp.concatenate(
        [
            grad_logits.reshape(-1),
            split_float(loss_part[None]).astype(FLOAT),
        ]
    )
    grad_attn_b = spread(grad_after_attn.astype(BFLOAT), BOTH).reshape(queries, width)

    cut_grad = grad_in.reshape(local_experts, shard_count, slice_rows, 2 * units)
    cut_grad = cut_grad.transpose(1, 0, 2, 3).astype(BFLOAT)
    cut_grad, grad_attn_b = lax.optimization_barrier((cut_grad, grad_attn_b))
    sum_expert_in = swap(cut_grad, "dp")

    order = np.arange(width).reshape(blocks, QUAD, 2, HALF).swapaxes(1, 2).reshape(-1)
    fold = jnp.asarray((np.arange(width)[:, None] == order[None, :]).astype(ml_dtypes.bfloat16))
    all_normed_one = rms_forward(all_start, norm_gains[0])[0].astype(BFLOAT)
    chunk = min(queries, LANES)
    chunks = queries // chunk

    sum_attend_out = contract(
        lax.dynamic_slice_in_dim(all_mixed_b, my_shard * slice_rows, slice_rows, 1),
        grad_attn_b,
        TN,
    )
    side = QUAD * chunk
    quarter = 2 * width // owners
    grad_embed, grad_kv, grad_query, grad_gain, met, embed_square = pl.pallas_call(
        functools.partial(backward_kernel, kept, chunks, blocks, token_bits, experts),
        in_specs=[SMEM_SPEC] * 4
        + [VMEM_SPEC]
        + ([VMEM_SPEC] + [any_spec] * 2 if kept else [any_spec] + [VMEM_SPEC] * 2)
        + [VMEM_SPEC] * 9,
        out_specs=(any_spec,) + (VMEM_SPEC,) * 5,
        scratch_shapes=[
            pltpu.VMEM((1, width), FLOAT),
            pltpu.VMEM((2, tile, width), BFLOAT),
            pltpu.VMEM((width, 2 * width), BFLOAT),
            pltpu.VMEM((chunks, blocks, side, 2 * LANES), BFLOAT),
            pltpu.VMEM((chunks, blocks, 2 * LANES, side), BFLOAT),
            pltpu.VMEM((chunks, blocks, side, 2 * LANES), BFLOAT),
            pltpu.VMEM((chunks, blocks, 2 * LANES, side), BFLOAT),
            pltpu.VMEM((chunks, blocks, 1, side), FLOAT),
            pltpu.VMEM((chunks, blocks, 1, side), FLOAT),
            pltpu.VMEM((tile, side), BFLOAT),
            pltpu.VMEM((chunks, blocks, 2 * LANES, chunk), FLOAT),
            pltpu.VMEM((tile, 2 * width), BFLOAT),
            pltpu.VMEM((8 if kept else tile, width), FLOAT),
            pltpu.VMEM((tile, width), FLOAT),
            pltpu.VMEM((tile, width), FLOAT),
            pltpu.SemaphoreType.DMA((2,)),
        ]
        + (
            [
                pltpu.VMEM((2, tile, width), BFLOAT),
                pltpu.VMEM((2, tile, 2 * LANES), FLOAT),
                pltpu.SemaphoreType.DMA((2, 2)),
            ]
            if kept
            else [pltpu.VMEM((1, tile), jnp.int32), pltpu.SemaphoreType.DMA]
        ),
        out_shape=(
            jax.ShapeDtypeStruct((everything, width), BFLOAT),
            jax.ShapeDtypeStruct((width, quarter), FLOAT),
            jax.ShapeDtypeStruct((chunks, blocks, 2, HALF, chunk), FLOAT),
            jax.ShapeDtypeStruct((1, width), FLOAT),
            jax.ShapeDtypeStruct((queries, width), FLOAT),
            jax.ShapeDtypeStruct((8, LANES), FLOAT),
        ),
        compiler_params=pltpu.CompilerParams(vmem_limit_bytes=VMEM_LIMIT),
        cost_estimate=pl.CostEstimate(
            flops=60_000_000_000, bytes_accessed=60_000_000, transcendentals=6_000_000
        ),
    )(
        tile_count,
        my_owner.astype(jnp.int32).reshape(1),
        first_row,
        last_row,
        scored_local[:, None],
        info,
        saved[0] if kept else embed_b,
        saved[1] if kept else table,
        gain_row,
        both_w,
        fold,
        all_told.reshape(chunks, chunk, -1),
        grad_attn_b.reshape(chunks, chunk, width),
        cos_wide.reshape(chunks, chunk, LANES),
        sin_wide.reshape(chunks, chunk, LANES),
        own_code.reshape(chunks, 1, chunk),
        base_code.reshape(chunks, 1, chunk),
    )

    pieces = grad_query.transpose(0, 4, 1, 2, 3).reshape(groups, NCONT, part)
    met = jnp.where(scored_here[:, None], met, 0.0)
    met = lax.dynamic_slice_in_dim(met, my_owner * part, part, 1).reshape(groups, NCONT, part)
    thin = width // groups
    sent = jnp.concatenate(
        [
            grad_kv.astype(BFLOAT).reshape(groups, thin, quarter),
            split_float(pieces),
            split_float(met),
        ],
        1,
    )
    sent, sum_expert_in = lax.optimization_barrier((sent, sum_expert_in))
    def by_rows(low, high, late):
        place = slice(low, high)
        spec = pl.BlockSpec((block_rows, width), lambda i: (i, 0))
        return pl.pallas_call(
            functools.partial(gather_kernel, token_bits),
            grid=(high - low,),
            out_shape=jax.ShapeDtypeStruct(((high - low) * block_rows, width), BFLOAT),
            in_specs=[SMEM_SPEC] * 6 + [VMEM_SPEC] + [any_spec] * 2,
            out_specs=spec,
            scratch_shapes=[
                pltpu.VMEM((block_rows, width), FLOAT),
                pltpu.VMEM((2, tile, width), BFLOAT),
                pltpu.SemaphoreType.DMA((2,)),
            ],
            compiler_params=pltpu.CompilerParams(vmem_limit_bytes=VMEM_LIMIT),
            cost_estimate=pl.CostEstimate(
                flops=10_000_000_000, bytes_accessed=12_000_000, transcendentals=0
            ),
        )(
            jnp.full((1,), low * block_rows, jnp.int32),
            begins[place],
            ends[place],
            orders[place],
            first_row,
            last_row,
            info,
            grad_embed,
            late,
        )

    grad_low = by_rows(0, low_blocks, sent)
    got = swap(sent, BOTH)
    leader = (my_owner == 0).astype(FLOAT)
    rest_square = (
        jnp.sum(grad_in * grad_in)
        + jnp.sum(grad_expert_out * grad_expert_out)
        + leader * jnp.sum(sum_attend_out * sum_attend_out)
    )
    misc_lane = misc.shape[0]
    misc = jnp.pad(misc, (0, width - misc_lane))
    blank = jnp.zeros((width,), FLOAT)
    rows = [blank, grad_gain_ffn, grad_gain_final] + grad_vectors + [grad_head, misc, blank]
    told, sum_kv = pl.pallas_call(
        functools.partial(owner_kernel, owners, thin, misc_lane),
        out_shape=(
            jax.ShapeDtypeStruct((groups, 16, width), BFLOAT),
            jax.ShapeDtypeStruct((thin, 2 * width), FLOAT),
        ),
        in_specs=[SMEM_SPEC] * 2 + [VMEM_SPEC] * 10 + [any_spec],
        out_specs=(VMEM_SPEC,) * 2,
        compiler_params=pltpu.CompilerParams(vmem_limit_bytes=VMEM_LIMIT),
    )(
        rest_square.reshape(1),
        leader.reshape(1),
        got,
        query_w,
        start_x,
        grad_after_attn,
        own_cos,
        own_sin,
        gain_row,
        grad_gain,
        embed_square,
        jnp.stack(rows),
        grad_low,
    )
    grad_high = by_rows(low_blocks, row_blocks, told)
    told = spread_made(told, BOTH).reshape(16 * groups, width)
    told, sum_kv = lax.optimization_barrier((told, sum_kv))
    all_kv = spread(sum_kv.astype(BFLOAT), "expert").reshape(slice_rows, 2 * width)
    rates = learn_rates()
    normed_slice = lax.dynamic_slice_in_dim(
        all_normed_one, my_shard * slice_rows, slice_rows, 1
    )
    small_states = (
        router.T,
        router_first.T,
        router_second.T,
        norm_gains,
        norm_gains_first,
        norm_gains_second,
        const_vectors,
        const_vectors_first,
        const_vectors_second,
        *head_states,
    )
    all_extra_b, sum_query_w, scalars, *made_small = pl.pallas_call(
        functools.partial(finish_kernel, rates[5:], DECAYS[5:], columns),
        out_shape=(
            jax.ShapeDtypeStruct((queries, width), BFLOAT),
            jax.ShapeDtypeStruct((slice_rows, width), FLOAT),
            jax.ShapeDtypeStruct((8, LANES), FLOAT),
        )
        + tuple(jax.ShapeDtypeStruct(array.shape, FLOAT) for array in small_states),
        in_specs=[VMEM_SPEC] * 18,
        out_specs=(VMEM_SPEC,) * 15,
        compiler_params=pltpu.CompilerParams(vmem_limit_bytes=VMEM_LIMIT),
    )(
        told,
        scored_ids.reshape(-1, 1),
        scored_ids.reshape(1, -1),
        contract(all_normed_one, all_normed_one, NT),
        all_normed_b,
        normed_slice,
        *small_states,
    )
    loss_total, norm_total, factor = scalars[0, 0], scalars[0, 1], scalars[0, 2]
    key_grad = contract(all_kv[:, :width], fold, NT)
    sum_attend_in = jnp.concatenate(
        [sum_query_w, key_grad, all_kv[:, width:].astype(FLOAT)], 1
    )

    row_spec = pl.BlockSpec((block_rows, width), lambda i: (i, 0))
    low_spec = pl.BlockSpec((block_rows, width), lambda i: (jnp.minimum(i, low_blocks - 1), 0))
    high_spec = pl.BlockSpec((block_rows, width), lambda i: (jnp.maximum(i - low_blocks, 0), 0))
    made_embedding = pl.pallas_call(
        functools.partial(adam_kernel, rates[0], DECAYS[0], low_blocks),
        grid=(shard_rows // block_rows,),
        out_shape=(jax.ShapeDtypeStruct((shard_rows, width), FLOAT),) * 3,
        in_specs=[SMEM_SPEC] + [VMEM_SPEC] * 2 + [low_spec, high_spec] + [row_spec] * 3,
        out_specs=(row_spec,) * 3,
        compiler_params=pltpu.CompilerParams(vmem_limit_bytes=VMEM_LIMIT),
        cost_estimate=pl.CostEstimate(
            flops=4_000_000_000, bytes_accessed=176_000_000, transcendentals=12_000_000
        ),
    )(
        factor.reshape(1),
        jnp.where(scored_here, scored_local, -1)[None],
        all_extra_b,
        grad_low,
        grad_high,
        embedding,
        embedding_first,
        embedding_second,
    )
    cut_rows = 32
    cells = pl.BlockSpec((1, cut_rows, hidden_units), lambda l, h, r: (l, r, h))
    cut_spec = pl.BlockSpec((shard_count, 1, cut_rows, units), lambda l, h, r: (0, l, r, h))
    if units % LANES == 0 and slice_rows % cut_rows == 0:
        made_in = pl.pallas_call(
            functools.partial(matrix_adam_kernel, rates[3], DECAYS[3]),
            grid=(local_experts, 2, slice_rows // cut_rows),
            out_shape=(jax.ShapeDtypeStruct(expert_in.shape, FLOAT),) * 3,
            in_specs=[SMEM_SPEC] + [cells] * 3 + [cut_spec],
            out_specs=(cells,) * 3,
            compiler_params=pltpu.CompilerParams(vmem_limit_bytes=SMALL_LIMIT),
            cost_estimate=pl.CostEstimate(
                flops=100_000_000, bytes_accessed=20_000_000, transcendentals=1_600_000
            ),
        )(factor.reshape(1), expert_in, expert_in_first, expert_in_second, sum_expert_in)
    else:
        whole_in = sum_expert_in.astype(FLOAT).reshape(
            shard_count, local_experts, slice_rows, 2, units
        )
        whole_in = whole_in.transpose(1, 2, 3, 0, 4).reshape(expert_in.shape)
        made_in = adam_update(
            expert_in, expert_in_first, expert_in_second, whole_in * factor, rates[3], DECAYS[3]
        )
    made = list(made_embedding)
    states = (
        (attend_in, attend_in_first, attend_in_second, sum_attend_in),
        (attend_out, attend_out_first, attend_out_second, sum_attend_out),
        None,
        (expert_out, expert_out_first, expert_out_second, grad_expert_out),
    )
    for which, state in enumerate(states):
        if state is None:
            made += made_in
            continue
        *state, grad = state
        made += adam_update(*state, grad * factor, rates[which + 1], DECAYS[which + 1])
    made += [array.T for array in made_small[:3]] + made_small[3:9]
    made += [array.reshape(-1) for array in made_small[9:]]
    return tuple(made) + (loss_total, norm_total)


def solution(mesh):
    pair = P(BOTH, None)
    triple = P(BOTH, None, None)
    rows = P("dp", None)
    cells = P("expert", "dp", None)
    placed = (pair, triple, pair, triple) + (rows,) * 9 + (cells,) * 6 + (P(),) * 12
    return jax.shard_map(
        shards,
        mesh=mesh,
        in_specs=placed,
        out_specs=(rows,) * 9 + (cells,) * 6 + (P(),) * 14,
        check_vma=False,
    )
```

```python
import functools

import jax
import jax.numpy as jnp
import ml_dtypes
import numpy as np
from jax import lax
from jax.experimental import pallas as pl
from jax.experimental.pallas import tpu as pltpu
from jax.sharding import PartitionSpec as P

D = 768
HEAD = 64
FF = 2048
PROMPT = 512
CLEN = 128
NCONT = 4
NPAIR = 4
ADAM_STEP = 5
TOK = PROMPT + NCONT * CLEN
SPAN = PROMPT + CLEN
HALF = HEAD // 2
QUAD = 4
TILE = 512
TILE_SMALL = 256
ROWS = 256
WINDOW = 1536
KEEP = 65536
TOK_BITS = TOK.bit_length() - 1
CLEN_BITS = CLEN.bit_length() - 1
HALF_BITS = HALF.bit_length() - 1
LANES = 128

HIGH = lax.Precision.HIGHEST
EPS_NORM = 1e-05
THRESH = 0.05
BETA_ONE = 0.5
BETA_TWO = 0.5
ADAM_EPS = 1e-08
ROPE_BASE = 10000.0
DECAYS = (0.1, 0.1, 0.1, 0.1, 0.1, 0.1, 0.0, 0.0, 0.0)
BFLOAT = jnp.bfloat16
FLOAT = jnp.float32
BOTH = ("dp", "expert")
SCALE = HEAD ** (-0.5)
FAR = -1e30
VMEM_LIMIT = 127 * 512 * 1024
SMALL_LIMIT = 16 * 1024 * 1024
FORWARD_LIMIT = 40 * 1024 * 1024


VMEM_SPEC = pl.BlockSpec(memory_space=pltpu.VMEM)
SMEM_SPEC = pl.BlockSpec(memory_space=pltpu.SMEM)


def learn_rates():
    return (
        1.0,
        D ** (-0.5),
        (D * 16 // PROMPT) ** (-0.5),
        D ** (-0.5),
        (FF // 64) ** (-0.5),
        (2 * D) ** (-0.5),
        0.5,
        1.0,
        D ** (-0.5),
    )


def rms_forward(values, gain):
    factor = lax.rsqrt(jnp.mean(values * values, -1, keepdims=True) + EPS_NORM)
    return (values * factor * gain, factor)


def rms_backward(values, factor, gain, upstream):
    weighted = upstream * gain
    inner = jnp.mean(weighted * values, -1, keepdims=True)
    return (
        factor * weighted - values * factor * factor * factor * inner,
        jnp.sum(upstream * values * factor, 0),
    )


def adam_update(weight, first, second, grad, rate, decay):
    first = BETA_ONE * first + (1.0 - BETA_ONE) * grad
    second = BETA_TWO * second + (1.0 - BETA_TWO) * grad * grad
    step_dir = (
        first
        / (1.0 - BETA_ONE**ADAM_STEP)
        / (jnp.sqrt(second / (1.0 - BETA_TWO**ADAM_STEP)) + ADAM_EPS)
    )
    return (weight - rate * (step_dir + decay * weight), first, second)


def rope_constants():
    freq = np.float32(ROPE_BASE) ** (-np.arange(HALF, dtype=np.float32) / np.float32(HALF))
    angle = np.arange(SPAN, dtype=np.float32)[:, None] * freq.astype(np.float32)[None, :]
    angle = angle.astype(np.float64)
    return np.cos(angle).astype(np.float32), np.sin(angle).astype(np.float32)


def rope_split():
    parts = []
    for table in rope_constants():
        high = table.astype(ml_dtypes.bfloat16)
        low = (table - high.astype(np.float32)).astype(ml_dtypes.bfloat16)
        parts += [np.tile(high, (1, QUAD)), np.tile(low, (1, QUAD))]
    return np.concatenate(parts, 1)


def spread(array, axes):
    count = lax.axis_size(axes)
    return lax.all_to_all(
        jnp.broadcast_to(array[None], (count,) + array.shape), axes, 0, 0, tiled=True
    )


def spread_made(copies, axes):
    return lax.all_to_all(copies, axes, 0, 0, tiled=True)


def swap(array, axes):
    return lax.all_to_all(array, axes, 0, 0, tiled=True)


def contract(left, right, dims):
    return lax.dot_general(left, right, (dims, ((), ())), preferred_element_type=FLOAT)


NN = ((1,), (0,))
NT = ((1,), (1,))
TN = ((0,), (0,))


def tile_tokens(key_row, token_bits):
    real = key_row >= 0
    local = lax.shift_right_arithmetic(key_row, token_bits)
    place = key_row & (TOK - 1)
    group = lax.shift_right_arithmetic(key_row & ((1 << token_bits) - 1), TOK_BITS)
    late = place - PROMPT
    seg = lax.shift_right_arithmetic(late, CLEN_BITS) + 1
    code = group * 8 + jnp.where(late < 0, 0, seg)
    spot = jnp.where(late < 0, place, PROMPT + (late & (CLEN - 1)))
    return jnp.where(real, local, -1), jnp.where(real, code, -1), spot


def to_column(row):
    return jnp.transpose(jnp.broadcast_to(row.astype(FLOAT), (8, row.shape[1])))[:, 0:1].astype(jnp.int32)


def one_hot(matches):
    return matches.astype(FLOAT).astype(BFLOAT)


def tile_rows(id_col, low, high, embed_ref, start_ref):
    limit = embed_ref.shape[0]
    window = min(WINDOW, limit)
    align = 16
    origin = lax.div(low, align) * align
    lanes = lax.broadcasted_iota(jnp.int32, (id_col.shape[0], window), 1)

    def pick(turn):
        least = origin + turn * window
        base = pl.multiple_of(jnp.minimum(least, limit - window), align)
        wanted = jnp.where(id_col >= least, id_col - base, -1)
        return contract(one_hot(wanted == lanes), embed_ref[pl.ds(base, window), :], NN)

    start_ref[...] = pick(0)

    def more(turn, carry):
        start_ref[...] += pick(turn)
        return carry

    lax.fori_loop(1, lax.div(high - origin, window) + 1, more, 0)
    return start_ref[...]


def tile_rope(pos_col, table_ref):
    spots = lax.broadcasted_iota(jnp.int32, (pos_col.shape[0], SPAN), 1)
    both = contract(one_hot(pos_col == spots), table_ref[...], NN)
    cosine = both[:, :LANES] + both[:, LANES : 2 * LANES]
    sine = both[:, 2 * LANES : 3 * LANES] + both[:, 3 * LANES :]
    return cosine, sine


def forward_kernel(
    token_bits,
    count_ref,
    first_ref,
    last_ref,
    info_ref,
    embed_ref,
    gain_ref,
    weights_ref,
    table_ref,
    query_ref,
    own_ref,
    base_ref,
    scored_ref,
    sent_ref,
    *rest,
):
    kept = len(rest) > 4
    *rest, out_ref, peak_ref, total_ref, start_ref = rest
    tile = info_ref.shape[2]
    if kept:
        *rest, embed_buf, whole_ref, embed_sems = rest
        slots, piece = embed_buf.shape[:2]
        pieces = whole_ref.shape[0] // piece

        def fetch(part):
            slot = lax.rem(part, slots)
            place = pl.ds(pl.multiple_of(part * piece, piece), piece)
            return pltpu.make_async_copy(
                embed_ref.at[place], embed_buf.at[slot], embed_sems.at[slot]
            )

        for part in range(min(slots, pieces)):
            fetch(part).start()

        def take(part, carry):
            fetch(part).wait()
            place = pl.ds(pl.multiple_of(part * piece, piece), piece)
            whole_ref[place, :] = embed_buf[lax.rem(part, slots)].astype(BFLOAT)

            @pl.when(part + slots < pieces)
            def _():
                fetch(part + slots).start()

            return carry

    else:
        whole_ref = embed_ref
    wide = 2 * LANES
    out_ref[...] = jnp.zeros_like(out_ref)
    peak_ref[...] = jnp.full_like(peak_ref, FAR)
    total_ref[...] = jnp.zeros_like(total_ref)

    def saves(step):
        start_out, rope_out, start_buf, rope_buf, sems = rest
        slot = lax.rem(step, 2)
        place = pl.ds(pl.multiple_of(step * tile, tile), tile)
        return (
            pltpu.make_async_copy(start_buf.at[slot], start_out.at[place], sems.at[0, slot]),
            pltpu.make_async_copy(rope_buf.at[slot], rope_out.at[place], sems.at[1, slot]),
        )

    def body(step, carry):
        id_row, code_row, pos_row = tile_tokens(info_ref[step], token_bits)
        id_col, pos_col = to_column(id_row), to_column(pos_row)
        low, high = first_ref[step], last_ref[step]
        taken = carry
        if kept:
            limit = whole_ref.shape[0]
            needed = jnp.minimum(limit, high + min(WINDOW, limit))
            wanted = lax.div(needed + piece - 1, piece)
            lax.fori_loop(taken, wanted, take, 0)
            taken = jnp.maximum(taken, wanted)
        start = tile_rows(id_col, low, high, whole_ref, start_ref)
        factor = lax.rsqrt(jnp.mean(start * start, -1, keepdims=True) + EPS_NORM)
        normed = (start * factor * gain_ref[...]).astype(BFLOAT)
        cosine, sine = tile_rope(pos_col, table_ref)
        if kept:

            @pl.when(step >= 2)
            def _():
                for copy in saves(step - 2):
                    copy.wait()

            slot = lax.rem(step, 2)
            rest[2][slot] = start.astype(BFLOAT)
            rest[3][slot] = jnp.concatenate([cosine, sine], 1)
            for copy in saves(step):
                copy.start()
        raw = contract(normed, weights_ref[:, wide : 2 * wide], NN)
        former, latter = raw[:, :LANES], raw[:, LANES:]
        keys = jnp.concatenate(
            [former * cosine - latter * sine, latter * cosine + former * sine], 1
        ).astype(BFLOAT)
        values = contract(normed, weights_ref[:, 2 * wide :], NN).astype(BFLOAT)
        scores = contract(query_ref[...], keys, NT)
        seen = (own_ref[...] == code_row) | (base_ref[...] == code_row)
        scores = jnp.where(seen, scores, FAR)
        peak = peak_ref[...]
        newer = jnp.maximum(peak, jnp.max(scores, 1, keepdims=True))
        expos = jnp.where(seen, jnp.exp(scores - newer[:, 0:1]), 0.0)
        shrink = jnp.exp(peak - newer)
        peak_ref[...] = newer
        total_ref[...] = total_ref[...] * shrink + jnp.sum(expos, 1, keepdims=True)
        out_ref[...] = out_ref[...] * shrink[:, 0:1] + contract(
            expos.astype(BFLOAT), values, NN
        )
        return taken

    count = count_ref[0]
    taken = lax.fori_loop(0, count, body, jnp.int32(0))
    if kept:
        lax.fori_loop(taken, pieces, take, 0)
    if kept:
        for back in (2, 1):

            @pl.when(count >= back)
            def _():
                for copy in saves(count - back):
                    copy.wait()

    queries, part = scored_ref.shape
    per_owner = part // HEAD
    cuts = [slice(head * queries, (head + 1) * queries) for head in range(per_owner)]
    mixed = [out_ref[cuts[h], h * HEAD : (h + 1) * HEAD] for h in range(per_owner)]
    fine = [peak_ref[cuts[h], 0:1] for h in range(per_owner)]
    fine += [total_ref[cuts[h], 0:1] for h in range(per_owner)]
    coarse = [value.astype(BFLOAT).astype(FLOAT) for value in fine]
    rest_of = [value - high for value, high in zip(fine, coarse)]
    filler = jnp.zeros((queries, sent_ref.shape[1] - 2 * part - 4 * per_owner), FLOAT)
    sent_ref[...] = jnp.concatenate(
        mixed + [scored_ref[...]] + coarse + rest_of + [filler], 1
    ).astype(BFLOAT)


def backward_kernel(
    kept,
    chunks,
    blocks,
    token_bits,
    fine_gap,
    steps_ref,
    owner_ref,
    first_ref,
    last_ref,
    scored_ref,
    info_ref,
    start_in_ref,
    rope_in_ref,
    gain_ref,
    both_ref,
    fold_ref,
    told_ref,
    upper_in_ref,
    cosine_ref,
    sine_ref,
    own_ref,
    base_ref,
    grad_embed_ref,
    grad_w_ref,
    grad_turned_ref,
    grad_gain_ref,
    met_ref,
    square_ref,
    carry_ref,
    row_buf,
    both_w_ref,
    query_ref,
    query_t_ref,
    upper_ref,
    upper_t_ref,
    level_ref,
    inner_ref,
    lowered_ref,
    grad_query_ref,
    grad_kv_ref,
    start_ref,
    grad_keys_ref,
    grad_values_ref,
    copy_sem,
    *loaded,
):
    wide = 2 * LANES
    tile = info_ref.shape[2]
    count = steps_ref[0]

    def loads(step):
        start_buf, rope_buf, sems = loaded
        slot = lax.rem(step, 2)
        place = pl.ds(pl.multiple_of(step * tile, tile), tile)
        return (
            pltpu.make_async_copy(start_in_ref.at[place], start_buf.at[slot], sems.at[0, slot]),
            pltpu.make_async_copy(rope_in_ref.at[place], rope_buf.at[slot], sems.at[1, slot]),
        )

    if kept:

        @pl.when(count > 0)
        def _():
            for copy in loads(0):
                copy.start()

    def row_copy(step):
        slot = lax.rem(step, 2)
        place = pl.ds(pl.multiple_of(step * tile, tile), tile)
        return pltpu.make_async_copy(
            row_buf.at[slot], grad_embed_ref.at[place], copy_sem.at[slot]
        )

    met_ref[...] = jnp.zeros_like(met_ref)
    carry_ref[...] = jnp.zeros_like(carry_ref)
    grad_w_ref[...] = jnp.zeros_like(grad_w_ref)
    grad_query_ref[...] = jnp.zeros_like(grad_query_ref)
    grad_gain_ref[...] = jnp.zeros_like(grad_gain_ref)
    owner = owner_ref[0]
    mine = pl.ds(pl.multiple_of(owner * LANES, LANES), LANES)
    part = grad_w_ref.shape[1]
    mine_kv = pl.ds(pl.multiple_of(owner * part, LANES), part)
    lane_head = lax.broadcasted_iota(jnp.int32, (LANES, wide), 1)
    row_head = lax.broadcasted_iota(jnp.int32, (wide, LANES), 0)

    width = gain_ref.shape[1]
    heads = blocks * QUAD
    query_w = contract(both_ref[:, :width], fold_ref[...], NN).astype(BFLOAT)
    both_w_ref[:, :width] = contract(both_ref[:, width : 2 * width], fold_ref[...], NN).astype(
        BFLOAT
    )
    both_w_ref[:, width:] = both_ref[:, 2 * width : 3 * width]

    def unfold(chunk, carry):
        begin = told_ref[chunk, :, width : 2 * width].astype(FLOAT)
        scale = lax.rsqrt(jnp.mean(begin * begin, -1, keepdims=True) + EPS_NORM)
        raw = contract((begin * scale * gain_ref[...]).astype(BFLOAT), query_w, NN)
        cos_one, sin_one = cosine_ref[chunk] * SCALE, sine_ref[chunk] * SCALE
        fine = told_ref[chunk, :, 3 * width :].astype(FLOAT)
        level = jnp.transpose(fine)
        upper_all = contract(upper_in_ref[chunk], both_ref[:, 3 * width :], NT)
        upper_all = upper_all.astype(BFLOAT).astype(FLOAT)
        joint_all = upper_all * told_ref[chunk, :, 2 * width : 3 * width].astype(FLOAT)
        for block in range(blocks):
            place = slice(block * wide, (block + 1) * wide)
            former = raw[:, block * wide : block * wide + LANES]
            latter = raw[:, block * wide + LANES : (block + 1) * wide]
            query = jnp.concatenate(
                [former * cos_one - latter * sin_one, latter * cos_one + former * sin_one], 1
            )
            upper = upper_all[:, place]
            query_t, upper_t = jnp.transpose(query), jnp.transpose(upper)
            joint = jnp.transpose(joint_all[:, place])
            for head in range(QUAD):
                low, high = head * HEAD, (head + 1) * HEAD
                cut = slice(head * LANES, (head + 1) * LANES)
                kept_lanes = (lane_head >= low) & (lane_head < high)
                kept_rows = (row_head >= low) & (row_head < high)
                upper_ref[chunk, block, cut, :] = jnp.where(kept_lanes, upper, 0.0).astype(BFLOAT)
                upper_t_ref[chunk, block, :, cut] = jnp.where(kept_rows, upper_t, 0.0).astype(
                    BFLOAT
                )
                inner_ref[chunk, block, :, cut] = jnp.sum(joint[low:high], 0, keepdims=True)
                row = block * QUAD + head
                fine_row = heads + fine_gap + row
                level_ref[chunk, block, :, cut] = (
                    level[row : row + 1] + level[fine_row : fine_row + 1]
                )
                kept_lanes = lax.shift_right_arithmetic(lane_head & (LANES - 1), HALF_BITS) == head
                kept_rows = lax.shift_right_arithmetic(row_head & (LANES - 1), HALF_BITS) == head
                query_ref[chunk, block, cut, :] = jnp.where(kept_lanes, query, 0.0).astype(BFLOAT)
                query_t_ref[chunk, block, :, cut] = jnp.where(kept_rows, query_t, 0.0).astype(
                    BFLOAT
                )
        return carry

    lax.fori_loop(0, chunks, unfold, 0)

    def body(step, square):
        return square + tile_step(step)

    def tile_step(step):
        if kept:
            key_row = info_ref[step]
        else:
            slab_buf, slab_sem = loaded
            copy = pltpu.make_async_copy(info_ref.at[step], slab_buf, slab_sem)
            copy.start()
            copy.wait()
            key_row = slab_buf[...]
        id_row, code_row, pos_row = tile_tokens(key_row, token_bits)
        code_col = to_column(code_row)
        if kept:

            @pl.when(step + 1 < count)
            def _():
                for copy in loads(step + 1):
                    copy.start()

            for copy in loads(step):
                copy.wait()
            slot = lax.rem(step, 2)
            start = loaded[0][slot].astype(FLOAT)
            cosine, sine = loaded[1][slot, :, :LANES], loaded[1][slot, :, LANES:]
        else:
            id_col, pos_col = to_column(id_row), to_column(pos_row)
            start = tile_rows(id_col, first_ref[step], last_ref[step], start_in_ref, start_ref)
            cosine, sine = tile_rope(pos_col, rope_in_ref)
        factor = lax.rsqrt(jnp.mean(start * start, -1, keepdims=True) + EPS_NORM)
        normed = (start * factor * gain_ref[...]).astype(BFLOAT)
        raw = contract(normed, both_w_ref[:, :width], NN)
        values = contract(normed, both_w_ref[:, width:], NN).astype(BFLOAT)
        keys = []
        for block in range(blocks):
            former = raw[:, block * wide : block * wide + LANES]
            latter = raw[:, block * wide + LANES : (block + 1) * wide]
            keys.append(
                jnp.concatenate(
                    [former * cosine - latter * sine, latter * cosine + former * sine], 1
                ).astype(BFLOAT)
            )
        if chunks > 1:
            grad_keys_ref[...] = jnp.zeros_like(grad_keys_ref)
            grad_values_ref[...] = jnp.zeros_like(grad_values_ref)

        def attend(chunk):
            seen = (code_col == own_ref[chunk]) | (code_col == base_ref[chunk])
            hidden = jnp.where(seen, 0.0, FAR)
            hidden = jnp.concatenate([hidden] * QUAD, 1)
            for block in range(blocks):
                place = pl.ds(block * wide, wide)
                scores = contract(keys[block], query_t_ref[chunk, block], NN)
                weights = jnp.exp(scores - level_ref[chunk, block] + hidden)
                slopes = contract(
                    values[:, block * wide : (block + 1) * wide], upper_t_ref[chunk, block], NN
                )
                lowered = (weights * (slopes - inner_ref[chunk, block])).astype(BFLOAT)
                lowered_ref[...] = lowered
                grad_query_ref[chunk, block] += contract(keys[block], lowered_ref[:, mine], TN)
                grad_k = contract(lowered, query_ref[chunk, block], NN)
                grad_v = contract(weights.astype(BFLOAT), upper_ref[chunk, block], NN)
                if chunks > 1:
                    grad_keys_ref[:, place] += grad_k
                    grad_values_ref[:, place] += grad_v
                else:
                    grad_keys_ref[:, place] = grad_k
                    grad_values_ref[:, place] = grad_v

        if chunks > 1:
            lax.fori_loop(0, chunks, lambda chunk, c: (attend(chunk), c)[1], 0)
        else:
            attend(0)
        pieces = []
        for block in range(blocks):
            former = grad_keys_ref[:, pl.ds(block * wide, LANES)]
            latter = grad_keys_ref[:, pl.ds(block * wide + LANES, LANES)]
            pieces.append((former * cosine + latter * sine).astype(BFLOAT))
            pieces.append((latter * cosine - former * sine).astype(BFLOAT))
        grad_kv = jnp.concatenate(pieces + [grad_values_ref[...].astype(BFLOAT)], 1)
        grad_kv_ref[...] = grad_kv
        grad_w_ref[...] += contract(normed, grad_kv_ref[:, mine_kv], TN)
        grad_normed = contract(grad_kv, both_w_ref[...], NT)
        scaled = start * factor
        grad_gain_ref[...] += jnp.sum(grad_normed * scaled, 0, keepdims=True)
        weighted = grad_normed * gain_ref[...]
        inner = jnp.mean(weighted * scaled, -1, keepdims=True)
        grad_start = (factor * (weighted - scaled * inner)).astype(BFLOAT)

        @pl.when(step >= 2)
        def _():
            row_copy(step - 2).wait()

        row_buf[lax.rem(step, 2)] = grad_start
        row_copy(step).start()
        met_ref[...] += contract(one_hot(scored_ref[...] == id_row), grad_start, NN)
        before = jnp.where(step > 0, last_ref[jnp.maximum(step - 1, 0)], -2)
        final = last_ref[step]
        line = lax.broadcasted_iota(jnp.int32, (8, tile), 0)
        edges = ((line == 0) & (id_row == before)) | ((line == 1) & (id_row == final))
        edges = contract(one_hot(edges), grad_start, NN)
        held = carry_ref[...]
        products = contract(grad_start, grad_start, NT)
        square = jnp.sum(jnp.where(to_column(id_row) == id_row, products, 0.0))
        square += 2.0 * jnp.sum(held * edges[0:1])
        carry_ref[...] = edges[1:2] + jnp.where(final == before, held, 0.0)
        return square

    square = lax.fori_loop(0, count, body, jnp.float32(0.0))
    line = lax.broadcasted_iota(jnp.int32, square_ref.shape, 0)
    lane = lax.broadcasted_iota(jnp.int32, square_ref.shape, 1)
    square_ref[...] = jnp.where((line == 0) & (lane == 0), square, 0.0)
    for back in (2, 1):

        @pl.when(count >= back)
        def _():
            row_copy(count - back).wait()

    for half in range(2):
        place = pl.ds(pl.multiple_of(half * LANES + owner * HALF, HALF), HALF)
        grad_turned_ref[:, :, half] = grad_query_ref[:, :, place, :] * SCALE


def owner_kernel(
    owners,
    thin,
    misc_lane,
    rest_ref,
    leader_ref,
    got_ref,
    query_w_ref,
    start_ref,
    after_ref,
    cosine_ref,
    sine_ref,
    gain_ref,
    gain_part_ref,
    square_ref,
    rows_ref,
    late_ref,
    told_ref,
    kv_ref,
):
    groups, _, quarter = got_ref.shape
    part = quarter // 2
    per_owner = part // HEAD
    cosine, sine = cosine_ref[...], sine_ref[...]
    square, turned, met = 0.0, {}, []
    for owner in range(owners):

        def add(shard, total):
            return total + got_ref[shard * owners + owner].astype(FLOAT)

        total = lax.fori_loop(
            0, groups // owners, add, jnp.zeros((thin + 2 * NCONT, quarter), FLOAT)
        )
        rows = total[:thin]
        kv_ref[:, owner * quarter : (owner + 1) * quarter] = rows
        square += jnp.sum(rows * rows)
        near = total[thin : thin + NCONT]
        near = near[:, :part] + near[:, part:]
        for slot in range(per_owner):
            former = near[:, slot * HEAD : slot * HEAD + HALF]
            latter = near[:, slot * HEAD + HALF : (slot + 1) * HEAD]
            turned[slot * owners + owner] = [
                former * cosine + latter * sine,
                latter * cosine - former * sine,
            ]
        far = total[thin + NCONT :]
        met.append(far[:, :part] + far[:, part:])
    met = jnp.concatenate(met, 1)
    grad_query = jnp.concatenate(sum([turned[head] for head in range(len(turned))], []), 1)
    grad_query = grad_query.astype(BFLOAT)
    upstream = contract(grad_query, query_w_ref[...], NT)
    start = start_ref[...]
    factor = lax.rsqrt(jnp.mean(start * start, -1, keepdims=True) + EPS_NORM)
    scaled = start * factor
    weighted = upstream * gain_ref[...]
    inner = jnp.mean(weighted * scaled, -1, keepdims=True)
    extra = after_ref[...] + factor * (weighted - scaled * inner)
    extra = extra.astype(BFLOAT).astype(FLOAT)
    gain = jnp.sum(upstream * scaled, 0, keepdims=True) + gain_part_ref[...] * (1.0 / owners)
    square += rest_ref[0] + 2.0 * jnp.sum(met * extra)
    square += leader_ref[0] * jnp.sum(square_ref[...])
    rows = rows_ref[...]
    line = lax.broadcasted_iota(jnp.int32, rows.shape, 0)
    lane = lax.broadcasted_iota(jnp.int32, rows.shape, 1)
    whole = jnp.full(rows.shape, square, FLOAT)
    high = whole.astype(BFLOAT).astype(FLOAT)
    rows = jnp.where(line == 0, gain, rows)
    rows = jnp.where((line == 6) & (lane == misc_lane), high, rows)
    rows = jnp.where((line == 6) & (lane == misc_lane + 1), whole - high, rows)
    payload = jnp.concatenate([extra, grad_query.astype(FLOAT), rows], 0).astype(BFLOAT)

    def put(group, carry):
        told_ref[group] = payload
        return carry

    lax.fori_loop(0, groups, put, 0)


def finish_kernel(rates, decays, columns, told_ref, id_col_ref, id_row_ref, gram_ref, *refs):
    normed_ref, slice_ref, *refs = refs
    sources, refs = refs[:12], refs[12:]
    extra_ref, query_ref, scalar_ref, *made_refs = refs
    count = extra_ref.shape[0]
    chunk = min(count, LANES)
    span = 16 * chunk // NCONT
    row = lax.broadcasted_iota(jnp.int32, (chunk, span), 0)
    col = lax.broadcasted_iota(jnp.int32, (chunk, span), 1)
    spot = 16 * lax.shift_right_arithmetic(row, 2)
    place = row & (NCONT - 1)
    line = lax.broadcasted_iota(jnp.int32, (8, span), 0)
    side = lax.broadcasted_iota(jnp.int32, (8, span), 1)
    which = lax.broadcasted_iota(jnp.int32, (chunk, columns), 0) & (NCONT - 1)
    sums, extra, query, logits = 0.0, [], [], []
    for begin in range(0, count, chunk):
        told = told_ref[begin // NCONT * 16 : begin // NCONT * 16 + span, :]
        extra.append(contract(one_hot(col == spot + place), told, NN).astype(BFLOAT))
        query.append(contract(one_hot(col == spot + place + NCONT), told, NN).astype(BFLOAT))
        misc = contract(one_hot(col == spot + 14), told[:, :LANES], NN)
        own = jnp.zeros((chunk, columns), FLOAT)
        for turn in range(NCONT):
            own = jnp.where(which == turn, misc[:, turn * columns : (turn + 1) * columns], own)
        logits.append(own.astype(BFLOAT))
        sums = sums + contract(one_hot((side & 15) == line + 8), told, NN)
    extra, query, logits = (jnp.concatenate(parts, 0) for parts in (extra, query, logits))
    extra_ref[...] = extra
    query_ref[...] = contract(slice_ref[...], query, TN)
    same = id_col_ref[...] == id_row_ref[...]
    square = jnp.sum(jnp.where(same, contract(extra, extra, NT), 0.0))
    square += jnp.sum(gram_ref[...] * contract(query, query, NT))
    grad_router = contract(logits, normed_ref[...], TN)
    gains, vectors, head = sums[0:3], sums[3:5], sums[5:6]
    misc = sums[6:7, NCONT * columns : NCONT * columns + 4]
    loss = jnp.sum(misc[:, 0:2])
    square += jnp.sum(misc[:, 2:4]) + jnp.sum(grad_router * grad_router)
    square += jnp.sum(sums[0:6] * sums[0:6])
    norm = jnp.sqrt(jnp.full((8, LANES), square, FLOAT))
    factor = THRESH / jnp.maximum(norm, THRESH)
    lane = lax.broadcasted_iota(jnp.int32, (8, LANES), 1)
    scalar_ref[...] = jnp.where(lane == 0, loss, jnp.where(lane == 1, norm, factor))
    factor = factor[0:1, 0:1]
    for index, grad in enumerate((grad_router, gains, vectors, head)):
        state = [sources[3 * index + part][...] for part in range(3)]
        made = adam_update(*state, grad * factor, rates[index], decays[index])
        for part in range(3):
            made_refs[3 * index + part][...] = made[part]


def expert_kernel(
    experts,
    owner_ref,
    told_ref,
    gates_ref,
    inner_ref,
    result_ref,
    down_ref,
    in_ref,
    sent_ref,
    grad_result_ref,
    grad_inner_ref,
    upstream_ref,
    back_ref,
):
    count, width = upstream_ref.shape
    local, units = down_ref.shape[0], down_ref.shape[1]

    def gather(pair, carry):
        rows = [told_ref[2 * pair + side].astype(FLOAT) for side in range(2)]
        place = pl.ds(pl.multiple_of(pair * 2 * NCONT, 2 * NCONT), 2 * NCONT)
        upstream_ref[place, :] = jnp.concatenate(rows, 0)
        return carry

    lax.fori_loop(0, count // (2 * NCONT), gather, 0)
    upstream = upstream_ref[...]
    owner = owner_ref[0]
    lane = lax.broadcasted_iota(jnp.int32, (count, LANES), 1)
    tail = jnp.zeros((count, LANES), FLOAT)
    back = 0.0
    for which in range(local):
        result = result_ref[which]
        dots = jnp.sum(upstream * result, -1, keepdims=True)
        high = dots.astype(BFLOAT).astype(FLOAT)
        spot = owner * local + which
        tail = jnp.where(lane == spot, high, tail)
        tail = jnp.where(lane == spot + experts, dots - high, tail)
        grad_result = (gates_ref[:, which : which + 1] * upstream).astype(BFLOAT)
        grad_result_ref[which] = grad_result
        grad_active = contract(grad_result, down_ref[which], NT)
        gate_half, up_half = inner_ref[which, :, :units], inner_ref[which, :, units:]
        sigma = lax.logistic(gate_half)
        grad_gate = grad_active * up_half * sigma * (1.0 + gate_half * (1.0 - sigma))
        grad_up = grad_active * gate_half * sigma
        grad_inner = jnp.concatenate([grad_gate, grad_up], 1).astype(BFLOAT)
        grad_inner_ref[which] = grad_inner
        back += contract(grad_inner, in_ref[which], NT)
    back_ref[...] = jnp.concatenate([back, tail], 1)

    def scatter(pair, carry):
        place = pl.ds(pl.multiple_of(pair * 2 * NCONT, 2 * NCONT), 2 * NCONT)
        rows = back_ref[place, :]
        for side in range(2):
            sent_ref[2 * pair + side] = rows[side * NCONT : (side + 1) * NCONT].astype(BFLOAT)
        return carry

    lax.fori_loop(0, count // (2 * NCONT), scatter, 0)


def pick_kernel(rows_ref, source_ref, picked_ref, copy_sem):
    count = picked_ref.shape[0]

    def fetch(spot, carry):
        pltpu.make_async_copy(
            source_ref.at[pl.ds(rows_ref[spot], 1)], picked_ref.at[pl.ds(spot, 1)], copy_sem
        ).start()
        return carry

    lax.fori_loop(0, count, fetch, 0)
    pltpu.make_async_copy(source_ref.at[pl.ds(0, count)], picked_ref, copy_sem).wait()


def gather_kernel(
    token_bits,
    base_ref,
    begin_ref,
    end_ref,
    order_ref,
    first_row_ref,
    last_row_ref,
    info_ref,
    rows_ref,
    late_ref,
    made_ref,
    grad_ref,
    row_buf,
    sems,
):
    rows = made_ref.shape[0]
    tile = info_ref.shape[2]
    block, blocks = pl.program_id(0), pl.num_programs(0)
    base = base_ref[0] + block * rows
    begin, end = begin_ref[block], end_ref[block]

    def fetch(step, turn):
        slot = lax.rem(turn, 2)
        place = pl.ds(pl.multiple_of(step * tile, tile), tile)
        return pltpu.make_async_copy(rows_ref.at[place], row_buf.at[slot], sems.at[slot])

    @pl.when(block == 0)
    def _():
        fetch(begin, order_ref[block]).start()

    grad_ref[...] = jnp.zeros_like(grad_ref)
    lines = lax.broadcasted_iota(jnp.int32, (ROWS, tile), 0)

    def gather(step, carry):
        turn = order_ref[block] + step - begin
        later = step + 1 < end
        following = jnp.where(later, step + 1, begin_ref[jnp.minimum(block + 1, blocks - 1)])

        @pl.when(later | (block + 1 < blocks))
        def _():
            fetch(following, turn + 1).start()

        fetch(step, turn).wait()
        key_row = info_ref[step]
        id_row = jnp.where(key_row >= 0, lax.shift_right_arithmetic(key_row, token_bits), -1)
        id_row = id_row - base
        slot = lax.rem(turn, 2)

        def put(part, inner):
            place = pl.multiple_of(part * ROWS, ROWS)
            grad_ref[pl.ds(place, ROWS), :] += contract(
                one_hot(id_row == lines + place), row_buf[slot], NN
            )
            return inner

        low = jnp.maximum(first_row_ref[step] - base, 0)
        high = jnp.minimum(last_row_ref[step] - base, rows - 1)
        reach = jnp.where(high >= low, lax.div(jnp.maximum(high, 0), ROWS) + 1, 0)
        lax.fori_loop(lax.div(low, ROWS), reach, put, 0)
        return carry

    lax.fori_loop(begin, end, gather, 0)
    made_ref[...] = grad_ref[...].astype(BFLOAT)


def adam_kernel(
    rate,
    decay,
    low_blocks,
    factor_ref,
    ids_ref,
    extra_ref,
    low_ref,
    high_ref,
    weight_ref,
    first_ref,
    second_ref,
    weight_out,
    first_out,
    second_out,
):
    rows = weight_out.shape[0]
    block = pl.program_id(0)
    spots = lax.broadcasted_iota(jnp.int32, (rows, ids_ref.shape[1]), 0) + block * rows
    extra = contract(one_hot(ids_ref[...] == spots), extra_ref[...], NN)
    chosen = (block < low_blocks).astype(FLOAT)
    grad = low_ref[...].astype(FLOAT) * chosen + high_ref[...].astype(FLOAT) * (1.0 - chosen)
    grad = (grad + extra) * factor_ref[0]
    made = adam_update(weight_ref[...], first_ref[...], second_ref[...], grad, rate, decay)
    weight_out[...], first_out[...], second_out[...] = made


def matrix_adam_kernel(
    rate, decay, factor_ref, weight_ref, first_ref, second_ref, grad_ref, weight_out, first_out, second_out
):
    units = grad_ref.shape[3]
    for source in range(grad_ref.shape[0]):
        place = slice(source * units, (source + 1) * units)
        grad = grad_ref[source, 0].astype(FLOAT) * factor_ref[0]
        made = adam_update(
            weight_ref[0, :, place], first_ref[0, :, place], second_ref[0, :, place], grad, rate, decay
        )
        weight_out[0, :, place], first_out[0, :, place], second_out[0, :, place] = made


def split_float(values):
    high = lax.reduce_precision(values, 8, 7)
    return jnp.concatenate([high, values - high], -1).astype(BFLOAT)


def join_float(parts):
    half = parts.shape[-1] // 2
    parts = parts.astype(FLOAT)
    return parts[..., :half] + parts[..., half:]


def shards(
    token_ids,
    routes,
    last_valid,
    rank_pairs,
    embedding,
    embedding_first,
    embedding_second,
    attend_in,
    attend_in_first,
    attend_in_second,
    attend_out,
    attend_out_first,
    attend_out_second,
    expert_in,
    expert_in_first,
    expert_in_second,
    expert_out,
    expert_out_first,
    expert_out_second,
    router,
    router_first,
    router_second,
    norm_gains,
    norm_gains_first,
    norm_gains_second,
    const_vectors,
    const_vectors_first,
    const_vectors_second,
    score_head,
    score_head_first,
    score_head_second,
):
    shard_count = lax.axis_size("dp")
    owners = lax.axis_size("expert")
    groups = shard_count * owners
    my_shard = lax.axis_index("dp")
    my_owner = lax.axis_index("expert")
    width = embedding.shape[1]
    heads = width // HEAD
    blocks = heads // QUAD
    per_owner = heads // owners
    local_experts = expert_in.shape[0]
    experts = local_experts * owners
    routed = experts + 4
    hidden_units = expert_in.shape[2] // 2
    shard_rows = embedding.shape[0]
    slice_rows = attend_in.shape[0]
    queries = groups * NCONT
    everything = groups * TOK
    tile = TILE if everything <= KEEP else TILE_SMALL
    far_key = jnp.iinfo(jnp.int32).max
    gain_row = norm_gains[0:1]

    packed = jnp.concatenate(
        [token_ids[0], last_valid[0], jnp.zeros(LANES - NCONT, jnp.int32)]
    )
    known = spread(packed, BOTH)

    attend_b = attend_in.astype(BFLOAT)
    into = jnp.arange(3 * 2 * LANES, dtype=jnp.int32)
    which_part, spot = into // (2 * LANES), into % (2 * LANES)
    folded_head, folded_dim = spot % LANES // HALF, spot // LANES * HALF + spot % HALF
    is_value = which_part == 2
    head_slot = jnp.where(is_value, spot // HEAD, folded_head)
    dim = jnp.where(is_value, spot % HEAD, folded_dim)
    origin = which_part * width + (head_slot * owners + my_owner) * HEAD + dim
    origin = jnp.where(head_slot < per_owner, origin, -1)
    select = (jnp.arange(3 * width, dtype=jnp.int32)[:, None] == origin[None, :]).astype(BFLOAT)
    mine_in = jnp.dot(attend_b, select, preferred_element_type=FLOAT).astype(BFLOAT)
    weights_e = lax.all_gather(mine_in, "dp", tiled=True)
    piece = slice_rows // owners
    both_b = jnp.concatenate([attend_b, attend_out.astype(BFLOAT)], 1)
    both_b = lax.dynamic_slice_in_dim(both_b, my_owner * piece, piece, 0)

    units = hidden_units // shard_count
    cut_in = expert_in.astype(BFLOAT).reshape(
        local_experts, slice_rows, 2, shard_count, units
    )
    cut_in = cut_in.transpose(3, 0, 1, 2, 4)
    cut_in = cut_in.reshape(shard_count, local_experts * slice_rows, 2 * units)
    cut_in, known = lax.optimization_barrier((cut_in, known))
    ids, last = known[:, :TOK], known[:, TOK : TOK + NCONT]
    got_in = swap(cut_in, "dp")

    places = jnp.arange(TOK, dtype=jnp.int32)
    offsets = jnp.arange(CLEN, dtype=jnp.int32)
    seen_late = (offsets[None, None, :] <= last[:, :, None]).reshape(groups, NCONT * CLEN)
    seen = jnp.concatenate([jnp.ones((groups, PROMPT), bool), seen_late], 1)
    local = ids - my_shard * shard_rows
    here = seen & (local >= 0) & (local < shard_rows)
    index = jnp.arange(everything, dtype=jnp.int32).reshape(groups, TOK)
    key = jnp.where(here, local * everything + index, far_key)
    ordered = lax.sort(key.reshape(-1))
    tile_count = (jnp.sum(here.astype(jnp.int32)) + tile - 1) // tile
    ordered = jnp.where(ordered == far_key, -1, ordered)
    info = ordered.reshape(everything // tile, 1, tile)
    token_bits = everything.bit_length() - 1
    rows_of = jnp.maximum(lax.shift_right_arithmetic(ordered, token_bits), 0)
    rows_of = rows_of.reshape(everything // tile, tile)
    first_row = rows_of[:, 0]
    last_row = jnp.max(rows_of, 1)
    tile_count = jnp.maximum(tile_count, 1).reshape(1)

    at_last = (offsets[None, None, :] == last[:, :, None]).astype(jnp.int32)
    scored_ids = jnp.sum(ids[:, PROMPT:].reshape(groups, NCONT, CLEN) * at_last, 2)
    scored_local = scored_ids.reshape(-1) - my_shard * shard_rows
    scored_here = (scored_local >= 0) & (scored_local < shard_rows)
    scored_row = jnp.clip(scored_local, 0, shard_rows - 1)
    scored_row = scored_row.astype(jnp.int32)
    scored_start = pl.pallas_call(
        pick_kernel,
        out_shape=jax.ShapeDtypeStruct((queries, width), FLOAT),
        in_specs=[SMEM_SPEC, pl.BlockSpec(memory_space=pl.ANY)],
        out_specs=VMEM_SPEC,
        scratch_shapes=[pltpu.SemaphoreType.DMA],
    )(scored_row, embedding)
    scored_start = jnp.where(scored_here[:, None], scored_start, 0.0)
    scored_start = lax.reduce_precision(scored_start, 8, 7)
    scored_normed = rms_forward(scored_start, norm_gains[0])[0].astype(BFLOAT)
    cos_table, sin_table = rope_constants()
    late_cos, late_sin = jnp.asarray(cos_table[PROMPT:]), jnp.asarray(sin_table[PROMPT:])
    at_late = (offsets[None, :] == last.reshape(-1)[:, None]).astype(FLOAT)
    scored_cos = jnp.dot(at_late, late_cos, precision=HIGH)
    scored_sin = jnp.dot(at_late, late_sin, precision=HIGH)
    own_last = last_valid[0]
    own_pick = (offsets[None, :] == own_last[:, None]).astype(jnp.int32)
    route_row = jnp.sum(
        routes[0, PROMPT:].reshape(NCONT, CLEN, 2) * own_pick[..., None], 1
    )
    pick_table = (route_row[:, :, None] == jnp.arange(routed)[None, None, :]).astype(FLOAT)
    base_code = (jnp.arange(queries, dtype=jnp.int32) // NCONT) * 8
    own_code = base_code + jnp.arange(queries, dtype=jnp.int32) % NCONT + 1
    own_tall = jnp.tile(own_code, per_owner)[:, None]
    base_tall = jnp.tile(base_code, per_owner)[:, None]
    (
        weights_e,
        both_b,
        info,
        scored_normed,
        scored_cos,
        scored_sin,
        pick_table,
        own_tall,
        base_tall,
        tile_count,
    ) = lax.optimization_barrier(
        (
            weights_e,
            both_b,
            info,
            scored_normed,
            scored_cos,
            scored_sin,
            pick_table,
            own_tall,
            base_tall,
            tile_count,
        )
    )
    cos_wide, sin_wide = jnp.tile(scored_cos, (1, QUAD)), jnp.tile(scored_sin, (1, QUAD))
    query_w_e = weights_e[:, : 2 * LANES]
    both_w = lax.all_gather(both_b, BOTH, tiled=True)
    query_w, out_w = both_w[:, :width], both_w[:, 3 * width :]
    raw = jnp.dot(scored_normed, query_w_e, preferred_element_type=FLOAT)
    former, latter = raw[:, :LANES], raw[:, LANES:]
    query_part = jnp.concatenate(
        [former * cos_wide - latter * sin_wide, latter * cos_wide + former * sin_wide], 1
    ).astype(BFLOAT)
    kept = everything <= KEEP
    embed_b = embedding if kept else embedding.astype(BFLOAT)
    used = per_owner * HALF
    query_part = jnp.concatenate([query_part[:, :used], query_part[:, LANES : LANES + used]], 1)
    query_e = jnp.sum(spread(query_part, "dp").astype(FLOAT), 0)
    late_heads = (score_head, score_head_first, score_head_second)
    query_e, late_last, late_heads = lax.optimization_barrier((query_e, own_last, late_heads))
    head_states = [array[None] for array in late_heads]
    own_late = (offsets[None, :] == late_last[:, None]).astype(FLOAT)
    own_cos = jnp.dot(own_late, late_cos, precision=HIGH)
    own_sin = jnp.dot(own_late, late_sin, precision=HIGH)
    down_w = expert_out.astype(BFLOAT)
    idle = jnp.zeros((queries, LANES - used), FLOAT)
    query_e = jnp.concatenate([query_e[:, :used], idle, query_e[:, used:], idle], 1)

    lane_head = (jnp.arange(2 * LANES) % LANES) // HALF
    head_lanes = (lane_head[None, :] == jnp.arange(per_owner)[:, None]).astype(FLOAT)
    query_rows = (query_e[None] * SCALE * head_lanes[:, None, :]).astype(BFLOAT)
    query_rows = query_rows.reshape(per_owner * queries, 2 * LANES)
    table = jnp.asarray(rope_split())
    any_spec = pl.BlockSpec(memory_space=pl.ANY)
    part = per_owner * HEAD
    start_cut = lax.dynamic_slice_in_dim(scored_start, my_owner * part, part, 1)
    sent_lanes = 2 * part + LANES
    query_count = per_owner * queries
    kept_shapes = (
        jax.ShapeDtypeStruct((everything, width), BFLOAT),
        jax.ShapeDtypeStruct((everything, 2 * LANES), FLOAT),
    )
    sent, *saved = pl.pallas_call(
        functools.partial(forward_kernel, token_bits),
        in_specs=[SMEM_SPEC] * 3
        + [VMEM_SPEC, any_spec if kept else VMEM_SPEC]
        + [VMEM_SPEC] * 7,
        out_specs=(VMEM_SPEC,) + (any_spec,) * (2 * kept),
        scratch_shapes=[
            pltpu.VMEM((2, tile, width), BFLOAT),
            pltpu.VMEM((2, tile, 2 * LANES), FLOAT),
            pltpu.SemaphoreType.DMA((2, 2)),
            pltpu.VMEM((4, min(2 * ROWS, shard_rows), width), FLOAT),
            pltpu.VMEM((shard_rows, width), BFLOAT),
            pltpu.SemaphoreType.DMA((4,)),
        ]
        * kept
        + [
            pltpu.VMEM((query_count, 2 * LANES), FLOAT),
            pltpu.VMEM((query_count, LANES), FLOAT),
            pltpu.VMEM((query_count, LANES), FLOAT),
            pltpu.VMEM((tile, width), FLOAT),
        ],
        out_shape=(jax.ShapeDtypeStruct((queries, sent_lanes), BFLOAT),) + kept_shapes * kept,
        compiler_params=pltpu.CompilerParams(vmem_limit_bytes=FORWARD_LIMIT),
        cost_estimate=pl.CostEstimate(
            flops=30_000_000_000, bytes_accessed=20_000_000, transcendentals=2_000_000
        ),
    )(
        tile_count,
        first_row,
        last_row,
        info,
        embed_b,
        gain_row,
        weights_e,
        table,
        query_rows,
        own_tall,
        base_tall,
        start_cut,
    )
    sent, got_in = lax.optimization_barrier((sent, got_in))
    in_w = got_in.reshape(shard_count, local_experts, slice_rows, 2 * units)
    in_w = in_w.transpose(1, 0, 2, 3).reshape(local_experts, width, 2 * units)
    got = swap(sent.reshape(groups, NCONT, -1), BOTH)
    got = got.reshape(shard_count, owners, NCONT, -1)
    got = got.astype(FLOAT)
    got_out = got[..., :part].reshape(shard_count, owners, NCONT, per_owner, HEAD)
    got_start = got[..., part : 2 * part]
    got_fine = join_float(got[..., 2 * part : 2 * part + 4 * per_owner])
    got_peak, got_total = got_fine[..., :per_owner], got_fine[..., per_owner:]
    peak = jnp.max(got_peak, 0)
    share = jnp.exp(got_peak - peak[None])
    total = jnp.sum(share * got_total, 0)
    mixed = jnp.sum(share[..., None] * got_out, 0) / total[..., None]
    mixed = mixed.transpose(1, 2, 0, 3).reshape(NCONT, width)
    level = (peak + jnp.log(total)).transpose(1, 2, 0).reshape(NCONT, heads)
    start_x = jnp.sum(got_start, 0).transpose(1, 0, 2).reshape(NCONT, width)

    router_b = router.astype(BFLOAT)
    after_attn = start_x + jnp.dot(mixed.astype(BFLOAT), out_w, preferred_element_type=FLOAT)
    normed_two, factor_two = rms_forward(after_attn, norm_gains[1])
    normed_two_b = normed_two.astype(BFLOAT)
    logits = jnp.dot(normed_two_b, router_b, preferred_element_type=FLOAT)
    gate_probs = jax.nn.softmax(logits[:, :routed], -1)
    alphas = [
        jax.nn.softmax(logits[:, routed + 2 * which : routed + 2 * which + 2], -1)
        for which in range(2)
    ]
    gate_pick = jnp.sum(pick_table * gate_probs[:, None, :], -1)
    gate_full = jnp.sum(pick_table * gate_pick[..., None], 1)[:, :experts]
    fine = split_float(jnp.concatenate([level, gate_full], 1))
    tail = jnp.zeros((NCONT, LANES - 2 * (heads + experts)), BFLOAT)
    told = jnp.concatenate(
        [normed_two_b, start_x.astype(BFLOAT), mixed.astype(BFLOAT), fine, tail], 1
    )
    told, first_late, last_late = lax.optimization_barrier((told, first_row, last_row))
    block_rows = min(4 * ROWS, shard_rows // 2)
    row_blocks = shard_rows // block_rows
    low_blocks = max(1, row_blocks * 3 // 8)
    bases = jnp.arange(0, shard_rows, block_rows, dtype=jnp.int32)[:, None]
    filled = (jnp.arange(everything // tile) < tile_count)[None, :]
    begins = jnp.sum((filled & (last_late[None, :] < bases)).astype(jnp.int32), 1)
    begins = jnp.minimum(begins, tile_count - 1)
    ends = jnp.sum((filled & (first_late[None, :] < bases + block_rows)).astype(jnp.int32), 1)
    ends = jnp.maximum(ends, begins + 1)
    earlier = np.arange(row_blocks)[:, None] > np.arange(row_blocks)[None, :]
    orders = jnp.sum((ends - begins)[None, :] * earlier.astype(np.int32), 1)
    told = all_told = spread(told, BOTH).reshape(queries, -1)
    all_normed_b = told[:, :width]
    all_start = told[:, width : 2 * width].astype(FLOAT)
    all_mixed_b = told[:, 2 * width : 3 * width]
    all_fine = join_float(told[:, 3 * width : 3 * width + 2 * (heads + experts)])
    all_level, all_gates = all_fine[:, :heads], all_fine[:, heads:]
    own_gates = lax.dynamic_slice_in_dim(all_gates, my_owner * local_experts, local_experts, 1)

    inner_all, active_all, result_all = [], [], []
    for which in range(local_experts):
        inner = jnp.dot(all_normed_b, in_w[which], preferred_element_type=FLOAT)
        active = (jax.nn.silu(inner[:, :units]) * inner[:, units:]).astype(BFLOAT)
        inner_all.append(inner)
        active_all.append(active)
        result_all.append(jnp.dot(active, down_w[which], preferred_element_type=FLOAT))
    combined = sum(own_gates[:, w : w + 1] * result_all[w] for w in range(local_experts))
    combined = combined.astype(BFLOAT).reshape(groups, NCONT, width)
    fetched = jnp.sum(swap(combined, BOTH).astype(FLOAT), 0)

    is_copy = (route_row == experts + 1).astype(FLOAT)[..., None]
    chosen = [(route_row == experts + 2 + which).astype(FLOAT)[..., None] for which in range(2)]
    branch = is_copy * normed_two[:, None, :]
    for which in range(2):
        constant = (
            alphas[which][:, None, 0:1] * normed_two[:, None, :]
            + alphas[which][:, None, 1:2] * const_vectors[which]
        )
        branch = branch + chosen[which] * constant
    after_ffn = after_attn + fetched + jnp.sum(gate_pick[..., None] * branch, 1)
    final, factor_three = rms_forward(after_ffn, norm_gains[2])
    picked = jnp.sum(final * score_head[None, :], -1)
    pair_rows = rank_pairs[0]
    lead = (pair_rows[:, 0:1] == jnp.arange(NCONT)[None, :]).astype(FLOAT)
    other = (pair_rows[:, 1:2] == jnp.arange(NCONT)[None, :]).astype(FLOAT)
    sides = lead - other
    margin = jnp.sum(sides * picked[None, :], 1)
    loss_part = jnp.sum(jax.nn.softplus(-margin))
    grad_margin = -jax.nn.sigmoid(-margin) * (1.0 / (groups * NPAIR))
    grad_picked = jnp.sum(sides * grad_margin[:, None], 0)
    grad_head = jnp.sum(grad_picked[:, None] * final, 0)
    grad_ffn, grad_gain_final = rms_backward(
        after_ffn, factor_three, norm_gains[2], grad_picked[:, None] * score_head[None, :]
    )
    all_ffn = spread(grad_ffn.astype(BFLOAT), BOTH)

    returned, grad_result, grad_inner = pl.pallas_call(
        functools.partial(expert_kernel, experts),
        out_shape=(
            jax.ShapeDtypeStruct((groups, NCONT, width + LANES), BFLOAT),
            jax.ShapeDtypeStruct((local_experts, queries, width), BFLOAT),
            jax.ShapeDtypeStruct((local_experts, queries, 2 * units), BFLOAT),
        ),
        in_specs=[SMEM_SPEC] + [VMEM_SPEC] * 6,
        out_specs=(VMEM_SPEC,) * 3,
        scratch_shapes=[
            pltpu.VMEM((queries, width), FLOAT),
            pltpu.VMEM((queries, width + LANES), FLOAT),
        ],
        compiler_params=pltpu.CompilerParams(vmem_limit_bytes=VMEM_LIMIT),
    )(
        my_owner.astype(jnp.int32).reshape(1),
        all_ffn,
        own_gates,
        jnp.stack(inner_all),
        jnp.stack(result_all),
        down_w,
        in_w,
    )
    returned = jnp.sum(swap(returned, BOTH).astype(FLOAT), 0)
    returned_grad = returned[:, :width]
    returned_dots = join_float(returned[:, width : width + 2 * experts])
    grad_in = jnp.stack(
        [contract(all_normed_b, grad_inner[w], TN) for w in range(local_experts)]
    )
    grad_expert_out = jnp.stack(
        [contract(active_all[w], grad_result[w], TN) for w in range(local_experts)]
    )

    grad_pick = jnp.sum(grad_ffn[:, None, :] * branch, -1) + jnp.sum(
        pick_table[:, :, :experts] * returned_dots[:, None, :], -1
    )
    grad_branch = gate_pick[..., None] * grad_ffn[:, None, :]
    grad_normed_two = returned_grad + jnp.sum(grad_branch * is_copy, 1)
    grad_vectors = []
    grad_alpha_parts = []
    for which in range(2):
        masked = jnp.sum(chosen[which] * grad_branch, 1)
        grad_vectors.append(jnp.sum(masked * alphas[which][:, 1:2], 0))
        grad_alpha = jnp.stack(
            [jnp.sum(masked * normed_two, -1), jnp.sum(masked * const_vectors[which], -1)], -1
        )
        grad_alpha_parts.append(
            alphas[which] * (grad_alpha - jnp.sum(alphas[which] * grad_alpha, -1, keepdims=True))
        )
        grad_normed_two = grad_normed_two + masked * alphas[which][:, 0:1]
    grad_probs = jnp.sum(pick_table * grad_pick[..., None], 1)
    grad_main = gate_probs * (grad_probs - jnp.sum(gate_probs * grad_probs, -1, keepdims=True))
    grad_logits = jnp.concatenate([grad_main] + grad_alpha_parts, -1)
    grad_normed_two = grad_normed_two + jnp.einsum(
        "tc,dc->td", grad_logits, router_b.astype(FLOAT), precision=HIGH
    )
    grad_attn_part, grad_gain_ffn = rms_backward(
        after_attn, factor_two, norm_gains[1], grad_normed_two
    )
    grad_after_attn = grad_ffn + grad_attn_part
    columns = grad_logits.shape[1]
    misc = jnp.concatenate(
        [
            grad_logits.reshape(-1),
            split_float(loss_part[None]).astype(FLOAT),
        ]
    )
    grad_attn_b = spread(grad_after_attn.astype(BFLOAT), BOTH).reshape(queries, width)

    cut_grad = grad_in.reshape(local_experts, shard_count, slice_rows, 2 * units)
    cut_grad = cut_grad.transpose(1, 0, 2, 3).astype(BFLOAT)
    cut_grad, grad_attn_b = lax.optimization_barrier((cut_grad, grad_attn_b))
    sum_expert_in = swap(cut_grad, "dp")

    order = np.arange(width).reshape(blocks, QUAD, 2, HALF).swapaxes(1, 2).reshape(-1)
    fold = jnp.asarray((np.arange(width)[:, None] == order[None, :]).astype(ml_dtypes.bfloat16))
    all_normed_one = rms_forward(all_start, norm_gains[0])[0].astype(BFLOAT)
    chunk = min(queries, LANES)
    chunks = queries // chunk

    sum_attend_out = contract(
        lax.dynamic_slice_in_dim(all_mixed_b, my_shard * slice_rows, slice_rows, 1),
        grad_attn_b,
        TN,
    )
    side = QUAD * chunk
    quarter = 2 * width // owners
    grad_embed, grad_kv, grad_query, grad_gain, met, embed_square = pl.pallas_call(
        functools.partial(backward_kernel, kept, chunks, blocks, token_bits, experts),
        in_specs=[SMEM_SPEC] * 4
        + [VMEM_SPEC]
        + ([VMEM_SPEC] + [any_spec] * 2 if kept else [any_spec] + [VMEM_SPEC] * 2)
        + [VMEM_SPEC] * 9,
        out_specs=(any_spec,) + (VMEM_SPEC,) * 5,
        scratch_shapes=[
            pltpu.VMEM((1, width), FLOAT),
            pltpu.VMEM((2, tile, width), BFLOAT),
            pltpu.VMEM((width, 2 * width), BFLOAT),
            pltpu.VMEM((chunks, blocks, side, 2 * LANES), BFLOAT),
            pltpu.VMEM((chunks, blocks, 2 * LANES, side), BFLOAT),
            pltpu.VMEM((chunks, blocks, side, 2 * LANES), BFLOAT),
            pltpu.VMEM((chunks, blocks, 2 * LANES, side), BFLOAT),
            pltpu.VMEM((chunks, blocks, 1, side), FLOAT),
            pltpu.VMEM((chunks, blocks, 1, side), FLOAT),
            pltpu.VMEM((tile, side), BFLOAT),
            pltpu.VMEM((chunks, blocks, 2 * LANES, chunk), FLOAT),
            pltpu.VMEM((tile, 2 * width), BFLOAT),
            pltpu.VMEM((8 if kept else tile, width), FLOAT),
            pltpu.VMEM((tile, width), FLOAT),
            pltpu.VMEM((tile, width), FLOAT),
            pltpu.SemaphoreType.DMA((2,)),
        ]
        + (
            [
                pltpu.VMEM((2, tile, width), BFLOAT),
                pltpu.VMEM((2, tile, 2 * LANES), FLOAT),
                pltpu.SemaphoreType.DMA((2, 2)),
            ]
            if kept
            else [pltpu.VMEM((1, tile), jnp.int32), pltpu.SemaphoreType.DMA]
        ),
        out_shape=(
            jax.ShapeDtypeStruct((everything, width), BFLOAT),
            jax.ShapeDtypeStruct((width, quarter), FLOAT),
            jax.ShapeDtypeStruct((chunks, blocks, 2, HALF, chunk), FLOAT),
            jax.ShapeDtypeStruct((1, width), FLOAT),
            jax.ShapeDtypeStruct((queries, width), FLOAT),
            jax.ShapeDtypeStruct((8, LANES), FLOAT),
        ),
        compiler_params=pltpu.CompilerParams(vmem_limit_bytes=VMEM_LIMIT),
        cost_estimate=pl.CostEstimate(
            flops=60_000_000_000, bytes_accessed=60_000_000, transcendentals=6_000_000
        ),
    )(
        tile_count,
        my_owner.astype(jnp.int32).reshape(1),
        first_row,
        last_row,
        scored_local[:, None],
        info,
        saved[0] if kept else embed_b,
        saved[1] if kept else table,
        gain_row,
        both_w,
        fold,
        all_told.reshape(chunks, chunk, -1),
        grad_attn_b.reshape(chunks, chunk, width),
        cos_wide.reshape(chunks, chunk, LANES),
        sin_wide.reshape(chunks, chunk, LANES),
        own_code.reshape(chunks, 1, chunk),
        base_code.reshape(chunks, 1, chunk),
    )

    pieces = grad_query.transpose(0, 4, 1, 2, 3).reshape(groups, NCONT, part)
    met = jnp.where(scored_here[:, None], met, 0.0)
    met = lax.dynamic_slice_in_dim(met, my_owner * part, part, 1).reshape(groups, NCONT, part)
    thin = width // groups
    sent = jnp.concatenate(
        [
            grad_kv.astype(BFLOAT).reshape(groups, thin, quarter),
            split_float(pieces),
            split_float(met),
        ],
        1,
    )
    sent, sum_expert_in = lax.optimization_barrier((sent, sum_expert_in))
    def by_rows(low, high, late):
        place = slice(low, high)
        spec = pl.BlockSpec((block_rows, width), lambda i: (i, 0))
        return pl.pallas_call(
            functools.partial(gather_kernel, token_bits),
            grid=(high - low,),
            out_shape=jax.ShapeDtypeStruct(((high - low) * block_rows, width), BFLOAT),
            in_specs=[SMEM_SPEC] * 6 + [VMEM_SPEC] + [any_spec] * 2,
            out_specs=spec,
            scratch_shapes=[
                pltpu.VMEM((block_rows, width), FLOAT),
                pltpu.VMEM((2, tile, width), BFLOAT),
                pltpu.SemaphoreType.DMA((2,)),
            ],
            compiler_params=pltpu.CompilerParams(vmem_limit_bytes=VMEM_LIMIT),
            cost_estimate=pl.CostEstimate(
                flops=10_000_000_000, bytes_accessed=12_000_000, transcendentals=0
            ),
        )(
            jnp.full((1,), low * block_rows, jnp.int32),
            begins[place],
            ends[place],
            orders[place],
            first_row,
            last_row,
            info,
            grad_embed,
            late,
        )

    grad_low = by_rows(0, low_blocks, sent)
    got = swap(sent, BOTH)
    leader = (my_owner == 0).astype(FLOAT)
    rest_square = (
        jnp.sum(grad_in * grad_in)
        + jnp.sum(grad_expert_out * grad_expert_out)
        + leader * jnp.sum(sum_attend_out * sum_attend_out)
    )
    misc_lane = misc.shape[0]
    misc = jnp.pad(misc, (0, width - misc_lane))
    blank = jnp.zeros((width,), FLOAT)
    rows = [blank, grad_gain_ffn, grad_gain_final] + grad_vectors + [grad_head, misc, blank]
    told, sum_kv = pl.pallas_call(
        functools.partial(owner_kernel, owners, thin, misc_lane),
        out_shape=(
            jax.ShapeDtypeStruct((groups, 16, width), BFLOAT),
            jax.ShapeDtypeStruct((thin, 2 * width), FLOAT),
        ),
        in_specs=[SMEM_SPEC] * 2 + [VMEM_SPEC] * 10 + [any_spec],
        out_specs=(VMEM_SPEC,) * 2,
        compiler_params=pltpu.CompilerParams(vmem_limit_bytes=VMEM_LIMIT),
    )(
        rest_square.reshape(1),
        leader.reshape(1),
        got,
        query_w,
        start_x,
        grad_after_attn,
        own_cos,
        own_sin,
        gain_row,
        grad_gain,
        embed_square,
        jnp.stack(rows),
        grad_low,
    )
    grad_high = by_rows(low_blocks, row_blocks, told)
    told = spread_made(told, BOTH).reshape(16 * groups, width)
    told, sum_kv = lax.optimization_barrier((told, sum_kv))
    all_kv = spread(sum_kv.astype(BFLOAT), "expert").reshape(slice_rows, 2 * width)
    rates = learn_rates()
    normed_slice = lax.dynamic_slice_in_dim(
        all_normed_one, my_shard * slice_rows, slice_rows, 1
    )
    small_states = (
        router.T,
        router_first.T,
        router_second.T,
        norm_gains,
        norm_gains_first,
        norm_gains_second,
        const_vectors,
        const_vectors_first,
        const_vectors_second,
        *head_states,
    )
    all_extra_b, sum_query_w, scalars, *made_small = pl.pallas_call(
        functools.partial(finish_kernel, rates[5:], DECAYS[5:], columns),
        out_shape=(
            jax.ShapeDtypeStruct((queries, width), BFLOAT),
            jax.ShapeDtypeStruct((slice_rows, width), FLOAT),
            jax.ShapeDtypeStruct((8, LANES), FLOAT),
        )
        + tuple(jax.ShapeDtypeStruct(array.shape, FLOAT) for array in small_states),
        in_specs=[VMEM_SPEC] * 18,
        out_specs=(VMEM_SPEC,) * 15,
        compiler_params=pltpu.CompilerParams(vmem_limit_bytes=VMEM_LIMIT),
    )(
        told,
        scored_ids.reshape(-1, 1),
        scored_ids.reshape(1, -1),
        contract(all_normed_one, all_normed_one, NT),
        all_normed_b,
        normed_slice,
        *small_states,
    )
    loss_total, norm_total, factor = scalars[0, 0], scalars[0, 1], scalars[0, 2]
    key_grad = contract(all_kv[:, :width], fold, NT)
    sum_attend_in = jnp.concatenate(
        [sum_query_w, key_grad, all_kv[:, width:].astype(FLOAT)], 1
    )

    row_spec = pl.BlockSpec((block_rows, width), lambda i: (i, 0))
    low_spec = pl.BlockSpec((block_rows, width), lambda i: (jnp.minimum(i, low_blocks - 1), 0))
    high_spec = pl.BlockSpec((block_rows, width), lambda i: (jnp.maximum(i - low_blocks, 0), 0))
    made_embedding = pl.pallas_call(
        functools.partial(adam_kernel, rates[0], DECAYS[0], low_blocks),
        grid=(shard_rows // block_rows,),
        out_shape=(jax.ShapeDtypeStruct((shard_rows, width), FLOAT),) * 3,
        in_specs=[SMEM_SPEC] + [VMEM_SPEC] * 2 + [low_spec, high_spec] + [row_spec] * 3,
        out_specs=(row_spec,) * 3,
        compiler_params=pltpu.CompilerParams(vmem_limit_bytes=VMEM_LIMIT),
        cost_estimate=pl.CostEstimate(
            flops=4_000_000_000, bytes_accessed=176_000_000, transcendentals=12_000_000
        ),
    )(
        factor.reshape(1),
        jnp.where(scored_here, scored_local, -1)[None],
        all_extra_b,
        grad_low,
        grad_high,
        embedding,
        embedding_first,
        embedding_second,
    )
    cut_rows = 48
    cells = pl.BlockSpec((1, cut_rows, hidden_units), lambda l, h, r: (l, r, h))
    cut_spec = pl.BlockSpec((shard_count, 1, cut_rows, units), lambda l, h, r: (0, l, r, h))
    if units % LANES == 0 and slice_rows % cut_rows == 0:
        made_in = pl.pallas_call(
            functools.partial(matrix_adam_kernel, rates[3], DECAYS[3]),
            grid=(local_experts, 2, slice_rows // cut_rows),
            out_shape=(jax.ShapeDtypeStruct(expert_in.shape, FLOAT),) * 3,
            in_specs=[SMEM_SPEC] + [cells] * 3 + [cut_spec],
            out_specs=(cells,) * 3,
            compiler_params=pltpu.CompilerParams(vmem_limit_bytes=SMALL_LIMIT),
            cost_estimate=pl.CostEstimate(
                flops=100_000_000, bytes_accessed=20_000_000, transcendentals=1_600_000
            ),
        )(factor.reshape(1), expert_in, expert_in_first, expert_in_second, sum_expert_in)
    else:
        whole_in = sum_expert_in.astype(FLOAT).reshape(
            shard_count, local_experts, slice_rows, 2, units
        )
        whole_in = whole_in.transpose(1, 2, 3, 0, 4).reshape(expert_in.shape)
        made_in = adam_update(
            expert_in, expert_in_first, expert_in_second, whole_in * factor, rates[3], DECAYS[3]
        )
    made = list(made_embedding)
    states = (
        (attend_in, attend_in_first, attend_in_second, sum_attend_in),
        (attend_out, attend_out_first, attend_out_second, sum_attend_out),
        None,
        (expert_out, expert_out_first, expert_out_second, grad_expert_out),
    )
    for which, state in enumerate(states):
        if state is None:
            made += made_in
            continue
        *state, grad = state
        made += adam_update(*state, grad * factor, rates[which + 1], DECAYS[which + 1])
    made += [array.T for array in made_small[:3]] + made_small[3:9]
    made += [array.reshape(-1) for array in made_small[9:]]
    return tuple(made) + (loss_total, norm_total)


def solution(mesh):
    pair = P(BOTH, None)
    triple = P(BOTH, None, None)
    rows = P("dp", None)
    cells = P("expert", "dp", None)
    placed = (pair, triple, pair, triple) + (rows,) * 9 + (cells,) * 6 + (P(),) * 12
    return jax.shard_map(
        shards,
        mesh=mesh,
        in_specs=placed,
        out_specs=(rows,) * 9 + (cells,) * 6 + (P(),) * 14,
        check_vma=False,
    )
```
